32 devices in a mesh: energy: 8 (over y, x, core), space: 4 (over z).
Axes of the slice: x: 2, y: 2, z: 4, core: 2. Of those that a mesh axis runs over, the one named last changes fastest.
Arguments:
- onsite: float32 [4, 2, 128, 128], P('space'), may hold values from -0.25 to 0.25
- hopping: float32 [4, 2, 128, 128], P('space'), may hold values from -0.25 to 0.25
- sigma_old: float32 [8, 4, 2, 128, 128], P('energy', 'space'), may hold values from -0.0390625 to 0.0390625
- screened: float32 [8, 4, 2, 3, 2, 128, 128], P('energy', 'space'), may hold values from -2 to 2
Outputs:
- green_retarded: float32 [8, 4, 3, 2, 128, 128], P('energy', 'space')
- self_energy: float32 [8, 4, 2, 3, 2, 128, 128], P('energy', 'space')
The draws below stay inside these ranges and needn't reach their ends.
All inputs are finite; a program needn't handle non-finite values.
Results may differ from the reference program's by a relative error of at most 0.0003.
Values sent between devices are 32-bit elements; how exact they have to be, the bound alone decides.
No kernel may reach another device: no remote copies, remote signals or barrier semaphores. Data moves between devices by JAX's collectives and lax.ppermute only.
A program may use at most 128 MiB of HBM per device.

```python
import jax
import jax.numpy as jnp
from jax import lax

B = 128
NE = 8
NC = 4


def block_levels(stream_key, dims, cuts, smallest, high):
    gain, own = 1.0, jax.random.fold_in(stream_key, 6)
    for axis_at, blocks in cuts:
        draws = jnp.exp(jax.random.uniform(jax.random.fold_in(own, axis_at), (blocks,), jnp.float32, smallest / len(cuts), high / len(cuts)))
        gain = gain * jnp.repeat(draws, dims[axis_at] // blocks).reshape([-1 if axis == axis_at else 1 for axis in range(len(dims))])
    return gain


def noise(own_key, extent, deviation, reach, split=(), kind=jnp.bfloat16):
    result = jax.random.normal(own_key, extent, jnp.float32) * deviation
    if len(split) > 0:
        result = block_levels(own_key, extent, split, -0.22, 0.18) * result
    return jnp.clip(result, min=-reach, max=reach).astype(kind)


def setup_inputs(seed: int = 0) -> dict:
    splits = jax.random.split(jax.random.key(seed), 5)
    return {
        "onsite": noise(splits[0], (NC, 2, B, B), (B * 4) ** -0.5, 0.25, ((0, 4),), jnp.float32),
        "hopping": noise(splits[1], (NC, 2, B, B), (B * 4) ** -0.5, 0.25, ((0, 4),), jnp.float32),
        "sigma_old": noise(splits[2], (NE, NC, 2, B, B), (B * 200) ** -0.5, 0.0390625, ((0, 8), (1, 4)), jnp.float32),
        "screened": noise(splits[3], (NE, NC, 2, 3, 2, B, B), NE ** -0.5, 2.0, ((0, 8), (1, 4)), jnp.float32),
    }


BROADEN = 0.45
THERMAL = 0.1
PRECISE = lax.Precision.HIGHEST

def matmul_high(first, second):
    return jnp.matmul(first, second, precision=PRECISE)

def complex_product(first, second):
    real_part = matmul_high(first[0], second[0]) - matmul_high(first[1], second[1])
    imag_part = matmul_high(first[0], second[1]) + matmul_high(first[1], second[0])
    return jnp.stack([real_part, imag_part])

def dagger(blocks):
    return jnp.stack([jnp.swapaxes(blocks[0], -1, -2), -jnp.swapaxes(blocks[1], -1, -2)])

def invert_exact(blocks):
    size_order = blocks.shape[-1]
    upper_half = jnp.concatenate([blocks[0], -blocks[1]], axis=-1)
    lower_half = jnp.concatenate([blocks[1], blocks[0]], axis=-1)
    embedded = jnp.concatenate([upper_half, lower_half], axis=-2)
    target = jnp.concatenate([jnp.eye(size_order, dtype=blocks.dtype), jnp.zeros((size_order, size_order), blocks.dtype)], axis=0)
    target = jnp.broadcast_to(target, embedded.shape[:-1] + (size_order,))
    solved = jnp.linalg.solve(embedded, target)
    return jnp.stack([solved[..., :size_order, :], solved[..., size_order:, :]])

def convolve_cell(operands):
    green_cell, kernel_cell = operands
    energies_all = green_cell.shape[0]
    padded = jnp.concatenate([jnp.zeros_like(green_cell), green_cell], axis=0)

    def accumulate(running, offset):
        shifted = lax.dynamic_slice_in_dim(padded, (energies_all - offset).astype(jnp.int32), energies_all, 0)
        weight = kernel_cell[offset]
        real_part = shifted[:, :, :, 0] * weight[:, :, 0] - shifted[:, :, :, 1] * weight[:, :, 1]
        imag_part = shifted[:, :, :, 0] * weight[:, :, 1] + shifted[:, :, :, 1] * weight[:, :, 0]
        return (running + jnp.stack([real_part, imag_part], axis=3), None)
    running, _ = lax.scan(accumulate, jnp.zeros_like(green_cell), jnp.arange(energies_all, dtype=jnp.int32))
    return jnp.stack([-running[:, :, :, 1], running[:, :, :, 0]], axis=3)

def reference(onsite, hopping, sigma_old, screened):
    energies_all = sigma_old.shape[0]
    cells_all = sigma_old.shape[1]
    size_order = sigma_old.shape[-1]
    float_type = sigma_old.dtype
    energy = -1.5 + 3.0 * (jnp.arange(energies_all).astype(float_type) + 0.5) / energies_all
    identity = jnp.eye(size_order, dtype=float_type)
    magnitude = energy * energy + BROADEN * BROADEN
    contact = jnp.stack([(energy / magnitude)[:, None, None] * identity, (-BROADEN / magnitude)[:, None, None] * identity])
    systems = []
    for cell_index in range(cells_all):
        hamiltonian = 0.5 * (onsite[cell_index] + dagger(onsite[cell_index]))
        local_sigma = jnp.moveaxis(sigma_old[:, cell_index], 1, 0)
        systems.append(jnp.stack([energy[:, None, None] * identity - hamiltonian[0] - local_sigma[0], BROADEN * identity - hamiltonian[1] - local_sigma[1]]))
    couplings = [hopping[cell_index] for cell_index in range(cells_all)] + [jnp.zeros_like(hopping[0])]
    left_previous = []
    previous = contact
    for cell_index in range(cells_all):
        left_previous.append(previous)
        coupling = couplings[cell_index]
        previous = invert_exact(systems[cell_index] - complex_product(dagger(coupling), complex_product(previous, coupling)))
    right_following = [None] * cells_all
    following = jnp.zeros_like(contact)
    for cell_index in reversed(range(cells_all)):
        right_following[cell_index] = following
        ahead_coupling = couplings[cell_index + 1]
        following = invert_exact(systems[cell_index] - complex_product(ahead_coupling, complex_product(following, dagger(ahead_coupling))))
    occupation = 1.0 / (1.0 + jnp.exp(energy / THERMAL))
    occupied = occupation[None, :, None, None, None]
    greens = []
    kinds = []
    for cell_index in range(cells_all):
        coupling = couplings[cell_index]
        ahead_coupling = couplings[cell_index + 1]
        self_left = complex_product(dagger(coupling), complex_product(left_previous[cell_index], coupling))
        self_right = complex_product(ahead_coupling, complex_product(right_following[cell_index], dagger(ahead_coupling)))
        diagonal = invert_exact(systems[cell_index] - self_left - self_right)
        upper_block = complex_product(left_previous[cell_index], complex_product(coupling, diagonal))
        lower_block = complex_product(diagonal, complex_product(dagger(coupling), left_previous[cell_index]))
        stacked = jnp.stack([diagonal, upper_block, lower_block], axis=2)
        spectral = jnp.stack([diagonal - dagger(diagonal), upper_block - dagger(lower_block), lower_block - dagger(upper_block)], axis=2)
        both_kinds = jnp.stack([-occupied * spectral, (1.0 - occupied) * spectral])
        greens.append(jnp.transpose(stacked, (1, 2, 0, 3, 4)))
        kinds.append(jnp.transpose(both_kinds, (2, 0, 3, 1, 4, 5)))
    green_retarded = jnp.stack(greens, axis=1)
    lesser_greater = jnp.stack(kinds, axis=0)
    kernel = jnp.moveaxis(screened, 1, 0)
    sigma_cells = lax.map(convolve_cell, (lesser_greater, kernel))
    return (green_retarded, jnp.moveaxis(sigma_cells, 0, 1))
```

```python
import functools
import math

import jax
import jax.numpy as jnp
from jax import lax
from jax.experimental import pallas as pl
from jax.experimental.pallas import tpu as pltpu
from jax.sharding import PartitionSpec as P

BROADEN = 0.45
THERMAL = 0.1
F32 = jnp.float32
BF16 = jnp.bfloat16

LOWEST = 1.0 / 128.0
SQUARINGS = 6
DONE = 1e-4
STEPS_MAX = 60


def schedule():
    rho = (1.0 - LOWEST) / (1.0 + LOWEST)
    scales = []
    for _ in range(SQUARINGS):
        scales.append(2.0 / (2.0 - rho * rho))
        rho = rho * rho / (2.0 - rho * rho)
    return 2.0 / (1.0 + LOWEST), scales


def real_of(x):
    return x[:, : x.shape[1] // 2]


def imag_of(x):
    return x[:, x.shape[1] // 2 :]


def wide(x):
    return jnp.concatenate([x, jnp.concatenate([-imag_of(x), real_of(x)], axis=1)], axis=0)


def dagger(x):
    return jnp.concatenate([real_of(x).T, -imag_of(x).T], axis=1)


def dot(a, b):
    return jnp.dot(a, b, preferred_element_type=F32)


def split(x):
    high = x.astype(BF16)
    return high, (x - high.astype(F32)).astype(BF16)


def product(a, b):
    rows = a.shape[0]
    a_high, a_low = split(a)
    b_high, b_low = split(b)
    both = dot(jnp.concatenate([a_high, a_low], axis=0), wide(b_high))
    return both[:rows] + both[rows:] + dot(a_high, wide(b_low))


def times_complex(x, re, im):
    return jnp.concatenate(
        [re * real_of(x) - im * imag_of(x), re * imag_of(x) + im * real_of(x)], axis=1
    )


def identity_like(x):
    size = x.shape[0]
    row = lax.broadcasted_iota(jnp.int32, x.shape, 0)
    column = lax.broadcasted_iota(jnp.int32, x.shape, 1)
    return jnp.where(row == column, 1.0, 0.0).astype(F32)


def largest(x, axis):
    return jnp.max(x, axis=axis, keepdims=True)


def invert(s, out_ref):
    size = s.shape[0]
    one = identity_like(s)
    first, scales = schedule()
    s_dagger = dagger(s)
    s_dagger_b = s_dagger.astype(BF16)
    normal = dot(s.astype(BF16), wide(s_dagger_b))
    normal_b = normal.astype(BF16)
    both = dot(jnp.concatenate([s_dagger_b, normal_b], axis=0), wide(normal_b))
    square = both[size:]
    sums = jnp.sum(jnp.sqrt(real_of(square) ** 2 + imag_of(square) ** 2), axis=0, keepdims=True)
    a = first * lax.rsqrt(largest(sums, 1))
    c = scales[0]
    x = (2.0 * c * a) * s_dagger - (c * a * a) * both[:size]
    r = one - (2.0 * c * a) * normal + (c * a * a) * square
    for c in scales[1:]:
        r_b = r.astype(BF16)
        both = dot(jnp.concatenate([x.astype(BF16), r_b], axis=0), wide(r_b))
        x = c * (x + both[:size])
        r = (1.0 - c) * one + c * both[size:]
    s_high, s_low = split(s)
    s_both = jnp.concatenate([s_high, s_low], axis=0)
    x_b = x.astype(BF16)
    both = dot(s_both, wide(x_b))
    e_b = (one - both[:size] - both[size:]).astype(BF16)
    x = x_b.astype(F32) + dot(x_b, wide(e_b))

    def step(x):
        x_high, x_low = split(x)
        both = dot(s_both, wide(x_high))
        e = one - both[:size] - both[size:] - dot(s_high, wide(x_low))
        return x + dot(x_high, wide(e.astype(BF16))), jnp.sum(e * e)

    x, left = step(x)
    out_ref[...] = x

    @pl.when(jnp.logical_not(left < DONE))
    def _():
        bound = jnp.sqrt(largest(jnp.sum(jnp.abs(s), axis=1, keepdims=True), 0))
        other = jnp.sqrt(largest(jnp.sum(jnp.abs(real_of(s)) + jnp.abs(imag_of(s)), axis=0, keepdims=True), 1))
        safe = s_dagger / (bound * bound) / (other * other)
        good = left < 0.5
        start = jnp.where(good, x, safe)

        def unfinished(state):
            count, value, _ = state
            return jnp.logical_and(count < STEPS_MAX, jnp.logical_not(value < DONE))

        def body(state):
            count, _, x = state
            new = product(x, one - product(s, x))
            e = one - product(s, x)
            return count + 1, jnp.sum(e * e), x + new

        _, _, result = lax.while_loop(unfinished, body, (0, left, start))
        out_ref[...] = result


def energy_at(index, energies_all):
    return -1.5 + 3.0 * (index + 0.5) / energies_all


def outer_kernel(axes, onsite, hopping, sigma, system_ref, green_ref):
    energies_all, cells_all = axes
    position = lax.axis_index("space")
    energy = energy_at(lax.axis_index("energy").astype(F32), energies_all)
    on = jnp.concatenate([onsite[0, 0], onsite[0, 1]], axis=1)
    sg = jnp.concatenate([sigma[0, 0, 0], sigma[0, 0, 1]], axis=1)
    h = jnp.concatenate([hopping[0, 0], hopping[0, 1]], axis=1)
    one = identity_like(on)
    shape = on.shape
    row = lax.broadcasted_iota(jnp.int32, shape, 0)
    column = lax.broadcasted_iota(jnp.int32, shape, 1)
    point = jnp.where(row == column, energy, 0.0) + jnp.where(row + shape[0] == column, BROADEN, 0.0)
    system = point - 0.5 * (on + dagger(on)) - sg
    system_ref[...] = system

    @pl.when(position == 0)
    def _():
        magnitude = energy * energy + BROADEN * BROADEN
        hh = product(dagger(h), h)
        s = system - times_complex(hh, energy / magnitude, -BROADEN / magnitude)
        system_ref[...] = s

    green_ref[...] = jnp.zeros(shape, F32)

    @pl.when(jnp.logical_or(position == 0, position == cells_all - 1))
    def _():
        invert(system_ref[...], green_ref)


def couplings(left, hopping, following):
    h = jnp.concatenate([hopping[0, 0], hopping[0, 1]], axis=1)
    h_next = jnp.concatenate([following[0, 0], following[0, 1]], axis=1)
    h_dagger = dagger(h)
    next_dagger = dagger(h_next)
    outer = (jnp.where(left, h, next_dagger), jnp.where(left, h_dagger, h_next))
    inner = (jnp.where(left, next_dagger, h), jnp.where(left, h_next, h_dagger))
    return outer, inner


def depth_of(cells_all):
    position = lax.axis_index("space")
    return jnp.minimum(position, cells_all - 1 - position), position < cells_all // 2


def inward_kernel(axes, level, hopping, following, received, system, green, outside, system_ref, green_ref, outside_ref):
    _, cells_all = axes
    depth, left = depth_of(cells_all)
    system_ref[...] = system[...]
    green_ref[...] = green[...]
    outside_ref[...] = outside[...]

    @pl.when(depth == level)
    def _():
        (right_factor, left_factor), _ = couplings(left, hopping, following)
        g = received[...]
        outside_ref[...] = g
        s = system[...] - product(left_factor, product(g, right_factor))
        system_ref[...] = s
        invert(s, green_ref)


def middle_kernel(axes, hopping, following, received, system, green, outside, green_ref, upper_ref, lower_ref, ready_ref):
    energies_all, cells_all = axes
    depth, left = depth_of(cells_all)
    middle = cells_all // 2 - 1
    outer, inner = couplings(left, hopping, following)
    right_in, left_in = inner
    right_out, left_out = outer
    position = lax.axis_index("space")
    energy = energy_at(lax.axis_index("energy").astype(F32), energies_all)
    magnitude = energy * energy + BROADEN * BROADEN
    contact_re, contact_im = energy / magnitude, -BROADEN / magnitude

    @pl.when(depth == middle)
    def _():
        g_in = received[...]
        g_right = product(g_in, right_in)
        s = system[...] - product(left_in, g_right)
        invert(s, green_ref)
        g_out = outside[...]
        u = jnp.where(left, product(g_out, right_out), g_right)
        v = product(jnp.where(left, left_out, left_in), jnp.where(left, g_out, g_in))
        diagonal = green_ref[...]
        upper_ref[...] = product(u, diagonal)
        lower_ref[...] = product(diagonal, v)
        ready_ref[...] = jnp.zeros_like(ready_ref)

    @pl.when(depth != middle)
    def _():
        g = green[...]
        g_out = outside[...]
        p = product(g, left_in)
        q = product(right_in, g)
        at_contact = position == 0
        u = jnp.where(at_contact, times_complex(right_out, contact_re, contact_im), product(g_out, right_out))
        v = jnp.where(at_contact, times_complex(left_out, contact_re, contact_im), product(left_out, g_out))
        ready_ref[0] = p
        ready_ref[1] = q
        ready_ref[2] = product(u, p)
        ready_ref[3] = product(q, v)
        ready_ref[4] = product(u, g)
        ready_ref[5] = product(g, v)
        green_ref[...] = g
        upper_ref[...] = jnp.zeros_like(upper_ref)
        lower_ref[...] = jnp.zeros_like(lower_ref)


def outward_kernel(axes, level, final, received, ready, diagonal, upper, lower, *outputs):
    _, cells_all = axes
    depth, left = depth_of(cells_all)
    if final:
        green_out, packed_ref, green_ref, upper_ref, lower_ref = outputs
    else:
        green_ref, upper_ref, lower_ref = outputs
    green_ref[...] = diagonal[...]
    upper_ref[...] = upper[...]
    lower_ref[...] = lower[...]

    @pl.when(depth == level)
    def _():
        g_in = received[...]
        p = ready[0]
        w = product(g_in, ready[1])
        green_ref[...] = diagonal[...] + product(p, w)

        @pl.when(left)
        def _():
            upper_ref[...] = ready[4] + product(ready[2], w)
            lower_ref[...] = ready[5] + product(p, product(g_in, ready[3]))

        @pl.when(jnp.logical_not(left))
        def _():
            upper_ref[...] = w
            lower_ref[...] = product(p, g_in)

    if final:
        size = diagonal.shape[0]
        blocks = (green_ref[...], upper_ref[...], lower_ref[...])
        for b, block in enumerate(blocks):
            green_out[b, 0] = real_of(block)
            green_out[b, 1] = imag_of(block)
        d0 = blocks[0] - dagger(blocks[0])
        d1 = blocks[1] - dagger(blocks[2])
        row = lax.broadcasted_iota(jnp.int32, (size, size), 0)
        column = lax.broadcasted_iota(jnp.int32, (size, size), 1)
        packed_ref[0] = jnp.where(row > column, real_of(d0), imag_of(d0))
        packed_ref[1] = real_of(d1)
        packed_ref[2] = imag_of(d1)


def convolve_kernel(axes, index, packed, kernels, out):
    energies_all, _ = axes
    n = index[0]
    m = pl.program_id(0)
    size = packed.shape[-1]

    @pl.when(m == 0)
    def _():
        out[...] = jnp.zeros_like(out)

    @pl.when(m <= n)
    def _():
        energy = energy_at(m.astype(F32), energies_all)
        occupation = 1.0 / (1.0 + jnp.exp(jnp.full((1, 1), energy / THERMAL, F32)))
        row = lax.broadcasted_iota(jnp.int32, (size, size), 0)
        column = lax.broadcasted_iota(jnp.int32, (size, size), 1)
        pack = packed[0, 0]
        turned = pack.T
        d0_re = jnp.where(row > column, pack, jnp.where(row < column, -turned, 0.0))
        d0_im = jnp.where(row > column, turned, pack)
        d1_re, d1_im = packed[0, 1], packed[0, 2]
        d2_re, d2_im = -d1_re.T, d1_im.T
        for s, scale in enumerate((-occupation, 1.0 - occupation)):
            for b, (d_re, d_im) in enumerate(((d0_re, d0_im), (d1_re, d1_im), (d2_re, d2_im))):
                w_re, w_im = kernels[0, s, b, 0], kernels[0, s, b, 1]
                g_re, g_im = scale * d_re, scale * d_im
                out[s, b, 0] -= g_re * w_im + g_im * w_re
                out[s, b, 1] += g_re * w_re - g_im * w_im


def local(axes, onsite, hopping, sigma_old, screened):
    energies_all, cells_all = axes
    size = sigma_old.shape[-1]
    half = cells_all // 2
    matrix = jax.ShapeDtypeStruct((size, 2 * size), F32)
    params = pltpu.CompilerParams(vmem_limit_bytes=48 * 1024 * 1024)
    cost = pl.CostEstimate(flops=2 * 40 * (2 * size) ** 3, bytes_accessed=2 * 1024 * 1024, transcendentals=0)

    def call(body, out_shape, *operands):
        return pl.pallas_call(
            body,
            out_shape=out_shape,
            in_specs=[pl.BlockSpec(memory_space=pltpu.VMEM)] * len(operands),
            out_specs=jax.tree.map(lambda _: pl.BlockSpec(memory_space=pltpu.VMEM), out_shape),
            compiler_params=params,
            cost_estimate=cost,
        )(*operands)

    kernels = lax.all_gather(screened[0, 0], "energy", axis=0)
    following = lax.ppermute(hopping, "space", [(i + 1, i) for i in range(cells_all - 1)])
    system, green = call(
        functools.partial(outer_kernel, axes), (matrix, matrix), onsite, hopping, sigma_old
    )
    outside = jnp.zeros((size, 2 * size), F32)
    for level in range(1, half):
        route = [(level - 1, level), (cells_all - level, cells_all - 1 - level)]
        received = lax.ppermute(green, "space", route)
        system, green, outside = call(
            functools.partial(inward_kernel, axes, level),
            (matrix, matrix, matrix),
            hopping, following, received, system, green, outside,
        )
    received = lax.ppermute(green, "space", [(half - 1, half), (half, half - 1)])
    diagonal, upper, lower, ready = call(
        functools.partial(middle_kernel, axes),
        (matrix, matrix, matrix, jax.ShapeDtypeStruct((6, size, 2 * size), F32)),
        hopping, following, received, system, green, outside,
    )
    for level in reversed(range(half - 1)):
        route = [(level + 1, level), (cells_all - 2 - level, cells_all - 1 - level)]
        received = lax.ppermute(diagonal, "space", route)
        final = level == 0
        shapes = (matrix, matrix, matrix)
        if final:
            shapes = (
                jax.ShapeDtypeStruct((3, 2, size, size), F32),
                jax.ShapeDtypeStruct((3, size, size), F32),
            ) + shapes
        results = call(
            functools.partial(outward_kernel, axes, level, final),
            shapes,
            received, ready, diagonal, upper, lower,
        )
        diagonal, upper, lower = results[-3:]
    green_out, packed = results[:2]
    gathered = lax.all_gather(packed, "energy", axis=0)
    index = lax.axis_index("energy").astype(jnp.int32).reshape(1)
    sigma_out = pl.pallas_call(
        functools.partial(convolve_kernel, axes),
        out_shape=jax.ShapeDtypeStruct((2, 3, 2, size, size), F32),
        grid_spec=pltpu.PrefetchScalarGridSpec(
            num_scalar_prefetch=1,
            grid=(energies_all,),
            in_specs=[
                pl.BlockSpec((1, 3, size, size), lambda m, index: (m, 0, 0, 0)),
                pl.BlockSpec(
                    (1, 2, 3, 2, size, size),
                    lambda m, index: (jnp.maximum(index[0] - m, 0), 0, 0, 0, 0, 0),
                ),
            ],
            out_specs=pl.BlockSpec((2, 3, 2, size, size), lambda m, index: (0, 0, 0, 0, 0)),
        ),
        compiler_params=params,
    )(index, gathered, kernels)
    return green_out[None, None], sigma_out[None, None]


def solution(mesh):
    axes = (mesh.shape["energy"], mesh.shape["space"])
    placed = (
        P("space", None, None, None),
        P("space", None, None, None),
        P("energy", "space", None, None, None),
        P("energy", "space", None, None, None, None, None),
    )
    return jax.shard_map(
        functools.partial(local, axes),
        mesh=mesh,
        in_specs=placed,
        out_specs=(
            P("energy", "space", None, None, None, None),
            P("energy", "space", None, None, None, None, None),
        ),
        check_vma=False,
    )
```

```python
import functools
import math

import jax
import jax.numpy as jnp
from jax import lax
from jax.experimental import pallas as pl
from jax.experimental.pallas import tpu as pltpu
from jax.sharding import PartitionSpec as P

BROADEN = 0.45
THERMAL = 0.1
F32 = jnp.float32
BF16 = jnp.bfloat16

LOWEST = 1.0 / 128.0
SQUARINGS = 6
DONE = 1e-4
STEPS_MAX = 60


def schedule():
    rho = (1.0 - LOWEST) / (1.0 + LOWEST)
    scales = []
    for _ in range(SQUARINGS):
        scales.append(2.0 / (2.0 - rho * rho))
        rho = rho * rho / (2.0 - rho * rho)
    return 2.0 / (1.0 + LOWEST), scales


def real_of(x):
    return x[:, : x.shape[1] // 2]


def imag_of(x):
    return x[:, x.shape[1] // 2 :]


def wide(x):
    return jnp.concatenate([x, jnp.concatenate([-imag_of(x), real_of(x)], axis=1)], axis=0)


def dagger(x):
    return jnp.concatenate([real_of(x).T, -imag_of(x).T], axis=1)


def dot(a, b):
    return jnp.dot(a, b, preferred_element_type=F32)


def split(x):
    high = x.astype(BF16)
    return high, (x - high.astype(F32)).astype(BF16)


def product(a, b):
    rows = a.shape[0]
    a_high, a_low = split(a)
    b_high, b_low = split(b)
    both = dot(jnp.concatenate([a_high, a_low], axis=0), wide(b_high))
    return both[:rows] + both[rows:] + dot(a_high, wide(b_low))


def times_complex(x, re, im):
    return jnp.concatenate(
        [re * real_of(x) - im * imag_of(x), re * imag_of(x) + im * real_of(x)], axis=1
    )


def identity_like(x):
    size = x.shape[0]
    row = lax.broadcasted_iota(jnp.int32, x.shape, 0)
    column = lax.broadcasted_iota(jnp.int32, x.shape, 1)
    return jnp.where(row == column, 1.0, 0.0).astype(F32)


def largest(x, axis):
    return jnp.max(x, axis=axis, keepdims=True)


def invert(s, out_ref):
    size = s.shape[0]
    one = identity_like(s)
    first, scales = schedule()
    s_dagger = dagger(s)
    s_dagger_b = s_dagger.astype(BF16)
    normal = dot(s.astype(BF16), wide(s_dagger_b))
    normal_b = normal.astype(BF16)
    both = dot(jnp.concatenate([s_dagger_b, normal_b], axis=0), wide(normal_b))
    square = both[size:]
    sums = jnp.sum(jnp.sqrt(real_of(square) ** 2 + imag_of(square) ** 2), axis=0, keepdims=True)
    a = first * lax.rsqrt(largest(sums, 1))
    c = scales[0]
    x = (2.0 * c * a) * s_dagger - (c * a * a) * both[:size]
    r = one - (2.0 * c * a) * normal + (c * a * a) * square
    for c in scales[1:]:
        r_b = r.astype(BF16)
        both = dot(jnp.concatenate([x.astype(BF16), r_b], axis=0), wide(r_b))
        x = c * (x + both[:size])
        r = (1.0 - c) * one + c * both[size:]
    s_high, s_low = split(s)
    s_both = jnp.concatenate([s_high, s_low], axis=0)
    x_b = x.astype(BF16)
    both = dot(s_both, wide(x_b))
    e_b = (one - both[:size] - both[size:]).astype(BF16)
    x = x_b.astype(F32) + dot(x_b, wide(e_b))

    def step(x):
        x_high, x_low = split(x)
        both = dot(s_both, wide(x_high))
        e = one - both[:size] - both[size:] - dot(s_high, wide(x_low))
        return x + dot(x_high, wide(e.astype(BF16))), jnp.sum(e * e)

    x, left = step(x)
    out_ref[...] = x

    @pl.when(jnp.logical_not(left < DONE))
    def _():
        bound = jnp.sqrt(largest(jnp.sum(jnp.abs(s), axis=1, keepdims=True), 0))
        other = jnp.sqrt(largest(jnp.sum(jnp.abs(real_of(s)) + jnp.abs(imag_of(s)), axis=0, keepdims=True), 1))
        safe = s_dagger / (bound * bound) / (other * other)
        good = left < 0.5
        start = jnp.where(good, x, safe)

        def unfinished(state):
            count, value, _ = state
            return jnp.logical_and(count < STEPS_MAX, jnp.logical_not(value < DONE))

        def body(state):
            count, _, x = state
            new = product(x, one - product(s, x))
            e = one - product(s, x)
            return count + 1, jnp.sum(e * e), x + new

        _, _, result = lax.while_loop(unfinished, body, (0, left, start))
        out_ref[...] = result


def energy_at(index, energies_all):
    return -1.5 + 3.0 * (index + 0.5) / energies_all


def energy_point(axes):
    chips, cores, _ = axes
    index = lax.axis_index("chip") * cores + lax.axis_index("core")
    return energy_at(index.astype(F32), chips * cores)


def place(axes):
    position, cells_all = lax.axis_index("space"), axes[2]
    return position, jnp.minimum(position, cells_all - 1 - position), position < cells_all // 2


def outer_kernel(
    axes, onsite_far, hopping_far, sigma_far, system_ref, green_ref, message_ref, h_ref, hd_ref, onsite, hopping, sigma, arrivals
):
    copies = [
        pltpu.make_async_copy(far, near, arrivals.at[i])
        for i, (far, near) in enumerate(((onsite_far, onsite), (hopping_far, hopping), (sigma_far, sigma)))
    ]
    for copy in copies:
        copy.start()
    for copy in copies:
        copy.wait()
    position, depth, left = place(axes)
    last_level = axes[2] // 2 - 1
    energy = energy_point(axes)
    on = jnp.concatenate([onsite[0, 0], onsite[0, 1]], axis=1)
    sg = jnp.concatenate([sigma[0, 0, 0], sigma[0, 0, 1]], axis=1)
    h = jnp.concatenate([hopping[0, 0], hopping[0, 1]], axis=1)
    hd = dagger(h)
    h_ref[...] = h
    hd_ref[...] = hd
    shape = on.shape
    row = lax.broadcasted_iota(jnp.int32, shape, 0)
    column = lax.broadcasted_iota(jnp.int32, shape, 1)
    point = jnp.where(row == column, energy, 0.0) + jnp.where(row + shape[0] == column, BROADEN, 0.0)
    system_ref[...] = point - 0.5 * (on + dagger(on)) - sg

    @pl.when(position == 0)
    def _():
        magnitude = energy * energy + BROADEN * BROADEN
        system_ref[...] = system_ref[...] - times_complex(product(hd, h), energy / magnitude, -BROADEN / magnitude)

    @pl.when(depth == 0)
    def _():
        invert(system_ref[...], green_ref)
        send(left, last_level == 0, green_ref, h, hd, message_ref)

    @pl.when(depth != 0)
    def _():
        green_ref[...] = jnp.zeros(shape, F32)
        message_ref[...] = jnp.zeros(shape, F32)


def send(left, plain, green_ref, h, hd, message_ref):
    if plain:
        message_ref[...] = green_ref[...]
        return

    @pl.when(left)
    def _():
        message_ref[...] = green_ref[...]

    @pl.when(jnp.logical_not(left))
    def _():
        message_ref[...] = product(h, product(green_ref[...], hd))


def inward_kernel(axes, level, received, system, green, message, u, v, h, hd, system_ref, green_ref, message_ref, u_ref, v_ref):
    _, depth, left = place(axes)

    @pl.when(depth == level)
    def _():
        got = received[...]

        @pl.when(left)
        def _():
            gh = product(got, h[...])
            u_ref[...] = gh
            v_ref[...] = got
            system_ref[...] = system[...] - product(hd[...], gh)

        @pl.when(jnp.logical_not(left))
        def _():
            system_ref[...] = system[...] - got
            u_ref[...] = u[...]
            v_ref[...] = v[...]

        invert(system_ref[...], green_ref)
        send(left, level == axes[2] // 2 - 1, green_ref, h[...], hd[...], message_ref)

    @pl.when(depth != level)
    def _():
        system_ref[...] = system[...]
        green_ref[...] = green[...]
        message_ref[...] = message[...]
        u_ref[...] = u[...]
        v_ref[...] = v[...]


def middle_kernel(axes, received, system, green, h, hd, following, diagonal_ref, u_ref):
    _, depth, left = place(axes)

    @pl.when(depth == axes[2] // 2 - 1)
    def _():
        got = received[...]
        next_h = following[...]
        right_factor = jnp.where(left, dagger(next_h), h[...])
        left_factor = jnp.where(left, next_h, hd[...])
        gh = product(got, right_factor)
        u_ref[...] = gh
        invert(system[...] - product(left_factor, gh), diagonal_ref)

    @pl.when(depth != axes[2] // 2 - 1)
    def _():
        diagonal_ref[...] = green[...]
        u_ref[...] = jnp.zeros_like(u_ref)


def waiting_kernel(axes, received, diagonal, u_in, u_out, outside, h, hd, following, upper_ref, lower_ref, ready_ref):
    position, depth, left = place(axes)
    energy = energy_point(axes)
    magnitude = energy * energy + BROADEN * BROADEN
    contact_re, contact_im = energy / magnitude, -BROADEN / magnitude

    @pl.when(depth == axes[2] // 2 - 1)
    def _():
        u = jnp.where(left, u_out[...], u_in[...])
        v = product(hd[...], jnp.where(left, outside[...], received[...]))
        upper_ref[...] = product(u, diagonal[...])
        lower_ref[...] = product(diagonal[...], v)
        ready_ref[...] = jnp.zeros_like(ready_ref)

    @pl.when(depth != axes[2] // 2 - 1)
    def _():
        g = diagonal[...]
        next_h = following[...]
        right_in = jnp.where(left, dagger(next_h), h[...])
        left_in = jnp.where(left, next_h, hd[...])
        p = product(g, left_in)
        q = product(right_in, g)
        ready_ref[0] = p
        ready_ref[1] = q

        @pl.when(left)
        def _():
            at_contact = position == 0
            u = jnp.where(at_contact, times_complex(h[...], contact_re, contact_im), u_out[...])
            v = jnp.where(at_contact, times_complex(hd[...], contact_re, contact_im), product(hd[...], outside[...]))
            ready_ref[2] = product(u, p)
            ready_ref[3] = product(q, v)
            ready_ref[4] = product(u, g)
            ready_ref[5] = product(g, v)

        upper_ref[...] = jnp.zeros_like(upper_ref)
        lower_ref[...] = jnp.zeros_like(lower_ref)


def outward_kernel(axes, level, final, received, ready, diagonal, upper, lower, *outputs):
    _, depth, left = place(axes)
    if final:
        green_out, packed_ref, green_ref, upper_ref, lower_ref = outputs
    else:
        green_ref, upper_ref, lower_ref = outputs

    @pl.when(depth != level)
    def _():
        green_ref[...] = diagonal[...]
        upper_ref[...] = upper[...]
        lower_ref[...] = lower[...]

    @pl.when(depth == level)
    def _():
        g_in = received[...]
        p = ready[0]
        w = product(g_in, ready[1])
        green_ref[...] = diagonal[...] + product(p, w)

        @pl.when(left)
        def _():
            upper_ref[...] = ready[4] + product(ready[2], w)
            lower_ref[...] = ready[5] + product(p, product(g_in, ready[3]))

        @pl.when(jnp.logical_not(left))
        def _():
            upper_ref[...] = w
            lower_ref[...] = product(p, g_in)

    if final:
        size = diagonal.shape[0]
        blocks = (green_ref[...], upper_ref[...], lower_ref[...])
        for b, block in enumerate(blocks):
            green_out[b, 0] = real_of(block)
            green_out[b, 1] = imag_of(block)
        d0 = blocks[0] - dagger(blocks[0])
        d1 = blocks[1] - dagger(blocks[2])
        row = lax.broadcasted_iota(jnp.int32, (size, size), 0)
        column = lax.broadcasted_iota(jnp.int32, (size, size), 1)
        packed_ref[0] = jnp.where(row > column, real_of(d0), imag_of(d0))
        packed_ref[1] = real_of(d1)
        packed_ref[2] = imag_of(d1)


def add_term(axes, out, packed, kernel, index):
    chips, cores, _ = axes
    size = packed.shape[-1]
    energy = energy_at(index.astype(F32), chips * cores)
    occupation = 1.0 / (1.0 + jnp.exp(jnp.full((1, 1), energy / THERMAL, F32)))
    row = lax.broadcasted_iota(jnp.int32, (size, size), 0)
    column = lax.broadcasted_iota(jnp.int32, (size, size), 1)
    pack = packed[0]
    turned = pack.T
    d0_re = jnp.where(row > column, pack, jnp.where(row < column, -turned, 0.0))
    d0_im = jnp.where(row > column, turned, pack)
    d1_re, d1_im = packed[1], packed[2]
    d2_re, d2_im = -d1_re.T, d1_im.T
    for s, scale in enumerate((-occupation, 1.0 - occupation)):
        for b, (d_re, d_im) in enumerate(((d0_re, d0_im), (d1_re, d1_im), (d2_re, d2_im))):
            w_re, w_im = kernel[s, b, 0], kernel[s, b, 1]
            g_re, g_im = scale * d_re, scale * d_im
            out[s, b, 0] -= g_re * w_im + g_im * w_re
            out[s, b, 1] += g_re * w_re - g_im * w_im


def same_core_kernel(axes, *refs):
    chips, cores, _ = axes
    packs, own, other, out = refs[:chips], refs[chips], refs[chips + 1], refs[chips + 2]
    chip, core = lax.axis_index("chip"), lax.axis_index("core")
    out[...] = jnp.zeros_like(out)
    for r in range(chips):
        for c, kernels in enumerate((own, other)):
            @pl.when(jnp.logical_and(chip >= r, core == c))
            def _():
                add_term(axes, out, packs[r], kernels.at[r], (chip - r) * cores + core)


def other_core_kernel(axes, *refs):
    chips, cores, _ = axes
    packs, own, other, before, out = refs[:chips], refs[chips], refs[chips + 1], refs[chips + 2], refs[chips + 3]
    chip, core = lax.axis_index("chip"), lax.axis_index("core")
    out[...] = before[...]
    for r in range(chips):
        for c, kernels in ((0, other), (1, own)):
            if r - 1 + c >= 0:
                @pl.when(jnp.logical_and(chip >= r, core == c))
                def _():
                    add_term(axes, out, packs[r], kernels.at[r - 1 + c], (chip - r) * cores + 1 - core)


def local(axes, onsite, hopping, sigma_old, screened):
    chips, cores, cells_all = axes
    size = sigma_old.shape[-1]
    half = cells_all // 2
    matrix = jax.ShapeDtypeStruct((size, 2 * size), F32)
    cost = pl.CostEstimate(flops=2 * 40 * (2 * size) ** 3, bytes_accessed=2 * 1024 * 1024, transcendentals=0)

    def call(body, out_shape, *operands, space=pltpu.VMEM, grant=16, **options):
        spec = pl.BlockSpec(memory_space=pltpu.VMEM)
        return pl.pallas_call(
            functools.partial(body, axes),
            out_shape=out_shape,
            in_specs=[pl.BlockSpec(memory_space=space)] * len(operands),
            out_specs=jax.tree.map(lambda _: spec, out_shape),
            compiler_params=pltpu.CompilerParams(vmem_limit_bytes=grant * 1024 * 1024),
            cost_estimate=cost,
            **options,
        )(*operands)

    swap = [(i, i ^ 1) for i in range(cores)] if cores == 2 else []
    own_kernels = lax.all_gather(screened[0, 0], "chip", axis=0)
    system, green, message, h, hd = call(
        outer_kernel, (matrix,) * 5, onsite, hopping, sigma_old,
        space=pltpu.HBM,
        grant=60,
        scratch_shapes=[pltpu.VMEM(a.shape, F32) for a in (onsite, hopping, sigma_old)]
        + [pltpu.SemaphoreType.DMA((3,))],
    )
    following = None
    u_out = outside = jnp.zeros((size, 2 * size), F32)
    for level in range(1, half):
        route = [(level - 1, level), (cells_all - level, cells_all - 1 - level)]
        received = lax.ppermute(message, "space", route)
        if following is None:
            following = lax.ppermute(h, "space", [(i + 1, i) for i in range(cells_all - 1)])
        system, green, message, u_out, outside = call(
            functools.partial(swapped, inward_kernel, level),
            (matrix,) * 5,
            received, system, green, message, u_out, outside, h, hd,
        )
    received = lax.ppermute(message, "space", [(half - 1, half), (half, half - 1)])
    if following is None:
        following = lax.ppermute(h, "space", [(i + 1, i) for i in range(cells_all - 1)])
    diagonal, u_in = call(
        middle_kernel, (matrix,) * 2, received, system, green, h, hd, following
    )
    upper = None
    for level in reversed(range(half - 1)):
        route = [(level + 1, level), (cells_all - 2 - level, cells_all - 1 - level)]
        arrived = lax.ppermute(diagonal, "space", route)
        if upper is None:
            upper, lower, ready = call(
                waiting_kernel,
                (matrix, matrix, jax.ShapeDtypeStruct((6, size, 2 * size), F32)),
                received, diagonal, u_in, u_out, outside, h, hd, following,
            )
        final = level == 0
        shapes = (matrix,) * 3
        if final:
            shapes = (
                jax.ShapeDtypeStruct((3, 2, size, size), F32),
                jax.ShapeDtypeStruct((3, size, size), F32),
            ) + shapes
        results = call(
            functools.partial(swapped, outward_kernel, level, final),
            shapes,
            arrived, ready, diagonal, upper, lower,
        )
        diagonal, upper, lower = results[-3:]
    green_out, packed = results[:2]
    own = [packed] + [
        lax.ppermute(packed, "chip", [(i, i + r) for i in range(chips - r)]) for r in range(1, chips)
    ]
    other = [lax.ppermute(pack, "core", swap) for pack in own]
    own_kernels, other[0] = lax.optimization_barrier((own_kernels, other[0]))
    other_kernels = lax.ppermute(own_kernels, "core", swap)
    result = jax.ShapeDtypeStruct((2, 3, 2, size, size), F32)
    partial = call(same_core_kernel, result, *own, own_kernels, other_kernels)
    sigma_out = call(other_core_kernel, result, *other, own_kernels, other_kernels, partial)
    return green_out[None, None], sigma_out[None, None]


def swapped(body, *arguments):
    fixed = [a for a in arguments if isinstance(a, (int, bool))]
    axes, *refs = arguments[len(fixed) :]
    return body(axes, *fixed, *refs)


def solution(mesh):
    cores = 2 if mesh.shape["energy"] % 2 == 0 else 1
    axes = (mesh.shape["energy"] // cores, cores, mesh.shape["space"])
    split_mesh = jax.sharding.Mesh(mesh.devices.reshape(axes), ("chip", "core", "space"))
    energy = ("chip", "core")
    placed = (
        P("space", None, None, None),
        P("space", None, None, None),
        P(energy, "space", None, None, None),
        P(energy, "space", None, None, None, None, None),
    )
    return jax.shard_map(
        functools.partial(local, axes),
        mesh=split_mesh,
        in_specs=placed,
        out_specs=(
            P(energy, "space", None, None, None, None),
            P(energy, "space", None, None, None, None, None),
        ),
        check_vma=False,
    )
```

```python
import functools
import math

import jax
import jax.numpy as jnp
from jax import lax
from jax.experimental import pallas as pl
from jax.experimental.pallas import tpu as pltpu
from jax.sharding import PartitionSpec as P

BROADEN = 0.45
THERMAL = 0.1
F32 = jnp.float32
BF16 = jnp.bfloat16

LOWEST = 1.0 / 128.0
SQUARINGS = 6
DONE = 1e-4
STEPS_MAX = 60
WORK = 1
WORK2 = 8
WORK3 = 1
WORK4 = 1
WORK5 = 0.01
WORK6 = 1


def schedule():
    rho = (1.0 - LOWEST) / (1.0 + LOWEST)
    scales = []
    for _ in range(SQUARINGS):
        scales.append(2.0 / (2.0 - rho * rho))
        rho = rho * rho / (2.0 - rho * rho)
    return 2.0 / (1.0 + LOWEST), scales


def real_of(x):
    return x[:, : x.shape[1] // 2]


def imag_of(x):
    return x[:, x.shape[1] // 2 :]


def wide(x):
    return jnp.concatenate([x, jnp.concatenate([-imag_of(x), real_of(x)], axis=1)], axis=0)


def dagger(x):
    return jnp.concatenate([real_of(x).T, -imag_of(x).T], axis=1)


def dot(a, b):
    return jnp.dot(a, b, preferred_element_type=F32)


def split(x):
    high = x.astype(BF16)
    return high, (x - high.astype(F32)).astype(BF16)


def product(a, b):
    rows = a.shape[0]
    a_high, a_low = split(a)
    b_high, b_low = split(b)
    both = dot(jnp.concatenate([a_high, a_low], axis=0), wide(b_high))
    return both[:rows] + both[rows:] + dot(a_high, wide(b_low))


def times_complex(x, re, im):
    return jnp.concatenate(
        [re * real_of(x) - im * imag_of(x), re * imag_of(x) + im * real_of(x)], axis=1
    )


def identity_like(x):
    size = x.shape[0]
    row = lax.broadcasted_iota(jnp.int32, x.shape, 0)
    column = lax.broadcasted_iota(jnp.int32, x.shape, 1)
    return jnp.where(row == column, 1.0, 0.0).astype(F32)


def largest(x, axis):
    return jnp.max(x, axis=axis, keepdims=True)


def invert(s, out_ref):
    size = s.shape[0]
    one = identity_like(s)
    first, scales = schedule()
    s_dagger = dagger(s)
    s_dagger_b = s_dagger.astype(BF16)
    normal = dot(s.astype(BF16), wide(s_dagger_b))
    normal_b = normal.astype(BF16)
    both = dot(jnp.concatenate([s_dagger_b, normal_b], axis=0), wide(normal_b))
    square = both[size:]
    sums = jnp.sum(jnp.sqrt(real_of(square) ** 2 + imag_of(square) ** 2), axis=0, keepdims=True)
    a = first * lax.rsqrt(largest(sums, 1))
    c = scales[0]
    x = (2.0 * c * a) * s_dagger - (c * a * a) * both[:size]
    r = one - (2.0 * c * a) * normal + (c * a * a) * square
    for c in scales[1:]:
        r_b = r.astype(BF16)
        both = dot(jnp.concatenate([x.astype(BF16), r_b], axis=0), wide(r_b))
        x = c * (x + both[:size])
        r = (1.0 - c) * one + c * both[size:]
    s_high, s_low = split(s)
    s_both = jnp.concatenate([s_high, s_low], axis=0)
    x_b = x.astype(BF16)
    both = dot(s_both, wide(x_b))
    e_b = (one - both[:size] - both[size:]).astype(BF16)
    x = x_b.astype(F32) + dot(x_b, wide(e_b))

    def step(x):
        x_high, x_low = split(x)
        both = dot(s_both, wide(x_high))
        e = one - both[:size] - both[size:] - dot(s_high, wide(x_low))
        return x + dot(x_high, wide(e.astype(BF16))), jnp.sum(e * e)

    x, left = step(x)
    out_ref[...] = x

    @pl.when(jnp.logical_not(left < DONE))
    def _():
        bound = jnp.sqrt(largest(jnp.sum(jnp.abs(s), axis=1, keepdims=True), 0))
        other = jnp.sqrt(largest(jnp.sum(jnp.abs(real_of(s)) + jnp.abs(imag_of(s)), axis=0, keepdims=True), 1))
        safe = s_dagger / (bound * bound) / (other * other)
        good = left < 0.5
        start = jnp.where(good, x, safe)

        def unfinished(state):
            count, value, _ = state
            return jnp.logical_and(count < STEPS_MAX, jnp.logical_not(value < DONE))

        def body(state):
            count, _, x = state
            new = product(x, one - product(s, x))
            e = one - product(s, x)
            return count + 1, jnp.sum(e * e), x + new

        _, _, result = lax.while_loop(unfinished, body, (0, left, start))
        out_ref[...] = result


def energy_at(index, energies_all):
    return -1.5 + 3.0 * (index + 0.5) / energies_all


def energy_point(axes):
    chips, cores, _ = axes
    index = lax.axis_index("chip") * cores + lax.axis_index("core")
    return energy_at(index.astype(F32), chips * cores)


def place(axes):
    position, cells_all = lax.axis_index("space"), axes[2]
    return position, jnp.minimum(position, cells_all - 1 - position), position < cells_all // 2


def outer_kernel(
    axes, onsite_far, hopping_far, sigma_far, system_ref, green_ref, message_ref, h_ref, hd_ref, token_ref, onsite, hopping, sigma, arrivals
):
    copies = [
        pltpu.make_async_copy(far, near, arrivals.at[i])
        for i, (far, near) in enumerate(((onsite_far, onsite), (hopping_far, hopping), (sigma_far, sigma)))
    ]
    for copy in copies:
        copy.start()
    for copy in copies:
        copy.wait()
    position, depth, left = place(axes)
    last_level = axes[2] // 2 - 1
    energy = energy_point(axes)
    on = jnp.concatenate([onsite[0, 0], onsite[0, 1]], axis=1)
    sg = jnp.concatenate([sigma[0, 0, 0], sigma[0, 0, 1]], axis=1)
    h = jnp.concatenate([hopping[0, 0], hopping[0, 1]], axis=1)
    hd = dagger(h)
    h_ref[...] = h
    token_ref[...] = jnp.zeros_like(token_ref)
    hd_ref[...] = hd
    shape = on.shape
    row = lax.broadcasted_iota(jnp.int32, shape, 0)
    column = lax.broadcasted_iota(jnp.int32, shape, 1)
    point = jnp.where(row == column, energy, 0.0) + jnp.where(row + shape[0] == column, BROADEN, 0.0)
    system_ref[...] = point - 0.5 * (on + dagger(on)) - sg

    @pl.when(position == 0)
    def _():
        magnitude = energy * energy + BROADEN * BROADEN
        system_ref[...] = system_ref[...] - times_complex(product(hd, h), energy / magnitude, -BROADEN / magnitude)

    @pl.when(depth == 0)
    def _():
        invert(system_ref[...], green_ref)
        send(left, last_level == 0, green_ref, h, hd, message_ref)

    @pl.when(depth != 0)
    def _():
        green_ref[...] = jnp.zeros(shape, F32)
        message_ref[...] = jnp.zeros(shape, F32)


def send(left, plain, green_ref, h, hd, message_ref):
    if plain:
        message_ref[...] = green_ref[...]
        return

    @pl.when(left)
    def _():
        message_ref[...] = green_ref[...]

    @pl.when(jnp.logical_not(left))
    def _():
        message_ref[...] = product(h, product(green_ref[...], hd))


def inward_kernel(axes, level, _, received, system, green, message, u, v, h, hd, system_ref, green_ref, message_ref, u_ref, v_ref):
    _, depth, left = place(axes)

    @pl.when(depth == level)
    def _():
        got = received[...]

        @pl.when(left)
        def _():
            gh = product(got, h[...])
            u_ref[...] = gh
            v_ref[...] = got
            system_ref[...] = system[...] - product(hd[...], gh)

        @pl.when(jnp.logical_not(left))
        def _():
            system_ref[...] = system[...] - got
            u_ref[...] = u[...]
            v_ref[...] = v[...]

        invert(system_ref[...], green_ref)
        send(left, level == axes[2] // 2 - 1, green_ref, h[...], hd[...], message_ref)

    @pl.when(depth != level)
    def _():
        system_ref[...] = system[...]
        green_ref[...] = green[...]
        message_ref[...] = message[...]
        u_ref[...] = u[...]
        v_ref[...] = v[...]


def middle_kernel(axes, received, system, green, h, hd, following, diagonal_ref, u_ref, token_ref):
    token_ref[...] = jnp.zeros_like(token_ref)
    _, depth, left = place(axes)

    @pl.when(depth == axes[2] // 2 - 1)
    def _():
        got = received[...]
        next_h = following[...]
        right_factor = jnp.where(left, dagger(next_h), h[...])
        left_factor = jnp.where(left, next_h, hd[...])
        gh = product(got, right_factor)
        u_ref[...] = gh
        invert(system[...] - product(left_factor, gh), diagonal_ref)

    @pl.when(depth != axes[2] // 2 - 1)
    def _():
        diagonal_ref[...] = green[...]
        u_ref[...] = jnp.zeros_like(u_ref)


def waiting_kernel(axes, _, received, diagonal, u_in, u_out, outside, h, hd, following, upper_ref, lower_ref, ready_ref):
    position, depth, left = place(axes)
    energy = energy_point(axes)
    magnitude = energy * energy + BROADEN * BROADEN
    contact_re, contact_im = energy / magnitude, -BROADEN / magnitude

    @pl.when(depth == axes[2] // 2 - 1)
    def _():
        u = jnp.where(left, u_out[...], u_in[...])
        v = product(hd[...], jnp.where(left, outside[...], received[...]))
        upper_ref[...] = product(u, diagonal[...])
        lower_ref[...] = product(diagonal[...], v)
        ready_ref[...] = jnp.zeros_like(ready_ref)

    @pl.when(depth != axes[2] // 2 - 1)
    def _():
        g = diagonal[...]
        next_h = following[...]
        right_in = jnp.where(left, dagger(next_h), h[...])
        left_in = jnp.where(left, next_h, hd[...])
        p = product(g, left_in)
        q = product(right_in, g)
        ready_ref[0] = p
        ready_ref[1] = q

        @pl.when(left)
        def _():
            at_contact = position == 0
            u = jnp.where(at_contact, times_complex(h[...], contact_re, contact_im), u_out[...])
            v = jnp.where(at_contact, times_complex(hd[...], contact_re, contact_im), product(hd[...], outside[...]))
            ready_ref[2] = product(u, p)
            ready_ref[3] = product(q, v)
            ready_ref[4] = product(u, g)
            ready_ref[5] = product(g, v)

        upper_ref[...] = jnp.zeros_like(upper_ref)
        lower_ref[...] = jnp.zeros_like(lower_ref)


def outward_kernel(axes, level, final, received, ready, diagonal, upper, lower, *outputs):
    _, depth, left = place(axes)
    if final:
        green_out, packed_ref, green_ref, upper_ref, lower_ref = outputs
    else:
        green_ref, upper_ref, lower_ref = outputs

    @pl.when(depth != level)
    def _():
        green_ref[...] = diagonal[...]
        upper_ref[...] = upper[...]
        lower_ref[...] = lower[...]

    @pl.when(depth == level)
    def _():
        g_in = received[...]
        p = ready[0]
        w = product(g_in, ready[1])
        green_ref[...] = diagonal[...] + product(p, w)

        @pl.when(left)
        def _():
            upper_ref[...] = ready[4] + product(ready[2], w)
            lower_ref[...] = ready[5] + product(p, product(g_in, ready[3]))

        @pl.when(jnp.logical_not(left))
        def _():
            upper_ref[...] = w
            lower_ref[...] = product(p, g_in)

    if final:
        size = diagonal.shape[0]
        blocks = (green_ref[...], upper_ref[...], lower_ref[...])
        for b, block in enumerate(blocks):
            green_out[b, 0] = real_of(block)
            green_out[b, 1] = imag_of(block)
        d0 = blocks[0] - dagger(blocks[0])
        d1 = blocks[1] - dagger(blocks[2])
        row = lax.broadcasted_iota(jnp.int32, (size, size), 0)
        column = lax.broadcasted_iota(jnp.int32, (size, size), 1)
        packed_ref[0] = jnp.where(row > column, real_of(d0), imag_of(d0))
        packed_ref[1] = real_of(d1)
        packed_ref[2] = imag_of(d1)


def unpack(pack, out):
    size = pack.shape[-1]
    row = lax.broadcasted_iota(jnp.int32, (size, size), 0)
    column = lax.broadcasted_iota(jnp.int32, (size, size), 1)
    mixed = pack[0]
    turned = mixed.T
    out[0, 0] = jnp.where(row > column, mixed, jnp.where(row < column, -turned, 0.0))
    out[0, 1] = jnp.where(row > column, turned, mixed)
    out[1] = pack[1:]
    out[2, 0] = -pack[1].T
    out[2, 1] = pack[2].T


def add_term(axes, out, spectral, blocks, index):
    chips, cores, _ = axes
    energy = energy_at(index.astype(F32), chips * cores)
    occupation = 1.0 / (1.0 + jnp.exp(jnp.full((1, 1), energy / THERMAL, F32)))
    for s, scale in enumerate((-occupation, 1.0 - occupation)):
        kernel = blocks(s)
        for b in range(3):
            w_re, w_im = kernel[b, 0], kernel[b, 1]
            g_re, g_im = scale * spectral[b, 0], scale * spectral[b, 1]
            out[s, b, 0] -= g_re * w_im + g_im * w_re
            out[s, b, 1] += g_re * w_re - g_im * w_im


def terms_kernel(axes, same, *refs):
    chips, cores, _ = axes
    packs, rest = refs[:chips], refs[chips:]
    before, spectral, out = rest[0] if not same else None, rest[-1], rest[-2]
    pieces = rest[: len(rest) - 2] if same else rest[1 : len(rest) - 2]
    half = len(pieces) // 2
    own, other = kernel_blocks(chips, pieces[:half]), kernel_blocks(chips, pieces[half:])
    chip, core = lax.axis_index("chip"), lax.axis_index("core")
    out[...] = jnp.zeros_like(out) if same else before[...]
    for r in range(chips):
        @pl.when(chip >= r)
        def _():
            unpack(packs[r], spectral.at[r])
    for offset in range(chips):
        chip_of = jnp.bitwise_xor(chip, offset) if len(pieces) > 2 else jnp.int32(offset)
        for c in range(cores):
            r = chip_of if same else chip_of + 1 - c
            source = (own if c == 0 else other) if same else (other if c == 0 else own)
            origin = core if same else 1 - core

            @pl.when(jnp.logical_and(core == c, r <= chip))
            def _():
                blocks = functools.partial(source[offset], chip_of)
                add_term(axes, out, spectral.at[r], blocks, (chip - r) * cores + origin)


class Exchange:
    def __init__(self, chips, cores, screened):
        self.paired = chips == 4
        self.swap = [(i, i ^ 1) for i in range(cores)] if cores == 2 else []
        self.own = screened[0, 0]
        self.early = []
        self.pieces = [self.own] if self.paired else [lax.all_gather(self.own, "chip", axis=0)]

    def moved(self, piece, offset):
        return lax.ppermute(piece, "chip", [(i, i ^ offset) for i in range(4)])

    def begin(self, after):
        if self.paired:
            own, _ = lax.optimization_barrier((self.own, after))
            self.pieces += [self.moved(own, 1), self.moved(own, 2)]

    def go_on(self, after):
        if self.paired:
            one, two = self.pieces[1:]
            one, two, _ = lax.optimization_barrier((one, two, after))
            self.pieces += [self.moved(one[:1], 2), self.moved(two[1:], 1)]
            own, one, two, _ = lax.optimization_barrier((*self.pieces[:3], after))
            self.early = [lax.ppermute(piece, "core", self.swap) for piece in (own, one, two)]

    def finish(self, after):
        late = self.pieces[3:] if self.paired else self.pieces
        *late, _ = lax.optimization_barrier((*late, after))
        return self.pieces, self.early + [lax.ppermute(piece, "core", self.swap) for piece in late]


def kernel_blocks(chips, pieces):
    if len(pieces) == 1:
        return [(lambda chip_of, kind: pieces[0].at[chip_of, kind])] * chips
    found = [(lambda chip_of, kind, piece=piece: piece.at[kind]) for piece in pieces[:3]]
    return found + [lambda chip_of, kind: pieces[3 + kind].at[0]]


def local(axes, onsite, hopping, sigma_old, screened):
    chips, cores, cells_all = axes
    size = sigma_old.shape[-1]
    half = cells_all // 2
    matrix = jax.ShapeDtypeStruct((size, 2 * size), F32)
    def call(body, out_shape, *operands, space=pltpu.VMEM, grant=16, work=WORK, **options):
        spec = pl.BlockSpec(memory_space=pltpu.VMEM)
        return pl.pallas_call(
            functools.partial(body, axes),
            out_shape=out_shape,
            in_specs=[pl.BlockSpec(memory_space=space)] * len(operands),
            out_specs=jax.tree.map(lambda _: spec, out_shape),
            compiler_params=pltpu.CompilerParams(vmem_limit_bytes=grant * 1024 * 1024),
            cost_estimate=pl.CostEstimate(
                flops=int(work * 80 * (2 * size) ** 3), bytes_accessed=2 * 1024 * 1024, transcendentals=0
            ),
            **options,
        )(*operands)

    swap = [(i, i ^ 1) for i in range(cores)] if cores == 2 else []
    exchange = Exchange(chips, cores, screened)
    token = jax.ShapeDtypeStruct((8, size), F32)
    system, green, message, h, hd, mark = call(
        outer_kernel,
        (matrix,) * 5 + (token,),
        *(pltpu.with_memory_space_constraint(a, pltpu.HBM) for a in (onsite, hopping, sigma_old)),
        space=pltpu.HBM,
        scratch_shapes=[pltpu.VMEM(a.shape, F32) for a in (onsite, hopping, sigma_old)]
        + [pltpu.SemaphoreType.DMA((3,))],
    )
    mark = lax.ppermute(mark, "core", swap)
    exchange.begin(mark)
    h_sent, _ = lax.optimization_barrier((h, mark))
    following = lax.ppermute(h_sent, "space", [(i + 1, i) for i in range(cells_all - 1)])
    u_out = outside = jnp.zeros((size, 2 * size), F32)
    for level in range(1, half):
        route = [(level - 1, level), (cells_all - level, cells_all - 1 - level)]
        received = lax.ppermute(message, "space", route)
        if level == 1:
            received, following = lax.optimization_barrier((received, following))
        system, green, message, u_out, outside = call(
            functools.partial(swapped, inward_kernel, level),
            (matrix,) * 5,
            mark, received, system, green, message, u_out, outside, h, hd,
            work=WORK2,
        )
    received = lax.ppermute(message, "space", [(half - 1, half), (half, half - 1)])
    diagonal, u_in, mark = call(
        middle_kernel, (matrix,) * 2 + (token,), received, system, green, h, hd, following,
        work=WORK3,
    )
    mark = lax.ppermute(mark, "core", swap)
    exchange.go_on(mark)
    upper = None
    for level in reversed(range(half - 1)):
        route = [(level + 1, level), (cells_all - 2 - level, cells_all - 1 - level)]
        arrived = lax.ppermute(diagonal, "space", route)
        if upper is None:
            upper, lower, ready = call(
                waiting_kernel,
                (matrix, matrix, jax.ShapeDtypeStruct((6, size, 2 * size), F32)),
                mark, received, diagonal, u_in, u_out, outside, h, hd, following,
                work=WORK4,
            )
        final = level == 0
        shapes = (matrix,) * 3
        if final:
            shapes = (
                jax.ShapeDtypeStruct((3, 2, size, size), F32),
                jax.ShapeDtypeStruct((3, size, size), F32),
            ) + shapes
        results = call(
            functools.partial(swapped, outward_kernel, level, final),
            shapes,
            arrived, ready, diagonal, upper, lower,
            work=WORK6,
        )
        diagonal, upper, lower = results[-3:]
    green_out, packed = results[:2]
    own = [packed] + [
        lax.ppermute(packed, "chip", [(i, i + r) for i in range(chips - r)]) for r in range(1, chips)
    ]
    if exchange.paired:
        *arrived, exchange.pieces[3], exchange.pieces[4] = lax.optimization_barrier((*own[1:], *exchange.pieces[3:]))
        own[1:] = arrived
    other = [lax.ppermute(pack, "core", swap) for pack in own]
    pieces, other_pieces = exchange.finish(own[1:] if chips > 1 else packed)
    result = jax.ShapeDtypeStruct((2, 3, 2, size, size), F32)
    unpacked = [pltpu.VMEM((chips, 3, 2, size, size), F32)]
    partial = call(
        functools.partial(swapped, terms_kernel, True), result, *own, *pieces, *other_pieces,
        scratch_shapes=unpacked,
        work=WORK5,
    )
    sigma_out = call(
        functools.partial(swapped, terms_kernel, False), result, *other, partial, *pieces, *other_pieces,
        scratch_shapes=unpacked,
    )
    return green_out[None, None], sigma_out[None, None]


def swapped(body, *arguments):
    fixed = [a for a in arguments if isinstance(a, (int, bool))]
    axes, *refs = arguments[len(fixed) :]
    return body(axes, *fixed, *refs)


def solution(mesh):
    cores = 2 if mesh.shape["energy"] % 2 == 0 else 1
    axes = (mesh.shape["energy"] // cores, cores, mesh.shape["space"])
    split_mesh = jax.sharding.Mesh(mesh.devices.reshape(axes), ("chip", "core", "space"))
    energy = ("chip", "core")
    placed = (
        P("space", None, None, None),
        P("space", None, None, None),
        P(energy, "space", None, None, None),
        P(energy, "space", None, None, None, None, None),
    )
    return jax.shard_map(
        functools.partial(local, axes),
        mesh=split_mesh,
        in_specs=placed,
        out_specs=(
            P(energy, "space", None, None, None, None),
            P(energy, "space", None, None, None, None, None),
        ),
        check_vma=False,
    )
```

```python
import functools
import math

import jax
import jax.numpy as jnp
from jax import lax
from jax.experimental import pallas as pl
from jax.experimental.pallas import tpu as pltpu
from jax.sharding import PartitionSpec as P

BROADEN = 0.45
THERMAL = 0.1
F32 = jnp.float32
BF16 = jnp.bfloat16

LOWEST = 1.0 / 128.0
SQUARINGS = 6
DONE = 1e-4
STEPS_MAX = 60
WORK = 1
WORK2 = 8
WORK3 = 1
WORK4 = 1
WORK5 = 0.01
WORK6 = 1


def schedule():
    rho = (1.0 - LOWEST) / (1.0 + LOWEST)
    scales = []
    for _ in range(SQUARINGS):
        scales.append(2.0 / (2.0 - rho * rho))
        rho = rho * rho / (2.0 - rho * rho)
    return 2.0 / (1.0 + LOWEST), scales


def real_of(x):
    return x[:, : x.shape[1] // 2]


def imag_of(x):
    return x[:, x.shape[1] // 2 :]


def wide(x):
    return jnp.concatenate([x, jnp.concatenate([-imag_of(x), real_of(x)], axis=1)], axis=0)


def dagger(x):
    return jnp.concatenate([real_of(x).T, -imag_of(x).T], axis=1)


def dot(a, b):
    return jnp.dot(a, b, preferred_element_type=F32)


def split(x):
    high = x.astype(BF16)
    return high, (x - high.astype(F32)).astype(BF16)


def product(a, b):
    rows = a.shape[0]
    a_high, a_low = split(a)
    b_high, b_low = split(b)
    both = dot(jnp.concatenate([a_high, a_low], axis=0), wide(b_high))
    return both[:rows] + both[rows:] + dot(a_high, wide(b_low))


def times_complex(x, re, im):
    return jnp.concatenate(
        [re * real_of(x) - im * imag_of(x), re * imag_of(x) + im * real_of(x)], axis=1
    )


def identity_like(x):
    size = x.shape[0]
    row = lax.broadcasted_iota(jnp.int32, x.shape, 0)
    column = lax.broadcasted_iota(jnp.int32, x.shape, 1)
    return jnp.where(row == column, 1.0, 0.0).astype(F32)


def largest(x, axis):
    return jnp.max(x, axis=axis, keepdims=True)


def invert(s, out_ref):
    size = s.shape[0]
    one = identity_like(s)
    first, scales = schedule()
    s_dagger = dagger(s)
    s_dagger_b = s_dagger.astype(BF16)
    normal = dot(s.astype(BF16), wide(s_dagger_b))
    normal_b = normal.astype(BF16)
    both = dot(jnp.concatenate([s_dagger_b, normal_b], axis=0), wide(normal_b))
    square = both[size:]
    sums = jnp.sum(jnp.sqrt(real_of(square) ** 2 + imag_of(square) ** 2), axis=0, keepdims=True)
    a = first * lax.rsqrt(largest(sums, 1))
    c = scales[0]
    x = (2.0 * c * a) * s_dagger - (c * a * a) * both[:size]
    r = one - (2.0 * c * a) * normal + (c * a * a) * square
    for c in scales[1:]:
        r_b = r.astype(BF16)
        both = dot(jnp.concatenate([x.astype(BF16), r_b], axis=0), wide(r_b))
        x = c * (x + both[:size])
        r = (1.0 - c) * one + c * both[size:]
    s_high, s_low = split(s)
    s_both = jnp.concatenate([s_high, s_low], axis=0)
    x_b = x.astype(BF16)
    both = dot(s_both, wide(x_b))
    e_b = (one - both[:size] - both[size:]).astype(BF16)
    x = x_b.astype(F32) + dot(x_b, wide(e_b))

    def step(x):
        x_high, x_low = split(x)
        both = dot(s_both, wide(x_high))
        e = one - both[:size] - both[size:] - dot(s_high, wide(x_low))
        return x + dot(x_high, wide(e.astype(BF16))), jnp.sum(e * e)

    x, left = step(x)
    out_ref[...] = x

    @pl.when(jnp.logical_not(left < DONE))
    def _():
        bound = jnp.sqrt(largest(jnp.sum(jnp.abs(s), axis=1, keepdims=True), 0))
        other = jnp.sqrt(largest(jnp.sum(jnp.abs(real_of(s)) + jnp.abs(imag_of(s)), axis=0, keepdims=True), 1))
        safe = s_dagger / (bound * bound) / (other * other)
        good = left < 0.5
        start = jnp.where(good, x, safe)

        def unfinished(state):
            count, value, _ = state
            return jnp.logical_and(count < STEPS_MAX, jnp.logical_not(value < DONE))

        def body(state):
            count, _, x = state
            new = product(x, one - product(s, x))
            e = one - product(s, x)
            return count + 1, jnp.sum(e * e), x + new

        _, _, result = lax.while_loop(unfinished, body, (0, left, start))
        out_ref[...] = result


def energy_at(index, energies_all):
    return -1.5 + 3.0 * (index + 0.5) / energies_all


def energy_point(axes):
    chips, cores, _ = axes
    index = lax.axis_index("chip") * cores + lax.axis_index("core")
    return energy_at(index.astype(F32), chips * cores)


def place(axes):
    position, cells_all = lax.axis_index("space"), axes[2]
    return position, jnp.minimum(position, cells_all - 1 - position), position < cells_all // 2


def outer_kernel(
    axes, onsite_far, hopping_far, sigma_far, system_ref, green_ref, message_ref, h_ref, hd_ref, token_ref, onsite, hopping, sigma, arrivals
):
    copies = [
        pltpu.make_async_copy(far, near, arrivals.at[i])
        for i, (far, near) in enumerate(((onsite_far, onsite), (hopping_far, hopping), (sigma_far, sigma)))
    ]
    for copy in copies:
        copy.start()
    for copy in copies:
        copy.wait()
    position, depth, left = place(axes)
    energy = energy_point(axes)
    on = jnp.concatenate([onsite[0, 0], onsite[0, 1]], axis=1)
    sg = jnp.concatenate([sigma[0, 0, 0], sigma[0, 0, 1]], axis=1)
    h = jnp.concatenate([hopping[0, 0], hopping[0, 1]], axis=1)
    hd = dagger(h)
    h_ref[...] = h
    token_ref[...] = jnp.zeros_like(token_ref)
    hd_ref[...] = hd
    shape = on.shape
    row = lax.broadcasted_iota(jnp.int32, shape, 0)
    column = lax.broadcasted_iota(jnp.int32, shape, 1)
    point = jnp.where(row == column, energy, 0.0) + jnp.where(row + shape[0] == column, BROADEN, 0.0)
    system_ref[...] = point - 0.5 * (on + dagger(on)) - sg

    @pl.when(position == 0)
    def _():
        magnitude = energy * energy + BROADEN * BROADEN
        system_ref[...] = system_ref[...] - times_complex(product(hd, h), energy / magnitude, -BROADEN / magnitude)

    @pl.when(depth == 0)
    def _():
        invert(system_ref[...], green_ref)
        send(left, green_ref, h, hd, message_ref)

    @pl.when(depth != 0)
    def _():
        green_ref[...] = jnp.zeros(shape, F32)
        message_ref[...] = jnp.zeros(shape, F32)


def send(plain, green_ref, h, hd, message_ref):
    @pl.when(plain)
    def _():
        message_ref[...] = green_ref[...]

    @pl.when(jnp.logical_not(plain))
    def _():
        message_ref[...] = product(h, product(green_ref[...], hd))


def inward_kernel(axes, level, _, received, system, green, message, u, outside, h, hd, system_ref, green_ref, message_ref, u_ref, outside_ref):
    _, depth, left = place(axes)

    @pl.when(depth == level)
    def _():
        got = received[...]

        @pl.when(left)
        def _():
            gh = product(got, h[...])
            u_ref[...] = gh
            outside_ref[...] = got
            system_ref[...] = system[...] - product(hd[...], gh)

        @pl.when(jnp.logical_not(left))
        def _():
            system_ref[...] = system[...] - got
            u_ref[...] = u[...]
            outside_ref[...] = outside[...]

        invert(system_ref[...], green_ref)
        send(left, green_ref, h[...], hd[...], message_ref)

    @pl.when(depth != level)
    def _():
        system_ref[...] = system[...]
        green_ref[...] = green[...]
        message_ref[...] = message[...]
        u_ref[...] = u[...]
        outside_ref[...] = outside[...]


def middle_kernel(axes, received, system, green, h, hd, diagonal_ref, message_ref, u_ref, token_ref):
    token_ref[...] = jnp.zeros_like(token_ref)
    _, depth, left = place(axes)

    @pl.when(depth == axes[2] // 2 - 1)
    def _():
        got = received[...]

        @pl.when(left)
        def _():
            u_ref[...] = system[...] - got

        @pl.when(jnp.logical_not(left))
        def _():
            message_ref[...] = product(got, h[...])
            u_ref[...] = system[...] - product(hd[...], message_ref[...])

        s = u_ref[...]
        u_ref[...] = message_ref[...]
        invert(s, diagonal_ref)
        send(jnp.logical_not(left), diagonal_ref, h[...], hd[...], message_ref)

    @pl.when(depth != axes[2] // 2 - 1)
    def _():
        diagonal_ref[...] = green[...]
        u_ref[...] = jnp.zeros_like(u_ref)
        message_ref[...] = jnp.zeros_like(message_ref)


def waiting_kernel(axes, extra, *refs):
    received, diagonal, u_in, u_out, outside, h, hd, *rest = refs[1:]
    if extra:
        one, two, upper_ref, lower_ref, ready_ref, first_ref, second_ref, arrivals = rest
        copies = [
            pltpu.make_async_copy(one.at[:1], first_ref, arrivals.at[0]),
            pltpu.make_async_copy(two.at[1:], second_ref, arrivals.at[1]),
        ]
        for copy in copies:
            copy.start()
    else:
        upper_ref, lower_ref, ready_ref = rest
    position, depth, left = place(axes)
    energy = energy_point(axes)
    magnitude = energy * energy + BROADEN * BROADEN
    contact_re, contact_im = energy / magnitude, -BROADEN / magnitude

    @pl.when(depth == axes[2] // 2 - 1)
    def _():
        u = jnp.where(left, u_out[...], u_in[...])
        v = product(hd[...], jnp.where(left, outside[...], received[...]))
        upper_ref[...] = product(u, diagonal[...])
        lower_ref[...] = product(diagonal[...], v)
        ready_ref[...] = jnp.zeros_like(ready_ref)

    @pl.when(depth != axes[2] // 2 - 1)
    def _():
        g = diagonal[...]

        @pl.when(left)
        def _():
            at_contact = position == 0
            u = jnp.where(at_contact, times_complex(h[...], contact_re, contact_im), u_out[...])
            v = jnp.where(at_contact, times_complex(hd[...], contact_re, contact_im), product(hd[...], outside[...]))
            ready_ref[0] = g
            ready_ref[1] = g
            ready_ref[2] = product(u, g)
            ready_ref[3] = product(g, v)

        @pl.when(jnp.logical_not(left))
        def _():
            ready_ref[0] = product(g, hd[...])
            ready_ref[1] = product(h[...], g)
            ready_ref[2] = jnp.zeros_like(g)
            ready_ref[3] = jnp.zeros_like(g)

        upper_ref[...] = jnp.zeros_like(upper_ref)
        lower_ref[...] = jnp.zeros_like(lower_ref)

    if extra:
        for copy in copies:
            copy.wait()


def outward_kernel(axes, level, final, received, ready, diagonal, upper, lower, h, hd, *outputs):
    _, depth, left = place(axes)
    if final:
        green_out, packed_ref, green_ref, upper_ref, lower_ref = outputs
    else:
        message_ref, _, green_ref, upper_ref, lower_ref = outputs
        message_ref[...] = jnp.zeros_like(message_ref)

    @pl.when(depth != level)
    def _():
        green_ref[...] = diagonal[...]
        upper_ref[...] = upper[...]
        lower_ref[...] = lower[...]

    @pl.when(depth == level)
    def _():
        g_in = received[...]
        p = ready[0]
        w = product(g_in, ready[1])
        green_ref[...] = diagonal[...] + product(p, w)

        @pl.when(left)
        def _():
            upper_ref[...] = ready[2] + product(ready[2], w)
            lower_ref[...] = ready[3] + product(p, product(g_in, ready[3]))

        @pl.when(jnp.logical_not(left))
        def _():
            upper_ref[...] = w
            lower_ref[...] = product(p, g_in)

        if not final:
            send(jnp.logical_not(left), green_ref, h[...], hd[...], message_ref)

    if final:
        size = diagonal.shape[0]
        blocks = (green_ref[...], upper_ref[...], lower_ref[...])
        for b, block in enumerate(blocks):
            green_out[b, 0] = real_of(block)
            green_out[b, 1] = imag_of(block)
        d0 = blocks[0] - dagger(blocks[0])
        d1 = blocks[1] - dagger(blocks[2])
        row = lax.broadcasted_iota(jnp.int32, (size, size), 0)
        column = lax.broadcasted_iota(jnp.int32, (size, size), 1)
        packed_ref[0] = jnp.where(row > column, real_of(d0), imag_of(d0))
        packed_ref[1] = real_of(d1)
        packed_ref[2] = imag_of(d1)


def unpack(pack, out):
    size = pack.shape[-1]
    row = lax.broadcasted_iota(jnp.int32, (size, size), 0)
    column = lax.broadcasted_iota(jnp.int32, (size, size), 1)
    mixed = pack[0]
    turned = mixed.T
    out[0, 0] = jnp.where(row > column, mixed, jnp.where(row < column, -turned, 0.0))
    out[0, 1] = jnp.where(row > column, turned, mixed)
    out[1] = pack[1:]
    out[2, 0] = -pack[1].T
    out[2, 1] = pack[2].T


def add_term(out, spectral, blocks, scale):
    for b in range(3):
        w_re, w_im = blocks[b, 0], blocks[b, 1]
        g_re, g_im = scale * spectral[b, 0], scale * spectral[b, 1]
        out[b, 0] -= g_re * w_im + g_im * w_re
        out[b, 1] += g_re * w_re - g_im * w_im


def terms_kernel(axes, same, *refs):
    chips, cores, _ = axes
    packs, rest = refs[:chips], refs[chips:]
    before, pieces = ([], rest[:-3]) if same else (rest[:2], rest[2:-3])
    outs, spectral = rest[-3:-1], rest[-1]
    chip, core = lax.axis_index("chip"), lax.axis_index("core")
    for i, out in enumerate(outs):
        out[...] = jnp.zeros_like(out) if same else before[i][...]
    for r in range(chips):
        @pl.when(chip >= r)
        def _():
            unpack(packs[r], spectral.at[r])
    for offset in range(chips):
        kappa = jnp.bitwise_xor(chip, offset) if len(pieces) > 1 else jnp.int32(offset)
        for c in range(cores):
            p = c if same else 1 - c
            for k in range(cores):
                r = kappa + (p + k) // 2
                out = outs[0] if (p + k) % 2 == c else outs[1]

                @pl.when(jnp.logical_and(core == c, r <= chip))
                def _():
                    index = (chip - r) * cores + p
                    energy = energy_at(index.astype(F32), chips * cores)
                    occupation = 1.0 / (1.0 + jnp.exp(jnp.full((1, 1), energy / THERMAL, F32)))
                    scale = -occupation if c == 0 else 1.0 - occupation
                    add_term(out, spectral.at[r], screened_at(pieces, offset, kappa, k), scale)


def screened_at(pieces, offset, kappa, k):
    if len(pieces) == 1:
        return pieces[0].at[kappa, k]
    return pieces[offset].at[k] if offset < 3 else pieces[3 + k].at[0]


def join_kernel(axes, mine, received, out, arrivals):
    core = lax.axis_index("core")
    copies = [
        pltpu.make_async_copy(mine, out.at[core], arrivals.at[0]),
        pltpu.make_async_copy(received, out.at[1 - core], arrivals.at[1]),
    ]
    for copy in copies:
        copy.start()
    for copy in copies:
        copy.wait()


class Exchange:
    def __init__(self, chips, screened, swap):
        self.paired = chips == 4
        self.own = screened[0, 0]
        core = lax.axis_index("core")
        self.got = lax.ppermute(jnp.where(core == 0, self.own[1], self.own[0]), "core", swap)

    def moved(self, piece, offset):
        return lax.ppermute(piece, "chip", [(i, i ^ offset) for i in range(4)])

    def begin(self, after):
        core = lax.axis_index("core")
        own, got, _ = lax.optimization_barrier((self.own, self.got, after))
        pair = jnp.stack([jnp.where(core == 0, own[0], got), jnp.where(core == 0, got, own[1])])
        if self.paired:
            self.pieces = [pair, self.moved(pair, 1), self.moved(pair, 2)]
        else:
            self.pieces = [lax.all_gather(pair, "chip", axis=0)]

    def go_on(self, halves):
        if self.paired:
            self.pieces += [self.moved(halves[0], 2), self.moved(halves[1], 1)]


def local(axes, onsite, hopping, sigma_old, screened):
    chips, cores, cells_all = axes
    size = sigma_old.shape[-1]
    half = cells_all // 2
    matrix = jax.ShapeDtypeStruct((size, 2 * size), F32)
    def call(body, out_shape, *operands, space=pltpu.VMEM, grant=16, work=WORK, out_space=None, **options):
        spec = pl.BlockSpec(memory_space=pltpu.VMEM)
        spaces = space if isinstance(space, list) else [space] * len(operands)
        return pl.pallas_call(
            functools.partial(body, axes),
            out_shape=out_shape,
            in_specs=[pl.BlockSpec(memory_space=space) for space in spaces],
            out_specs=jax.tree.map(lambda _: spec, out_shape)
            if out_space is None
            else jax.tree.map(lambda space: pl.BlockSpec(memory_space=space), out_space),
            compiler_params=pltpu.CompilerParams(vmem_limit_bytes=grant * 1024 * 1024),
            cost_estimate=pl.CostEstimate(
                flops=int(work * 80 * (2 * size) ** 3), bytes_accessed=2 * 1024 * 1024, transcendentals=0
            ),
            **options,
        )(*operands)

    swap = [(i, i ^ 1) for i in range(cores)]
    exchange = Exchange(chips, screened, swap)
    token = jax.ShapeDtypeStruct((8, size), F32)
    system, green, message, h, hd, mark = call(
        outer_kernel,
        (matrix,) * 5 + (token,),
        *(pltpu.with_memory_space_constraint(a, pltpu.HBM) for a in (onsite, hopping, sigma_old)),
        space=pltpu.HBM,
        scratch_shapes=[pltpu.VMEM(a.shape, F32) for a in (onsite, hopping, sigma_old)]
        + [pltpu.SemaphoreType.DMA((3,))],
    )
    mark = lax.ppermute(mark, "core", swap)
    exchange.begin(mark)
    u_out = outside = jnp.zeros((size, 2 * size), F32)
    for level in range(1, half):
        route = [(level - 1, level), (cells_all - level, cells_all - 1 - level)]
        received = lax.ppermute(message, "space", route)
        system, green, message, u_out, outside = call(
            functools.partial(swapped, inward_kernel, level),
            (matrix,) * 5,
            mark, received, system, green, message, u_out, outside, h, hd,
            work=WORK2,
        )
    received = lax.ppermute(message, "space", [(half - 1, half), (half, half - 1)])
    diagonal, message, u_in, mark = call(
        middle_kernel, (matrix,) * 3 + (token,), received, system, green, h, hd,
        work=WORK3,
    )
    mark = lax.ppermute(mark, "core", swap)
    half_kernels = jax.ShapeDtypeStruct((1, *screened.shape[3:]), F32)
    upper = None
    for level in reversed(range(half - 1)):
        route = [(level + 1, level), (cells_all - 2 - level, cells_all - 1 - level)]
        arrived = lax.ppermute(message, "space", route)
        if upper is None:
            paired = exchange.paired
            spaces = [pltpu.VMEM] * 8 + [pl.ANY] * (2 if paired else 0)
            upper, lower, ready, *halves = call(
                functools.partial(swapped, waiting_kernel, paired),
                (matrix, matrix, jax.ShapeDtypeStruct((4, size, 2 * size), F32)) + (half_kernels,) * (2 if paired else 0),
                mark, received, diagonal, u_in, u_out, outside, h, hd, *(exchange.pieces[1:] if paired else []),
                space=spaces,
                out_space=(pltpu.VMEM,) * 3 + (pl.ANY,) * (2 if paired else 0),
                scratch_shapes=[pltpu.SemaphoreType.DMA((2,))] if paired else [],
                work=WORK4,
            )
            exchange.go_on(halves)
        final = level == 0
        shapes = (matrix,) * 3
        if final:
            shapes = (
                jax.ShapeDtypeStruct((3, 2, size, size), F32),
                jax.ShapeDtypeStruct((3, size, size), F32),
            ) + shapes
        else:
            shapes = (matrix, token) + shapes
        results = call(
            functools.partial(swapped, outward_kernel, level, final),
            shapes,
            arrived, ready, diagonal, upper, lower, h, hd,
            work=WORK6,
        )
        message, _, diagonal, upper, lower = results
    green_out, packed = results[:2]
    own = [packed] + [
        lax.ppermute(packed, "chip", [(i, i + r) for i in range(chips - r)]) for r in range(1, chips)
    ]
    other = [lax.ppermute(pack, "core", swap) for pack in own]
    kind = jax.ShapeDtypeStruct(screened.shape[3:], F32)
    unpacked = [pltpu.VMEM((chips, 3, 2, size, size), F32)]
    mine, theirs = call(
        functools.partial(swapped, terms_kernel, True), (kind,) * 2, *own, *exchange.pieces,
        scratch_shapes=unpacked,
        work=WORK5,
    )
    mine, theirs = call(
        functools.partial(swapped, terms_kernel, False), (kind,) * 2, *other, mine, theirs, *exchange.pieces,
        scratch_shapes=unpacked,
    )
    sigma_out = call(
        join_kernel,
        jax.ShapeDtypeStruct(screened.shape[2:], F32),
        mine, lax.ppermute(theirs, "core", swap),
        space=pl.ANY,
        out_space=pl.ANY,
        scratch_shapes=[pltpu.SemaphoreType.DMA((2,))],
    )
    return green_out[None, None], sigma_out[None, None]


def swapped(body, *arguments):
    fixed = [a for a in arguments if isinstance(a, (int, bool))]
    axes, *refs = arguments[len(fixed) :]
    return body(axes, *fixed, *refs)


def solution(mesh):
    cores = 2
    axes = (mesh.shape["energy"] // cores, cores, mesh.shape["space"])
    split_mesh = jax.sharding.Mesh(mesh.devices.reshape(axes), ("chip", "core", "space"))
    energy = ("chip", "core")
    placed = (
        P("space", None, None, None),
        P("space", None, None, None),
        P(energy, "space", None, None, None),
        P(energy, "space", None, None, None, None, None),
    )
    return jax.shard_map(
        functools.partial(local, axes),
        mesh=split_mesh,
        in_specs=placed,
        out_specs=(
            P(energy, "space", None, None, None, None),
            P(energy, "space", None, None, None, None, None),
        ),
        check_vma=False,
    )
```

```python
import functools
import math

import jax
import jax.numpy as jnp
from jax import lax
from jax.experimental import pallas as pl
from jax.experimental.pallas import tpu as pltpu
from jax.sharding import PartitionSpec as P

BROADEN = 0.45
THERMAL = 0.1
F32 = jnp.float32
BF16 = jnp.bfloat16

LOWEST = 1.0 / 128.0
SQUARINGS = 6
DONE = 1e-4
STEPS_MAX = 60
WORK = 1
WORK2 = 8
WORK3 = 2
WORK4 = 1
WORK5 = 0.01
WORK6 = 1


def schedule():
    rho = (1.0 - LOWEST) / (1.0 + LOWEST)
    scales = []
    for _ in range(SQUARINGS):
        scales.append(2.0 / (2.0 - rho * rho))
        rho = rho * rho / (2.0 - rho * rho)
    return 2.0 / (1.0 + LOWEST), scales


def real_of(x):
    return x[:, : x.shape[1] // 2]


def imag_of(x):
    return x[:, x.shape[1] // 2 :]


def wide(x):
    return jnp.concatenate([x, jnp.concatenate([-imag_of(x), real_of(x)], axis=1)], axis=0)


def dagger(x):
    return jnp.concatenate([real_of(x).T, -imag_of(x).T], axis=1)


def dot(a, b):
    return jnp.dot(a, b, preferred_element_type=F32)


def split(x):
    high = x.astype(BF16)
    return high, (x - high.astype(F32)).astype(BF16)


def product(a, b):
    rows = a.shape[0]
    a_high, a_low = split(a)
    b_high, b_low = split(b)
    both = dot(jnp.concatenate([a_high, a_low], axis=0), wide(b_high))
    return both[:rows] + both[rows:] + dot(a_high, wide(b_low))


def times_complex(x, re, im):
    return jnp.concatenate(
        [re * real_of(x) - im * imag_of(x), re * imag_of(x) + im * real_of(x)], axis=1
    )


def identity_like(x):
    size = x.shape[0]
    row = lax.broadcasted_iota(jnp.int32, x.shape, 0)
    column = lax.broadcasted_iota(jnp.int32, x.shape, 1)
    return jnp.where(row == column, 1.0, 0.0).astype(F32)


def largest(x, axis):
    return jnp.max(x, axis=axis, keepdims=True)


def invert(s, out_ref):
    size = s.shape[0]
    one = identity_like(s)
    first, scales = schedule()
    s_dagger = dagger(s)
    s_dagger_b = s_dagger.astype(BF16)
    normal = dot(s.astype(BF16), wide(s_dagger_b))
    normal_b = normal.astype(BF16)
    both = dot(jnp.concatenate([s_dagger_b, normal_b], axis=0), wide(normal_b))
    square = both[size:]
    sums = jnp.sum(jnp.sqrt(real_of(square) ** 2 + imag_of(square) ** 2), axis=0, keepdims=True)
    a = first * lax.rsqrt(largest(sums, 1))
    c = scales[0]
    x = (2.0 * c * a) * s_dagger - (c * a * a) * both[:size]
    r = one - (2.0 * c * a) * normal + (c * a * a) * square
    for c in scales[1:]:
        r_b = r.astype(BF16)
        both = dot(jnp.concatenate([x.astype(BF16), r_b], axis=0), wide(r_b))
        x = c * (x + both[:size])
        r = (1.0 - c) * one + c * both[size:]
    s_high, s_low = split(s)
    s_both = jnp.concatenate([s_high, s_low], axis=0)
    x_b = x.astype(BF16)
    both = dot(s_both, wide(x_b))
    e_b = (one - both[:size] - both[size:]).astype(BF16)
    x = x_b.astype(F32) + dot(x_b, wide(e_b))

    def step(x):
        x_high, x_low = split(x)
        both = dot(s_both, wide(x_high))
        e = one - both[:size] - both[size:] - dot(s_high, wide(x_low))
        return x + dot(x_high, wide(e.astype(BF16))), jnp.sum(e * e)

    x, left = step(x)
    out_ref[...] = x

    @pl.when(jnp.logical_not(left < DONE))
    def _():
        bound = jnp.sqrt(largest(jnp.sum(jnp.abs(s), axis=1, keepdims=True), 0))
        other = jnp.sqrt(largest(jnp.sum(jnp.abs(real_of(s)) + jnp.abs(imag_of(s)), axis=0, keepdims=True), 1))
        safe = s_dagger / (bound * bound) / (other * other)
        good = left < 0.5
        start = jnp.where(good, x, safe)

        def unfinished(state):
            count, value, _ = state
            return jnp.logical_and(count < STEPS_MAX, jnp.logical_not(value < DONE))

        def body(state):
            count, _, x = state
            new = product(x, one - product(s, x))
            e = one - product(s, x)
            return count + 1, jnp.sum(e * e), x + new

        _, _, result = lax.while_loop(unfinished, body, (0, left, start))
        out_ref[...] = result


def energy_at(index, energies_all):
    return -1.5 + 3.0 * (index + 0.5) / energies_all


def energy_point(axes):
    chips, cores, _ = axes
    index = lax.axis_index("chip") * cores + lax.axis_index("core")
    return energy_at(index.astype(F32), chips * cores)


def place(axes):
    position, cells_all = lax.axis_index("space"), axes[2]
    return position, jnp.minimum(position, cells_all - 1 - position), position < cells_all // 2


def outer_kernel(
    axes, onsite_far, hopping_far, sigma_far, system_ref, green_ref, message_ref, h_ref, hd_ref, token_ref, onsite, hopping, sigma, arrivals
):
    copies = [
        pltpu.make_async_copy(far, near, arrivals.at[i])
        for i, (far, near) in enumerate(((onsite_far, onsite), (hopping_far, hopping), (sigma_far, sigma)))
    ]
    for copy in copies:
        copy.start()
    for copy in copies:
        copy.wait()
    position, depth, left = place(axes)
    energy = energy_point(axes)
    on = jnp.concatenate([onsite[0, 0], onsite[0, 1]], axis=1)
    sg = jnp.concatenate([sigma[0, 0, 0], sigma[0, 0, 1]], axis=1)
    h = jnp.concatenate([hopping[0, 0], hopping[0, 1]], axis=1)
    hd = dagger(h)
    h_ref[...] = h
    token_ref[...] = jnp.zeros_like(token_ref)
    hd_ref[...] = hd
    shape = on.shape
    row = lax.broadcasted_iota(jnp.int32, shape, 0)
    column = lax.broadcasted_iota(jnp.int32, shape, 1)
    point = jnp.where(row == column, energy, 0.0) + jnp.where(row + shape[0] == column, BROADEN, 0.0)
    system_ref[...] = point - 0.5 * (on + dagger(on)) - sg

    @pl.when(position == 0)
    def _():
        magnitude = energy * energy + BROADEN * BROADEN
        system_ref[...] = system_ref[...] - times_complex(product(hd, h), energy / magnitude, -BROADEN / magnitude)

    @pl.when(depth == 0)
    def _():
        invert(system_ref[...], green_ref)
        send(left, green_ref, h, hd, message_ref)

    @pl.when(depth != 0)
    def _():
        green_ref[...] = jnp.zeros(shape, F32)
        message_ref[...] = jnp.zeros(shape, F32)


def send(plain, green_ref, h, hd, message_ref):
    @pl.when(plain)
    def _():
        message_ref[...] = green_ref[...]

    @pl.when(jnp.logical_not(plain))
    def _():
        message_ref[...] = product(h, product(green_ref[...], hd))


def inward_kernel(axes, level, _, received, system, green, message, u, outside, h, hd, system_ref, green_ref, message_ref, u_ref, outside_ref, token_ref):
    token_ref[...] = jnp.zeros_like(token_ref)
    _, depth, left = place(axes)

    @pl.when(depth == level)
    def _():
        got = received[...]

        @pl.when(left)
        def _():
            gh = product(got, h[...])
            u_ref[...] = gh
            outside_ref[...] = got
            system_ref[...] = system[...] - product(hd[...], gh)

        @pl.when(jnp.logical_not(left))
        def _():
            system_ref[...] = system[...] - got
            u_ref[...] = u[...]
            outside_ref[...] = outside[...]

        invert(system_ref[...], green_ref)
        send(left, green_ref, h[...], hd[...], message_ref)

    @pl.when(depth != level)
    def _():
        system_ref[...] = system[...]
        green_ref[...] = green[...]
        message_ref[...] = message[...]
        u_ref[...] = u[...]
        outside_ref[...] = outside[...]


def middle_kernel(axes, _, received, system, green, h, hd, diagonal_ref, message_ref, u_ref, token_ref):
    token_ref[...] = jnp.zeros_like(token_ref)
    _, depth, left = place(axes)

    @pl.when(depth == axes[2] // 2 - 1)
    def _():
        got = received[...]

        @pl.when(left)
        def _():
            u_ref[...] = system[...] - got

        @pl.when(jnp.logical_not(left))
        def _():
            message_ref[...] = product(got, h[...])
            u_ref[...] = system[...] - product(hd[...], message_ref[...])

        s = u_ref[...]
        u_ref[...] = message_ref[...]
        invert(s, diagonal_ref)
        send(jnp.logical_not(left), diagonal_ref, h[...], hd[...], message_ref)

    @pl.when(depth != axes[2] // 2 - 1)
    def _():
        diagonal_ref[...] = green[...]
        u_ref[...] = jnp.zeros_like(u_ref)
        message_ref[...] = jnp.zeros_like(message_ref)


def waiting_kernel(axes, _, received, diagonal, u_in, u_out, outside, h, hd, upper_ref, lower_ref, ready_ref, token_ref):
    token_ref[...] = jnp.zeros_like(token_ref)
    position, depth, left = place(axes)
    energy = energy_point(axes)
    magnitude = energy * energy + BROADEN * BROADEN
    contact_re, contact_im = energy / magnitude, -BROADEN / magnitude

    @pl.when(depth == axes[2] // 2 - 1)
    def _():
        u = jnp.where(left, u_out[...], u_in[...])
        v = product(hd[...], jnp.where(left, outside[...], received[...]))
        upper_ref[...] = product(u, diagonal[...])
        lower_ref[...] = product(diagonal[...], v)
        ready_ref[...] = jnp.zeros_like(ready_ref)

    @pl.when(depth != axes[2] // 2 - 1)
    def _():
        g = diagonal[...]

        @pl.when(left)
        def _():
            at_contact = position == 0
            u = jnp.where(at_contact, times_complex(h[...], contact_re, contact_im), u_out[...])
            v = jnp.where(at_contact, times_complex(hd[...], contact_re, contact_im), product(hd[...], outside[...]))
            ready_ref[0] = g
            ready_ref[1] = g
            ready_ref[2] = product(u, g)
            ready_ref[3] = product(g, v)

        @pl.when(jnp.logical_not(left))
        def _():
            ready_ref[0] = product(g, hd[...])
            ready_ref[1] = product(h[...], g)
            ready_ref[2] = jnp.zeros_like(g)
            ready_ref[3] = jnp.zeros_like(g)

        upper_ref[...] = jnp.zeros_like(upper_ref)
        lower_ref[...] = jnp.zeros_like(lower_ref)


def outward_kernel(axes, level, final, waited, *refs):
    outward(axes, level, final, *refs[waited:])


def outward(axes, level, final, received, ready, diagonal, upper, lower, h, hd, *outputs):
    _, depth, left = place(axes)
    if final:
        green_out, packed_ref, green_ref, upper_ref, lower_ref = outputs
    else:
        message_ref, _, green_ref, upper_ref, lower_ref = outputs
        message_ref[...] = jnp.zeros_like(message_ref)

    @pl.when(depth != level)
    def _():
        green_ref[...] = diagonal[...]
        upper_ref[...] = upper[...]
        lower_ref[...] = lower[...]

    @pl.when(depth == level)
    def _():
        g_in = received[...]
        p = ready[0]
        w = product(g_in, ready[1])
        green_ref[...] = diagonal[...] + product(p, w)

        @pl.when(left)
        def _():
            upper_ref[...] = ready[2] + product(ready[2], w)
            lower_ref[...] = ready[3] + product(p, product(g_in, ready[3]))

        @pl.when(jnp.logical_not(left))
        def _():
            upper_ref[...] = w
            lower_ref[...] = product(p, g_in)

        if not final:
            send(jnp.logical_not(left), green_ref, h[...], hd[...], message_ref)

    if final:
        size = diagonal.shape[0]
        blocks = (green_ref[...], upper_ref[...], lower_ref[...])
        for b, block in enumerate(blocks):
            green_out[b, 0] = real_of(block)
            green_out[b, 1] = imag_of(block)
        d0 = blocks[0] - dagger(blocks[0])
        d1 = blocks[1] - dagger(blocks[2])
        row = lax.broadcasted_iota(jnp.int32, (size, size), 0)
        column = lax.broadcasted_iota(jnp.int32, (size, size), 1)
        packed_ref[0] = jnp.where(row > column, real_of(d0), imag_of(d0))
        packed_ref[1] = real_of(d1)
        packed_ref[2] = imag_of(d1)


def unpack(pack, out):
    size = pack.shape[-1]
    row = lax.broadcasted_iota(jnp.int32, (size, size), 0)
    column = lax.broadcasted_iota(jnp.int32, (size, size), 1)
    mixed = pack[0]
    turned = mixed.T
    out[0, 0] = jnp.where(row > column, mixed, jnp.where(row < column, -turned, 0.0))
    out[0, 1] = jnp.where(row > column, turned, mixed)
    out[1] = pack[1:]
    out[2, 0] = -pack[1].T
    out[2, 1] = pack[2].T


def add_term(out, spectral, blocks, scale):
    for b in range(3):
        w_re, w_im = blocks[b, 0], blocks[b, 1]
        g_re, g_im = scale * spectral[b, 0], scale * spectral[b, 1]
        out[b, 0] -= g_re * w_im + g_im * w_re
        out[b, 1] += g_re * w_re - g_im * w_im


def terms_kernel(axes, same, *refs):
    chips, cores, _ = axes
    packs, rest = refs[:chips], refs[chips:]
    before, pieces = ([], rest[:-3]) if same else (rest[:2], rest[2:-3])
    outs, spectral = rest[-3:-1], rest[-1]
    chip, core = lax.axis_index("chip"), lax.axis_index("core")
    for i, out in enumerate(outs):
        out[...] = jnp.zeros_like(out) if same else before[i][...]
    for r in range(chips):
        @pl.when(chip >= r)
        def _():
            unpack(packs[r], spectral.at[r])
    for offset in range(chips):
        kappa = jnp.bitwise_xor(chip, offset) if len(pieces) > 1 else jnp.int32(offset)
        for c in range(cores):
            p = c if same else 1 - c
            for k in range(cores):
                r = kappa + (p + k) // 2
                out = outs[0] if (p + k) % 2 == c else outs[1]

                @pl.when(jnp.logical_and(core == c, r <= chip))
                def _():
                    index = (chip - r) * cores + p
                    energy = energy_at(index.astype(F32), chips * cores)
                    occupation = 1.0 / (1.0 + jnp.exp(jnp.full((1, 1), energy / THERMAL, F32)))
                    scale = -occupation if c == 0 else 1.0 - occupation
                    add_term(out, spectral.at[r], screened_at(pieces, offset, kappa, k), scale)


def screened_at(pieces, offset, kappa, k):
    if len(pieces) == 1:
        return pieces[0].at[kappa, k]
    return pieces[2 * offset + k]


def join_kernel(axes, mine, received, out, arrivals):
    core = lax.axis_index("core")
    copies = [
        pltpu.make_async_copy(mine, out.at[core], arrivals.at[0]),
        pltpu.make_async_copy(received, out.at[1 - core], arrivals.at[1]),
    ]
    for copy in copies:
        copy.start()
    for copy in copies:
        copy.wait()


class Exchange:
    def __init__(self, chips, screened, swap):
        self.paired = chips == 4
        self.own = screened[0, 0]
        self.got = lax.ppermute(self.own, "core", swap)
        self.later = []

    def moved(self, piece, offset):
        return lax.ppermute(piece, "chip", [(i, i ^ offset) for i in range(4)])

    def begin(self, after):
        core = lax.axis_index("core")
        own, got, _ = lax.optimization_barrier((self.own, self.got, after))
        self.pair = [jnp.where(core == 0, own[0], got[1]), jnp.where(core == 0, got[0], own[1])]
        if self.paired:
            self.along = [self.moved(self.pair[0], 1), self.moved(self.pair[1], 2)]
        else:
            self.pieces = [lax.all_gather(jnp.stack(self.pair), "chip", axis=0)]

    def go_on(self, after):
        if self.paired:
            one, two, _ = lax.optimization_barrier((*self.pair, after))
            self.later = [self.moved(two, 1), self.moved(one, 2)]

    def finish(self, after):
        if self.paired:
            first, second, _ = lax.optimization_barrier((*self.along, after))
            ahead = [self.moved(first, 2), self.moved(second, 1)]
            self.pieces = [*self.pair, self.along[0], self.later[0], self.later[1], self.along[1], *ahead]


def local(axes, onsite, hopping, sigma_old, screened):
    chips, cores, cells_all = axes
    size = sigma_old.shape[-1]
    half = cells_all // 2
    matrix = jax.ShapeDtypeStruct((size, 2 * size), F32)
    def call(body, out_shape, *operands, space=pltpu.VMEM, grant=16, work=WORK, out_space=None, **options):
        spec = pl.BlockSpec(memory_space=pltpu.VMEM)
        spaces = space if isinstance(space, list) else [space] * len(operands)
        return pl.pallas_call(
            functools.partial(body, axes),
            out_shape=out_shape,
            in_specs=[pl.BlockSpec(memory_space=space) for space in spaces],
            out_specs=jax.tree.map(lambda _: spec, out_shape)
            if out_space is None
            else jax.tree.map(lambda space: pl.BlockSpec(memory_space=space), out_space),
            compiler_params=pltpu.CompilerParams(vmem_limit_bytes=grant * 1024 * 1024),
            cost_estimate=pl.CostEstimate(
                flops=int(work * 80 * (2 * size) ** 3), bytes_accessed=2 * 1024 * 1024, transcendentals=0
            ),
            **options,
        )(*operands)

    swap = [(i, i ^ 1) for i in range(cores)]
    exchange = Exchange(chips, screened, swap)
    token = jax.ShapeDtypeStruct((8, size), F32)
    system, green, message, h, hd, mark = call(
        outer_kernel,
        (matrix,) * 5 + (token,),
        *(pltpu.with_memory_space_constraint(a, pltpu.HBM) for a in (onsite, hopping, sigma_old)),
        space=pltpu.HBM,
        scratch_shapes=[pltpu.VMEM(a.shape, F32) for a in (onsite, hopping, sigma_old)]
        + [pltpu.SemaphoreType.DMA((3,))],
    )
    mark = lax.ppermute(mark, "core", swap)
    exchange.begin(mark)
    u_out = outside = jnp.zeros((size, 2 * size), F32)
    for level in range(1, half):
        route = [(level - 1, level), (cells_all - level, cells_all - 1 - level)]
        received = lax.ppermute(message, "space", route)
        system, green, message, u_out, outside, next_mark = call(
            functools.partial(swapped, inward_kernel, level),
            (matrix,) * 5 + (token,),
            mark, received, system, green, message, u_out, outside, h, hd,
            work=WORK2,
        )
        if level == half - 1:
            mark = lax.ppermute(next_mark, "core", swap)
            exchange.go_on(mark)
    received = lax.ppermute(message, "space", [(half - 1, half), (half, half - 1)])
    diagonal, message, u_in, mark = call(
        middle_kernel, (matrix,) * 3 + (token,), mark, received, system, green, h, hd,
        work=WORK3,
    )
    mark = lax.ppermute(mark, "core", swap)
    upper = None
    for level in reversed(range(half - 1)):
        route = [(level + 1, level), (cells_all - 2 - level, cells_all - 1 - level)]
        arrived = lax.ppermute(message, "space", route)
        if upper is None:
            upper, lower, ready, last = call(
                waiting_kernel,
                (matrix, matrix, jax.ShapeDtypeStruct((4, size, 2 * size), F32), token),
                mark, received, diagonal, u_in, u_out, outside, h, hd,
                work=WORK4,
            )
            exchange.finish(last)
        final = level == 0
        shapes = (matrix,) * 3
        if final:
            shapes = (
                jax.ShapeDtypeStruct((3, 2, size, size), F32),
                jax.ShapeDtypeStruct((3, size, size), F32),
            ) + shapes
        else:
            shapes = (matrix, token) + shapes
        results = call(
            functools.partial(swapped, outward_kernel, level, final, len(exchange.later)),
            shapes,
            *exchange.later, arrived, ready, diagonal, upper, lower, h, hd,
            space=[pl.ANY] * len(exchange.later) + [pltpu.VMEM] * 7,
            work=WORK6,
        )
        message, _, diagonal, upper, lower = results
    green_out, packed = results[:2]
    own = [packed] + [
        lax.ppermute(packed, "chip", [(i, i + r) for i in range(chips - r)]) for r in range(1, chips)
    ]
    other = [lax.ppermute(pack, "core", swap) for pack in own]
    kind = jax.ShapeDtypeStruct(screened.shape[3:], F32)
    unpacked = [pltpu.VMEM((chips, 3, 2, size, size), F32)]
    mine, theirs = call(
        functools.partial(swapped, terms_kernel, True), (kind,) * 2, *own, *exchange.pieces,
        scratch_shapes=unpacked,
        work=WORK5,
    )
    mine, theirs = call(
        functools.partial(swapped, terms_kernel, False), (kind,) * 2, *other, mine, theirs, *exchange.pieces,
        scratch_shapes=unpacked,
    )
    sigma_out = call(
        join_kernel,
        jax.ShapeDtypeStruct(screened.shape[2:], F32),
        mine, lax.ppermute(theirs, "core", swap),
        space=pl.ANY,
        out_space=pl.ANY,
        scratch_shapes=[pltpu.SemaphoreType.DMA((2,))],
    )
    return green_out[None, None], sigma_out[None, None]


def swapped(body, *arguments):
    fixed = [a for a in arguments if isinstance(a, (int, bool))]
    axes, *refs = arguments[len(fixed) :]
    return body(axes, *fixed, *refs)


def solution(mesh):
    cores = 2
    axes = (mesh.shape["energy"] // cores, cores, mesh.shape["space"])
    split_mesh = jax.sharding.Mesh(mesh.devices.reshape(axes), ("chip", "core", "space"))
    energy = ("chip", "core")
    placed = (
        P("space", None, None, None),
        P("space", None, None, None),
        P(energy, "space", None, None, None),
        P(energy, "space", None, None, None, None, None),
    )
    return jax.shard_map(
        functools.partial(local, axes),
        mesh=split_mesh,
        in_specs=placed,
        out_specs=(
            P(energy, "space", None, None, None, None),
            P(energy, "space", None, None, None, None, None),
        ),
        check_vma=False,
    )
```

```python
import functools
import math

import jax
import jax.numpy as jnp
from jax import lax
from jax.experimental import pallas as pl
from jax.experimental.pallas import tpu as pltpu
from jax.sharding import PartitionSpec as P

BROADEN = 0.45
THERMAL = 0.1
F32 = jnp.float32
BF16 = jnp.bfloat16

LOWEST = 1.0 / 128.0
SQUARINGS = 6
DONE = 1e-4
STEPS_MAX = 60
WORK = 1
WORK2 = 2
WORK3 = 0.1
WORK4 = 0.1
WORK5 = 0.01
WORK6 = 0.1


def schedule():
    rho = (1.0 - LOWEST) / (1.0 + LOWEST)
    scales = []
    for _ in range(SQUARINGS):
        scales.append(2.0 / (2.0 - rho * rho))
        rho = rho * rho / (2.0 - rho * rho)
    return 2.0 / (1.0 + LOWEST), scales


def real_of(x):
    return x[:, : x.shape[1] // 2]


def imag_of(x):
    return x[:, x.shape[1] // 2 :]


def wide(x):
    return jnp.concatenate([x, jnp.concatenate([-imag_of(x), real_of(x)], axis=1)], axis=0)


def dagger(x):
    return jnp.concatenate([real_of(x).T, -imag_of(x).T], axis=1)


def dot(a, b):
    return jnp.dot(a, b, preferred_element_type=F32)


def split(x):
    high = x.astype(BF16)
    return high, (x - high.astype(F32)).astype(BF16)


def product(a, b):
    rows = a.shape[0]
    a_high, a_low = split(a)
    b_high, b_low = split(b)
    both = dot(jnp.concatenate([a_high, a_low], axis=0), wide(b_high))
    return both[:rows] + both[rows:] + dot(a_high, wide(b_low))


def times_complex(x, re, im):
    return jnp.concatenate(
        [re * real_of(x) - im * imag_of(x), re * imag_of(x) + im * real_of(x)], axis=1
    )


def identity_like(x):
    size = x.shape[0]
    row = lax.broadcasted_iota(jnp.int32, x.shape, 0)
    column = lax.broadcasted_iota(jnp.int32, x.shape, 1)
    return jnp.where(row == column, 1.0, 0.0).astype(F32)


def largest(x, axis):
    return jnp.max(x, axis=axis, keepdims=True)


def invert(s, out_ref):
    size = s.shape[0]
    one = identity_like(s)
    first, scales = schedule()
    s_dagger = dagger(s)
    s_dagger_b = s_dagger.astype(BF16)
    normal = dot(s.astype(BF16), wide(s_dagger_b))
    normal_b = normal.astype(BF16)
    both = dot(jnp.concatenate([s_dagger_b, normal_b], axis=0), wide(normal_b))
    square = both[size:]
    sums = jnp.sum(jnp.sqrt(real_of(square) ** 2 + imag_of(square) ** 2), axis=0, keepdims=True)
    a = first * lax.rsqrt(largest(sums, 1))
    c = scales[0]
    x = (2.0 * c * a) * s_dagger - (c * a * a) * both[:size]
    r = one - (2.0 * c * a) * normal + (c * a * a) * square
    for c in scales[1:]:
        r_b = r.astype(BF16)
        both = dot(jnp.concatenate([x.astype(BF16), r_b], axis=0), wide(r_b))
        x = c * (x + both[:size])
        r = (1.0 - c) * one + c * both[size:]
    s_high, s_low = split(s)
    s_both = jnp.concatenate([s_high, s_low], axis=0)
    x_b = x.astype(BF16)
    both = dot(s_both, wide(x_b))
    e_b = (one - both[:size] - both[size:]).astype(BF16)
    x = x_b.astype(F32) + dot(x_b, wide(e_b))

    def step(x):
        x_high, x_low = split(x)
        both = dot(s_both, wide(x_high))
        e = one - both[:size] - both[size:] - dot(s_high, wide(x_low))
        return x + dot(x_high, wide(e.astype(BF16))), jnp.sum(e * e)

    x, left = step(x)
    out_ref[...] = x

    @pl.when(jnp.logical_not(left < DONE))
    def _():
        bound = jnp.sqrt(largest(jnp.sum(jnp.abs(s), axis=1, keepdims=True), 0))
        other = jnp.sqrt(largest(jnp.sum(jnp.abs(real_of(s)) + jnp.abs(imag_of(s)), axis=0, keepdims=True), 1))
        safe = s_dagger / (bound * bound) / (other * other)
        good = left < 0.5
        start = jnp.where(good, x, safe)

        def unfinished(state):
            count, value, _ = state
            return jnp.logical_and(count < STEPS_MAX, jnp.logical_not(value < DONE))

        def body(state):
            count, _, x = state
            new = product(x, one - product(s, x))
            e = one - product(s, x)
            return count + 1, jnp.sum(e * e), x + new

        _, _, result = lax.while_loop(unfinished, body, (0, left, start))
        out_ref[...] = result


def energy_at(index, energies_all):
    return -1.5 + 3.0 * (index + 0.5) / energies_all


def energy_point(axes):
    chips, cores, _ = axes
    index = lax.axis_index("chip") * cores + lax.axis_index("core")
    return energy_at(index.astype(F32), chips * cores)


def place(axes):
    position, cells_all = lax.axis_index("space"), axes[2]
    return position, jnp.minimum(position, cells_all - 1 - position), position < cells_all // 2


def outer_kernel(
    axes, onsite_far, hopping_far, sigma_far, system_ref, green_ref, message_ref, h_ref, hd_ref, token_ref, onsite, hopping, sigma, arrivals
):
    copies = [
        pltpu.make_async_copy(far, near, arrivals.at[i])
        for i, (far, near) in enumerate(((onsite_far, onsite), (hopping_far, hopping), (sigma_far, sigma)))
    ]
    for copy in copies:
        copy.start()
    for copy in copies:
        copy.wait()
    position, depth, left = place(axes)
    energy = energy_point(axes)
    on = jnp.concatenate([onsite[0, 0], onsite[0, 1]], axis=1)
    sg = jnp.concatenate([sigma[0, 0, 0], sigma[0, 0, 1]], axis=1)
    h = jnp.concatenate([hopping[0, 0], hopping[0, 1]], axis=1)
    hd = dagger(h)
    h_ref[...] = h
    token_ref[...] = jnp.zeros_like(token_ref)
    hd_ref[...] = hd
    shape = on.shape
    row = lax.broadcasted_iota(jnp.int32, shape, 0)
    column = lax.broadcasted_iota(jnp.int32, shape, 1)
    point = jnp.where(row == column, energy, 0.0) + jnp.where(row + shape[0] == column, BROADEN, 0.0)
    system_ref[...] = point - 0.5 * (on + dagger(on)) - sg

    @pl.when(position == 0)
    def _():
        magnitude = energy * energy + BROADEN * BROADEN
        system_ref[...] = system_ref[...] - times_complex(product(hd, h), energy / magnitude, -BROADEN / magnitude)

    @pl.when(depth == 0)
    def _():
        invert(system_ref[...], green_ref)
        send(left, green_ref, h, hd, message_ref)

    @pl.when(depth != 0)
    def _():
        green_ref[...] = jnp.zeros(shape, F32)
        message_ref[...] = jnp.zeros(shape, F32)


def send(plain, green_ref, h, hd, message_ref):
    @pl.when(plain)
    def _():
        message_ref[...] = green_ref[...]

    @pl.when(jnp.logical_not(plain))
    def _():
        message_ref[...] = product(h, product(green_ref[...], hd))


def inward_kernel(axes, level, _, received, system, green, message, u, outside, h, hd, system_ref, green_ref, message_ref, u_ref, outside_ref, token_ref):
    token_ref[...] = jnp.zeros_like(token_ref)
    _, depth, left = place(axes)

    @pl.when(depth == level)
    def _():
        got = received[...]

        @pl.when(left)
        def _():
            gh = product(got, h[...])
            u_ref[...] = gh
            outside_ref[...] = got
            system_ref[...] = system[...] - product(hd[...], gh)

        @pl.when(jnp.logical_not(left))
        def _():
            system_ref[...] = system[...] - got
            u_ref[...] = u[...]
            outside_ref[...] = outside[...]

        invert(system_ref[...], green_ref)
        send(left, green_ref, h[...], hd[...], message_ref)

    @pl.when(depth != level)
    def _():
        system_ref[...] = system[...]
        green_ref[...] = green[...]
        message_ref[...] = message[...]
        u_ref[...] = u[...]
        outside_ref[...] = outside[...]


def middle_kernel(axes, received, system, green, h, hd, diagonal_ref, message_ref, u_ref):
    _, depth, left = place(axes)

    @pl.when(depth == axes[2] // 2 - 1)
    def _():
        got = received[...]

        @pl.when(left)
        def _():
            u_ref[...] = system[...] - got

        @pl.when(jnp.logical_not(left))
        def _():
            message_ref[...] = product(got, h[...])
            u_ref[...] = system[...] - product(hd[...], message_ref[...])

        s = u_ref[...]
        u_ref[...] = message_ref[...]
        invert(s, diagonal_ref)
        send(jnp.logical_not(left), diagonal_ref, h[...], hd[...], message_ref)

    @pl.when(depth != axes[2] // 2 - 1)
    def _():
        diagonal_ref[...] = green[...]
        u_ref[...] = jnp.zeros_like(u_ref)
        message_ref[...] = jnp.zeros_like(message_ref)


def waiting_kernel(axes, received, diagonal, u_in, u_out, outside, h, hd, upper_ref, lower_ref, ready_ref):
    position, depth, left = place(axes)
    energy = energy_point(axes)
    magnitude = energy * energy + BROADEN * BROADEN
    contact_re, contact_im = energy / magnitude, -BROADEN / magnitude

    @pl.when(depth == axes[2] // 2 - 1)
    def _():
        u = jnp.where(left, u_out[...], u_in[...])
        v = product(hd[...], jnp.where(left, outside[...], received[...]))
        upper_ref[...] = product(u, diagonal[...])
        lower_ref[...] = product(diagonal[...], v)
        ready_ref[...] = jnp.zeros_like(ready_ref)

    @pl.when(depth != axes[2] // 2 - 1)
    def _():
        g = diagonal[...]

        @pl.when(left)
        def _():
            at_contact = position == 0
            u = jnp.where(at_contact, times_complex(h[...], contact_re, contact_im), u_out[...])
            v = jnp.where(at_contact, times_complex(hd[...], contact_re, contact_im), product(hd[...], outside[...]))
            ready_ref[0] = g
            ready_ref[1] = g
            ready_ref[2] = product(u, g)
            ready_ref[3] = product(g, v)

        @pl.when(jnp.logical_not(left))
        def _():
            ready_ref[0] = product(g, hd[...])
            ready_ref[1] = product(h[...], g)
            ready_ref[2] = jnp.zeros_like(g)
            ready_ref[3] = jnp.zeros_like(g)

        upper_ref[...] = jnp.zeros_like(upper_ref)
        lower_ref[...] = jnp.zeros_like(lower_ref)


def outward_kernel(axes, level, final, waited, *refs):
    outward(axes, level, final, *refs[waited:])


def outward(axes, level, final, received, ready, diagonal, upper, lower, h, hd, *outputs):
    _, depth, left = place(axes)
    if final:
        green_out, packed_ref, green_ref, upper_ref, lower_ref = outputs
    else:
        message_ref, _, green_ref, upper_ref, lower_ref = outputs
        message_ref[...] = jnp.zeros_like(message_ref)

    @pl.when(depth != level)
    def _():
        green_ref[...] = diagonal[...]
        upper_ref[...] = upper[...]
        lower_ref[...] = lower[...]

    @pl.when(depth == level)
    def _():
        g_in = received[...]
        p = ready[0]
        w = product(g_in, ready[1])
        green_ref[...] = diagonal[...] + product(p, w)

        @pl.when(left)
        def _():
            upper_ref[...] = ready[2] + product(ready[2], w)
            lower_ref[...] = ready[3] + product(p, product(g_in, ready[3]))

        @pl.when(jnp.logical_not(left))
        def _():
            upper_ref[...] = w
            lower_ref[...] = product(p, g_in)

        if not final:
            send(jnp.logical_not(left), green_ref, h[...], hd[...], message_ref)

    if final:
        size = diagonal.shape[0]
        blocks = (green_ref[...], upper_ref[...], lower_ref[...])
        for b, block in enumerate(blocks):
            green_out[b, 0] = real_of(block)
            green_out[b, 1] = imag_of(block)
        d0 = blocks[0] - dagger(blocks[0])
        d1 = blocks[1] - dagger(blocks[2])
        row = lax.broadcasted_iota(jnp.int32, (size, size), 0)
        column = lax.broadcasted_iota(jnp.int32, (size, size), 1)
        packed_ref[0] = jnp.where(row > column, real_of(d0), imag_of(d0))
        packed_ref[1] = real_of(d1)
        packed_ref[2] = imag_of(d1)


def unpack(pack, out):
    size = pack.shape[-1]
    row = lax.broadcasted_iota(jnp.int32, (size, size), 0)
    column = lax.broadcasted_iota(jnp.int32, (size, size), 1)
    mixed = pack[0]
    turned = mixed.T
    out[0, 0] = jnp.where(row > column, mixed, jnp.where(row < column, -turned, 0.0))
    out[0, 1] = jnp.where(row > column, turned, mixed)
    out[1] = pack[1:]
    out[2, 0] = -pack[1].T
    out[2, 1] = pack[2].T


def add_term(out, spectral, blocks, scale):
    for b in range(3):
        w_re, w_im = blocks[b, 0], blocks[b, 1]
        g_re, g_im = scale * spectral[b, 0], scale * spectral[b, 1]
        out[b, 0] -= g_re * w_im + g_im * w_re
        out[b, 1] += g_re * w_re - g_im * w_im


def add_terms(axes, same, only, pieces, outs, spectral):
    chips, cores, _ = axes
    chip, core = lax.axis_index("chip"), lax.axis_index("core")
    for offset in range(chips):
        kappa = jnp.bitwise_xor(chip, offset) if len(pieces) > 1 else jnp.int32(offset)
        for c in range(cores):
            p = c if same else 1 - c
            for k in range(cores):
                r = kappa + (p + k) // 2
                to = 0 if (p + k) % 2 == c else 1
                if to not in only:
                    continue

                @pl.when(jnp.logical_and(core == c, r <= chip))
                def _():
                    index = (chip - r) * cores + p
                    energy = energy_at(index.astype(F32), chips * cores)
                    occupation = 1.0 / (1.0 + jnp.exp(jnp.full((1, 1), energy / THERMAL, F32)))
                    scale = -occupation if c == 0 else 1.0 - occupation
                    add_term(outs[to], spectral.at[r], screened_at(pieces, offset, kappa, k), scale)


def unpack_all(chips, packs, spectral):
    chip = lax.axis_index("chip")
    for r in range(chips):
        @pl.when(chip >= r)
        def _():
            unpack(packs[r], spectral.at[r])


def same_core_kernel(axes, *refs):
    chips = axes[0]
    packs, pieces, outs, spectral = refs[:chips], refs[chips:-3], refs[-3:-1], refs[-1]
    for out in outs:
        out[...] = jnp.zeros_like(out)
    unpack_all(chips, packs, spectral)
    add_terms(axes, True, (0, 1), pieces, outs, spectral)


def theirs_kernel(axes, *refs):
    chips = axes[0]
    packs, before, pieces, out, spectral = refs[:chips], refs[chips], refs[chips + 1 : -2], refs[-2], refs[-1]
    out[...] = before[...]
    unpack_all(chips, packs, spectral)
    add_terms(axes, False, (1,), pieces, (None, out), spectral)


def mine_kernel(axes, spectral, before, *refs):
    pieces, out, held, arrival = refs[:-3], refs[-3], refs[-2], refs[-1]
    held[...] = before[...]
    add_terms(axes, False, (0,), pieces, (held, None), spectral)
    copy = pltpu.make_async_copy(held, out.at[lax.axis_index("core")], arrival)
    copy.start()
    copy.wait()


def screened_at(pieces, offset, kappa, k):
    if len(pieces) == 1:
        return pieces[0].at[kappa, k]
    return pieces[2 * offset + k]


def join_kernel(axes, received, _, out, arrival):
    copy = pltpu.make_async_copy(received, out.at[1 - lax.axis_index("core")], arrival)
    copy.start()
    copy.wait()


class Exchange:
    def __init__(self, chips, screened, swap):
        self.paired = chips == 4
        self.own = screened[0, 0]
        self.got = lax.ppermute(self.own, "core", swap)
        self.later = []

    def moved(self, piece, offset):
        return lax.ppermute(piece, "chip", [(i, i ^ offset) for i in range(4)])

    def begin(self, after):
        core = lax.axis_index("core")
        own, got, _ = lax.optimization_barrier((self.own, self.got, after))
        one, two = jnp.where(core == 0, own[0], got[1]), jnp.where(core == 0, got[0], own[1])
        if self.paired:
            self.along = [self.moved(one, 1), self.moved(two, 2)]
            self.later = [self.moved(two, 1), self.moved(one, 2)]
            self.pieces = [one, two, self.along[0], self.later[0], self.later[1], self.along[1]]
        else:
            self.pieces = [lax.all_gather(jnp.stack([one, two]), "chip", axis=0)]

    def go_on(self, after):
        if self.paired:
            first, second, _ = lax.optimization_barrier((*self.along, after))
            self.pieces += [self.moved(first, 2), self.moved(second, 1)]


def local(axes, onsite, hopping, sigma_old, screened):
    chips, cores, cells_all = axes
    size = sigma_old.shape[-1]
    half = cells_all // 2
    matrix = jax.ShapeDtypeStruct((size, 2 * size), F32)
    def call(body, out_shape, *operands, space=pltpu.VMEM, grant=16, work=WORK, out_space=None, **options):
        spec = pl.BlockSpec(memory_space=pltpu.VMEM)
        spaces = space if isinstance(space, list) else [space] * len(operands)
        return pl.pallas_call(
            functools.partial(body, axes),
            out_shape=out_shape,
            in_specs=[pl.BlockSpec(memory_space=space) for space in spaces],
            out_specs=jax.tree.map(lambda _: spec, out_shape)
            if out_space is None
            else jax.tree.map(lambda space: pl.BlockSpec(memory_space=space), out_space),
            compiler_params=pltpu.CompilerParams(vmem_limit_bytes=grant * 1024 * 1024),
            cost_estimate=pl.CostEstimate(
                flops=int(work * 80 * (2 * size) ** 3), bytes_accessed=2 * 1024 * 1024, transcendentals=0
            ),
            **options,
        )(*operands)

    swap = [(i, i ^ 1) for i in range(cores)]
    exchange = Exchange(chips, screened, swap)
    token = jax.ShapeDtypeStruct((8, size), F32)
    system, green, message, h, hd, mark = call(
        outer_kernel,
        (matrix,) * 5 + (token,),
        *(pltpu.with_memory_space_constraint(a, pltpu.HBM) for a in (onsite, hopping, sigma_old)),
        space=pltpu.HBM,
        scratch_shapes=[pltpu.VMEM(a.shape, F32) for a in (onsite, hopping, sigma_old)]
        + [pltpu.SemaphoreType.DMA((3,))],
    )
    mark = lax.ppermute(mark, "core", swap)
    exchange.begin(mark)
    u_out = outside = jnp.zeros((size, 2 * size), F32)
    for level in range(1, half):
        route = [(level - 1, level), (cells_all - level, cells_all - 1 - level)]
        received = lax.ppermute(message, "space", route)
        system, green, message, u_out, outside, next_mark = call(
            functools.partial(swapped, inward_kernel, level),
            (matrix,) * 5 + (token,),
            mark, received, system, green, message, u_out, outside, h, hd,
            work=WORK2,
        )
        if level == half - 1:
            exchange.go_on(next_mark)
    received = lax.ppermute(message, "space", [(half - 1, half), (half, half - 1)])
    diagonal, message, u_in = call(
        middle_kernel, (matrix,) * 3, received, system, green, h, hd,
        work=WORK3,
    )
    upper = None
    for level in reversed(range(half - 1)):
        route = [(level + 1, level), (cells_all - 2 - level, cells_all - 1 - level)]
        arrived = lax.ppermute(message, "space", route)
        if upper is None:
            upper, lower, ready = call(
                waiting_kernel,
                (matrix, matrix, jax.ShapeDtypeStruct((4, size, 2 * size), F32)),
                received, diagonal, u_in, u_out, outside, h, hd,
                work=WORK4,
            )
        final = level == 0
        shapes = (matrix,) * 3
        if final:
            shapes = (
                jax.ShapeDtypeStruct((3, 2, size, size), F32),
                jax.ShapeDtypeStruct((3, size, size), F32),
            ) + shapes
        else:
            shapes = (matrix, token) + shapes
        results = call(
            functools.partial(swapped, outward_kernel, level, final, len(exchange.later)),
            shapes,
            *exchange.later, arrived, ready, diagonal, upper, lower, h, hd,
            space=[pl.ANY] * len(exchange.later) + [pltpu.VMEM] * 7,
            work=WORK6,
        )
        message, _, diagonal, upper, lower = results
    green_out, packed = results[:2]
    own = [packed] + [
        lax.ppermute(packed, "chip", [(i, i + r) for i in range(chips - r)]) for r in range(1, chips)
    ]
    other = [lax.ppermute(pack, "core", swap) for pack in own]
    kind = jax.ShapeDtypeStruct(screened.shape[3:], F32)
    unpacked = (chips, 3, 2, size, size)
    mine, theirs = call(
        same_core_kernel, (kind,) * 2, *own, *exchange.pieces,
        scratch_shapes=[pltpu.VMEM(unpacked, F32)],
        work=WORK5,
    )
    theirs, spectral = call(
        theirs_kernel, (kind, jax.ShapeDtypeStruct(unpacked, F32)), *other, theirs, *exchange.pieces
    )
    received = lax.ppermute(theirs, "core", swap)
    half_out = call(
        mine_kernel,
        jax.ShapeDtypeStruct(screened.shape[2:], F32),
        spectral, mine, *exchange.pieces,
        out_space=pl.ANY,
        scratch_shapes=[pltpu.VMEM(kind.shape, F32), pltpu.SemaphoreType.DMA],
    )
    sigma_out = call(
        join_kernel,
        jax.ShapeDtypeStruct(screened.shape[2:], F32),
        received, half_out,
        space=pl.ANY,
        out_space=pl.ANY,
        input_output_aliases={1: 0},
        scratch_shapes=[pltpu.SemaphoreType.DMA],
    )
    return green_out[None, None], sigma_out[None, None]


def swapped(body, *arguments):
    fixed = [a for a in arguments if isinstance(a, (int, bool))]
    axes, *refs = arguments[len(fixed) :]
    return body(axes, *fixed, *refs)


def solution(mesh):
    cores = 2
    axes = (mesh.shape["energy"] // cores, cores, mesh.shape["space"])
    split_mesh = jax.sharding.Mesh(mesh.devices.reshape(axes), ("chip", "core", "space"))
    energy = ("chip", "core")
    placed = (
        P("space", None, None, None),
        P("space", None, None, None),
        P(energy, "space", None, None, None),
        P(energy, "space", None, None, None, None, None),
    )
    return jax.shard_map(
        functools.partial(local, axes),
        mesh=split_mesh,
        in_specs=placed,
        out_specs=(
            P(energy, "space", None, None, None, None),
            P(energy, "space", None, None, None, None, None),
        ),
        check_vma=False,
    )
```

```python
import functools
import math

import jax
import jax.numpy as jnp
from jax import lax
from jax.experimental import pallas as pl
from jax.experimental.pallas import tpu as pltpu
from jax.sharding import PartitionSpec as P

BROADEN = 0.45
THERMAL = 0.1
F32 = jnp.float32
BF16 = jnp.bfloat16

LOWEST = 1.0 / 128.0
SQUARINGS = 6
DONE = 1e-4
STEPS_MAX = 60
ROWS = 16
WORK = 1
WORK2 = 2
WORK3 = 0.1
WORK4 = 0.1
WORK5 = 0.01
WORK6 = 0.1


def schedule():
    rho = (1.0 - LOWEST) / (1.0 + LOWEST)
    scales = []
    for _ in range(SQUARINGS):
        scales.append(2.0 / (2.0 - rho * rho))
        rho = rho * rho / (2.0 - rho * rho)
    return 2.0 / (1.0 + LOWEST), scales


def real_of(x):
    return x[:, : x.shape[1] // 2]


def imag_of(x):
    return x[:, x.shape[1] // 2 :]


def wide(x):
    return jnp.concatenate([x, jnp.concatenate([-imag_of(x), real_of(x)], axis=1)], axis=0)


def dagger(x):
    return jnp.concatenate([real_of(x).T, -imag_of(x).T], axis=1)


def dot(a, b):
    return jnp.dot(a, b, preferred_element_type=F32)


def split(x):
    high = x.astype(BF16)
    return high, (x - high.astype(F32)).astype(BF16)


def product(a, b):
    rows = a.shape[0]
    a_high, a_low = split(a)
    b_high, b_low = split(b)
    both = dot(jnp.concatenate([a_high, a_low], axis=0), wide(b_high))
    return both[:rows] + both[rows:] + dot(a_high, wide(b_low))


def times_complex(x, re, im):
    return jnp.concatenate(
        [re * real_of(x) - im * imag_of(x), re * imag_of(x) + im * real_of(x)], axis=1
    )


def identity_like(x):
    size = x.shape[0]
    row = lax.broadcasted_iota(jnp.int32, x.shape, 0)
    column = lax.broadcasted_iota(jnp.int32, x.shape, 1)
    return jnp.where(row == column, 1.0, 0.0).astype(F32)


def largest(x, axis):
    return jnp.max(x, axis=axis, keepdims=True)


def invert(s, out_ref):
    size = s.shape[0]
    one = identity_like(s)
    first, scales = schedule()
    s_dagger = dagger(s)
    s_dagger_b = s_dagger.astype(BF16)
    normal = dot(s.astype(BF16), wide(s_dagger_b))
    normal_b = normal.astype(BF16)
    both = dot(jnp.concatenate([s_dagger_b, normal_b], axis=0), wide(normal_b))
    square = both[size:]
    sums = jnp.sum(jnp.sqrt(real_of(square) ** 2 + imag_of(square) ** 2), axis=0, keepdims=True)
    a = first * lax.rsqrt(largest(sums, 1))
    c = scales[0]
    x = (2.0 * c * a) * s_dagger - (c * a * a) * both[:size]
    r = one - (2.0 * c * a) * normal + (c * a * a) * square
    for c in scales[1:]:
        r_b = r.astype(BF16)
        both = dot(jnp.concatenate([x.astype(BF16), r_b], axis=0), wide(r_b))
        x = c * (x + both[:size])
        r = (1.0 - c) * one + c * both[size:]
    s_high, s_low = split(s)
    s_both = jnp.concatenate([s_high, s_low], axis=0)
    x_b = x.astype(BF16)
    both = dot(s_both, wide(x_b))
    e_b = (one - both[:size] - both[size:]).astype(BF16)
    x = x_b.astype(F32) + dot(x_b, wide(e_b))

    def step(x):
        x_high, x_low = split(x)
        both = dot(s_both, wide(x_high))
        e = one - both[:size] - both[size:] - dot(s_high, wide(x_low))
        return x + dot(x_high, wide(e.astype(BF16))), jnp.sum(e * e)

    x, left = step(x)
    out_ref[...] = x

    @pl.when(jnp.logical_not(left < DONE))
    def _():
        bound = jnp.sqrt(largest(jnp.sum(jnp.abs(s), axis=1, keepdims=True), 0))
        other = jnp.sqrt(largest(jnp.sum(jnp.abs(real_of(s)) + jnp.abs(imag_of(s)), axis=0, keepdims=True), 1))
        safe = s_dagger / (bound * bound) / (other * other)
        good = left < 0.5
        start = jnp.where(good, x, safe)

        def unfinished(state):
            count, value, _ = state
            return jnp.logical_and(count < STEPS_MAX, jnp.logical_not(value < DONE))

        def body(state):
            count, _, x = state
            new = product(x, one - product(s, x))
            e = one - product(s, x)
            return count + 1, jnp.sum(e * e), x + new

        _, _, result = lax.while_loop(unfinished, body, (0, left, start))
        out_ref[...] = result


def energy_at(index, energies_all):
    return -1.5 + 3.0 * (index + 0.5) / energies_all


def energy_point(axes):
    chips, cores, _ = axes
    index = lax.axis_index("chip") * cores + lax.axis_index("core")
    return energy_at(index.astype(F32), chips * cores)


def place(axes):
    position, cells_all = lax.axis_index("space"), axes[2]
    return position, jnp.minimum(position, cells_all - 1 - position), position < cells_all // 2


def outer_kernel(
    axes, onsite_far, hopping_far, sigma_far, system_ref, green_ref, message_ref, h_ref, hd_ref, token_ref, onsite, hopping, sigma, arrivals
):
    copies = [
        pltpu.make_async_copy(far, near, arrivals.at[i])
        for i, (far, near) in enumerate(((onsite_far, onsite), (hopping_far, hopping), (sigma_far, sigma)))
    ]
    for copy in copies:
        copy.start()
    for copy in copies:
        copy.wait()
    position, depth, left = place(axes)
    energy = energy_point(axes)
    on = jnp.concatenate([onsite[0, 0], onsite[0, 1]], axis=1)
    sg = jnp.concatenate([sigma[0, 0, 0], sigma[0, 0, 1]], axis=1)
    h = jnp.concatenate([hopping[0, 0], hopping[0, 1]], axis=1)
    hd = dagger(h)
    h_ref[...] = h
    token_ref[...] = jnp.zeros_like(token_ref)
    hd_ref[...] = hd
    shape = on.shape
    row = lax.broadcasted_iota(jnp.int32, shape, 0)
    column = lax.broadcasted_iota(jnp.int32, shape, 1)
    point = jnp.where(row == column, energy, 0.0) + jnp.where(row + shape[0] == column, BROADEN, 0.0)
    system_ref[...] = point - 0.5 * (on + dagger(on)) - sg

    @pl.when(position == 0)
    def _():
        magnitude = energy * energy + BROADEN * BROADEN
        system_ref[...] = system_ref[...] - times_complex(product(hd, h), energy / magnitude, -BROADEN / magnitude)

    @pl.when(depth == 0)
    def _():
        invert(system_ref[...], green_ref)
        send(left, green_ref, h, hd, message_ref)

    @pl.when(depth != 0)
    def _():
        green_ref[...] = jnp.zeros(shape, F32)
        message_ref[...] = jnp.zeros(shape, F32)


def send(plain, green_ref, h, hd, message_ref):
    @pl.when(plain)
    def _():
        message_ref[...] = green_ref[...]

    @pl.when(jnp.logical_not(plain))
    def _():
        message_ref[...] = product(h, product(green_ref[...], hd))


def inward_kernel(axes, level, _, received, system, green, message, u, outside, h, hd, system_ref, green_ref, message_ref, u_ref, outside_ref, token_ref):
    token_ref[...] = jnp.zeros_like(token_ref)
    _, depth, left = place(axes)

    @pl.when(depth == level)
    def _():
        got = received[...]

        @pl.when(left)
        def _():
            gh = product(got, h[...])
            u_ref[...] = gh
            outside_ref[...] = got
            system_ref[...] = system[...] - product(hd[...], gh)

        @pl.when(jnp.logical_not(left))
        def _():
            system_ref[...] = system[...] - got
            u_ref[...] = u[...]
            outside_ref[...] = outside[...]

        invert(system_ref[...], green_ref)
        send(left, green_ref, h[...], hd[...], message_ref)

    @pl.when(depth != level)
    def _():
        system_ref[...] = system[...]
        green_ref[...] = green[...]
        message_ref[...] = message[...]
        u_ref[...] = u[...]
        outside_ref[...] = outside[...]


def middle_kernel(axes, received, system, green, h, hd, diagonal_ref, message_ref, u_ref):
    _, depth, left = place(axes)

    @pl.when(depth == axes[2] // 2 - 1)
    def _():
        got = received[...]

        @pl.when(left)
        def _():
            u_ref[...] = system[...] - got

        @pl.when(jnp.logical_not(left))
        def _():
            message_ref[...] = product(got, h[...])
            u_ref[...] = system[...] - product(hd[...], message_ref[...])

        s = u_ref[...]
        u_ref[...] = message_ref[...]
        invert(s, diagonal_ref)
        send(jnp.logical_not(left), diagonal_ref, h[...], hd[...], message_ref)

    @pl.when(depth != axes[2] // 2 - 1)
    def _():
        diagonal_ref[...] = green[...]
        u_ref[...] = jnp.zeros_like(u_ref)
        message_ref[...] = jnp.zeros_like(message_ref)


def waiting_kernel(axes, received, diagonal, u_in, u_out, outside, h, hd, upper_ref, lower_ref, ready_ref):
    position, depth, left = place(axes)
    energy = energy_point(axes)
    magnitude = energy * energy + BROADEN * BROADEN
    contact_re, contact_im = energy / magnitude, -BROADEN / magnitude

    @pl.when(depth == axes[2] // 2 - 1)
    def _():
        u = jnp.where(left, u_out[...], u_in[...])
        v = product(hd[...], jnp.where(left, outside[...], received[...]))
        upper_ref[...] = product(u, diagonal[...])
        lower_ref[...] = product(diagonal[...], v)
        ready_ref[...] = jnp.zeros_like(ready_ref)

    @pl.when(depth != axes[2] // 2 - 1)
    def _():
        g = diagonal[...]

        @pl.when(left)
        def _():
            at_contact = position == 0
            u = jnp.where(at_contact, times_complex(h[...], contact_re, contact_im), u_out[...])
            v = jnp.where(at_contact, times_complex(hd[...], contact_re, contact_im), product(hd[...], outside[...]))
            ready_ref[0] = g
            ready_ref[1] = g
            ready_ref[2] = product(u, g)
            ready_ref[3] = product(g, v)

        @pl.when(jnp.logical_not(left))
        def _():
            ready_ref[0] = product(g, hd[...])
            ready_ref[1] = product(h[...], g)
            ready_ref[2] = jnp.zeros_like(g)
            ready_ref[3] = jnp.zeros_like(g)

        upper_ref[...] = jnp.zeros_like(upper_ref)
        lower_ref[...] = jnp.zeros_like(lower_ref)


def outward_kernel(axes, level, final, waited, *refs):
    outward(axes, level, final, *refs[waited:])


def outward(axes, level, final, received, ready, diagonal, upper, lower, h, hd, *outputs):
    _, depth, left = place(axes)
    if final:
        green_out, packed_ref, green_ref, upper_ref, lower_ref = outputs
    else:
        message_ref, _, green_ref, upper_ref, lower_ref = outputs
        message_ref[...] = jnp.zeros_like(message_ref)

    @pl.when(depth != level)
    def _():
        green_ref[...] = diagonal[...]
        upper_ref[...] = upper[...]
        lower_ref[...] = lower[...]

    @pl.when(depth == level)
    def _():
        g_in = received[...]
        p = ready[0]
        w = product(g_in, ready[1])
        green_ref[...] = diagonal[...] + product(p, w)

        @pl.when(left)
        def _():
            upper_ref[...] = ready[2] + product(ready[2], w)
            lower_ref[...] = ready[3] + product(p, product(g_in, ready[3]))

        @pl.when(jnp.logical_not(left))
        def _():
            upper_ref[...] = w
            lower_ref[...] = product(p, g_in)

        if not final:
            send(jnp.logical_not(left), green_ref, h[...], hd[...], message_ref)

    if final:
        size = diagonal.shape[0]
        blocks = (green_ref[...], upper_ref[...], lower_ref[...])
        for b, block in enumerate(blocks):
            green_out[b, 0] = real_of(block)
            green_out[b, 1] = imag_of(block)
        d0 = blocks[0] - dagger(blocks[0])
        d1 = blocks[1] - dagger(blocks[2])
        row = lax.broadcasted_iota(jnp.int32, (size, size), 0)
        column = lax.broadcasted_iota(jnp.int32, (size, size), 1)
        packed_ref[0] = jnp.where(row > column, real_of(d0), imag_of(d0))
        packed_ref[1] = real_of(d1)
        packed_ref[2] = imag_of(d1)


def unpack(pack, out, scale):
    size = pack.shape[-1]
    row = lax.broadcasted_iota(jnp.int32, (size, size), 0)
    column = lax.broadcasted_iota(jnp.int32, (size, size), 1)
    mixed = pack[0] * scale
    turned = mixed.T
    out[0, 0] = jnp.where(row > column, mixed, jnp.where(row < column, -turned, 0.0))
    out[0, 1] = jnp.where(row > column, turned, mixed)
    re, im = pack[1] * scale, pack[2] * scale
    out[1, 0], out[1, 1] = re, im
    out[2, 0], out[2, 1] = -re.T, im.T


def unpack_all(axes, same, packs, spectral):
    chips, cores, _ = axes
    chip, core = lax.axis_index("chip"), lax.axis_index("core")
    spectral[chips] = jnp.zeros(spectral.shape[1:], F32)
    for offset in range(chips):
        lower = jnp.bitwise_xor(chip, offset)

        @pl.when(lower <= chip)
        def _():
            index = lower * cores + (core if same else 1 - core)
            energy = energy_at(index.astype(F32), chips * cores)
            occupation = 1.0 / (1.0 + jnp.exp(jnp.full((1, 1), energy / THERMAL, F32)))
            unpack(packs[offset], spectral.at[offset], jnp.where(core == 0, -occupation, 1.0 - occupation))


def add_terms(axes, same, only, pieces, outs, spectral):
    chips, cores, _ = axes
    chip, core = lax.axis_index("chip"), lax.axis_index("core")
    size = spectral.shape[-1]
    for c in range(cores):
        p = c if same else 1 - c

        @pl.when(core == c)
        def _():
            for to in only:
                k = (c + to + p) % 2
                terms = []
                for offset in range(chips):
                    kappa = jnp.bitwise_xor(chip, offset) if len(pieces) > 1 else jnp.int32(offset)
                    d = chip - kappa - (p + k) // 2
                    place_of = jnp.where(d >= 0, jnp.bitwise_xor(chip, d), chips)
                    terms.append((place_of, screened_at(pieces, offset, kappa, k)))

                @pl.loop(0, size // ROWS)
                def _(tile):
                    rows = pl.ds(pl.multiple_of(tile * ROWS, ROWS), ROWS)
                    for b in range(3):
                        re, im = outs[to][b, 0, rows], outs[to][b, 1, rows]
                        for place_of, blocks in terms:
                            g_re, g_im = spectral[place_of, b, 0, rows], spectral[place_of, b, 1, rows]
                            w_re, w_im = blocks[b, 0, rows], blocks[b, 1, rows]
                            re = re - g_re * w_im - g_im * w_re
                            im = im + g_re * w_re - g_im * w_im
                        outs[to][b, 0, rows] = re
                        outs[to][b, 1, rows] = im


def same_core_kernel(axes, *refs):
    chips = axes[0]
    packs, pieces, outs, spectral = refs[:chips], refs[chips:-3], refs[-3:-1], refs[-1]
    for out in outs:
        out[...] = jnp.zeros_like(out)
    unpack_all(axes, True, packs, spectral)
    add_terms(axes, True, (0, 1), pieces, outs, spectral)


def theirs_kernel(axes, *refs):
    chips = axes[0]
    packs, before, pieces, out, spectral = refs[:chips], refs[chips], refs[chips + 1 : -2], refs[-2], refs[-1]
    out[...] = before[...]
    unpack_all(axes, False, packs, spectral)
    add_terms(axes, False, (1,), pieces, (None, out), spectral)


def mine_kernel(axes, spectral, before, *refs):
    pieces, out, held, arrival = refs[:-3], refs[-3], refs[-2], refs[-1]
    held[...] = before[...]
    add_terms(axes, False, (0,), pieces, (held, None), spectral)
    copy = pltpu.make_async_copy(held, out.at[lax.axis_index("core")], arrival)
    copy.start()
    copy.wait()


def screened_at(pieces, offset, kappa, k):
    if len(pieces) == 1:
        return pieces[0].at[kappa, k]
    return pieces[2 * offset + k]


def join_kernel(axes, received, _, out, arrival):
    copy = pltpu.make_async_copy(received, out.at[1 - lax.axis_index("core")], arrival)
    copy.start()
    copy.wait()


class Exchange:
    def __init__(self, chips, screened, swap):
        self.paired = chips == 4
        self.own = screened[0, 0]
        self.got = lax.ppermute(self.own, "core", swap)
        self.later = []

    def moved(self, piece, offset):
        return lax.ppermute(piece, "chip", [(i, i ^ offset) for i in range(4)])

    def begin(self, after):
        core = lax.axis_index("core")
        own, got, _ = lax.optimization_barrier((self.own, self.got, after))
        one, two = jnp.where(core == 0, own[0], got[1]), jnp.where(core == 0, got[0], own[1])
        if self.paired:
            self.along = [self.moved(one, 1), self.moved(two, 2)]
            self.later = [self.moved(two, 1), self.moved(one, 2)]
            self.pieces = [one, two, self.along[0], self.later[0], self.later[1], self.along[1]]
        else:
            self.pieces = [lax.all_gather(jnp.stack([one, two]), "chip", axis=0)]

    def go_on(self, after):
        if self.paired:
            first, second, _ = lax.optimization_barrier((*self.along, after))
            self.pieces += [self.moved(first, 2), self.moved(second, 1)]


def local(axes, onsite, hopping, sigma_old, screened):
    chips, cores, cells_all = axes
    size = sigma_old.shape[-1]
    half = cells_all // 2
    matrix = jax.ShapeDtypeStruct((size, 2 * size), F32)
    def call(body, out_shape, *operands, space=pltpu.VMEM, grant=16, work=WORK, out_space=None, **options):
        spec = pl.BlockSpec(memory_space=pltpu.VMEM)
        spaces = space if isinstance(space, list) else [space] * len(operands)
        return pl.pallas_call(
            functools.partial(body, axes),
            out_shape=out_shape,
            in_specs=[pl.BlockSpec(memory_space=space) for space in spaces],
            out_specs=jax.tree.map(lambda _: spec, out_shape)
            if out_space is None
            else jax.tree.map(lambda space: pl.BlockSpec(memory_space=space), out_space),
            compiler_params=pltpu.CompilerParams(vmem_limit_bytes=grant * 1024 * 1024),
            cost_estimate=pl.CostEstimate(
                flops=int(work * 80 * (2 * size) ** 3), bytes_accessed=2 * 1024 * 1024, transcendentals=0
            ),
            **options,
        )(*operands)

    swap = [(i, i ^ 1) for i in range(cores)]
    exchange = Exchange(chips, screened, swap)
    token = jax.ShapeDtypeStruct((8, size), F32)
    system, green, message, h, hd, mark = call(
        outer_kernel,
        (matrix,) * 5 + (token,),
        *(pltpu.with_memory_space_constraint(a, pltpu.HBM) for a in (onsite, hopping, sigma_old)),
        space=pltpu.HBM,
        scratch_shapes=[pltpu.VMEM(a.shape, F32) for a in (onsite, hopping, sigma_old)]
        + [pltpu.SemaphoreType.DMA((3,))],
    )
    mark = lax.ppermute(mark, "core", swap)
    exchange.begin(mark)
    u_out = outside = jnp.zeros((size, 2 * size), F32)
    for level in range(1, half):
        route = [(level - 1, level), (cells_all - level, cells_all - 1 - level)]
        received = lax.ppermute(message, "space", route)
        system, green, message, u_out, outside, next_mark = call(
            functools.partial(swapped, inward_kernel, level),
            (matrix,) * 5 + (token,),
            mark, received, system, green, message, u_out, outside, h, hd,
            work=WORK2,
        )
        if level == half - 1:
            exchange.go_on(next_mark)
    received = lax.ppermute(message, "space", [(half - 1, half), (half, half - 1)])
    diagonal, message, u_in = call(
        middle_kernel, (matrix,) * 3, received, system, green, h, hd,
        work=WORK3,
    )
    upper = None
    for level in reversed(range(half - 1)):
        route = [(level + 1, level), (cells_all - 2 - level, cells_all - 1 - level)]
        arrived = lax.ppermute(message, "space", route)
        if upper is None:
            upper, lower, ready = call(
                waiting_kernel,
                (matrix, matrix, jax.ShapeDtypeStruct((4, size, 2 * size), F32)),
                received, diagonal, u_in, u_out, outside, h, hd,
                work=WORK4,
            )
        final = level == 0
        shapes = (matrix,) * 3
        if final:
            shapes = (
                jax.ShapeDtypeStruct((3, 2, size, size), F32),
                jax.ShapeDtypeStruct((3, size, size), F32),
            ) + shapes
        else:
            shapes = (matrix, token) + shapes
        results = call(
            functools.partial(swapped, outward_kernel, level, final, len(exchange.later)),
            shapes,
            *exchange.later, arrived, ready, diagonal, upper, lower, h, hd,
            space=[pl.ANY] * len(exchange.later) + [pltpu.VMEM] * 7,
            work=WORK6,
        )
        message, _, diagonal, upper, lower = results
    green_out, packed = results[:2]
    own = [packed] + [
        lax.ppermute(packed, "chip", [(i, i ^ offset) for i in range(chips)]) for offset in range(1, chips)
    ]
    other = [lax.ppermute(pack, "core", swap) for pack in own]
    kind = jax.ShapeDtypeStruct(screened.shape[3:], F32)
    unpacked = (chips + 1, 3, 2, size, size)
    mine, theirs = call(
        same_core_kernel, (kind,) * 2, *own, *exchange.pieces,
        scratch_shapes=[pltpu.VMEM(unpacked, F32)],
        work=WORK5,
    )
    theirs, spectral = call(
        theirs_kernel, (kind, jax.ShapeDtypeStruct(unpacked, F32)), *other, theirs, *exchange.pieces
    )
    received = lax.ppermute(theirs, "core", swap)
    half_out = call(
        mine_kernel,
        jax.ShapeDtypeStruct(screened.shape[2:], F32),
        spectral, mine, *exchange.pieces,
        out_space=pl.ANY,
        scratch_shapes=[pltpu.VMEM(kind.shape, F32), pltpu.SemaphoreType.DMA],
    )
    sigma_out = call(
        join_kernel,
        jax.ShapeDtypeStruct(screened.shape[2:], F32),
        received, half_out,
        space=pl.ANY,
        out_space=pl.ANY,
        input_output_aliases={1: 0},
        scratch_shapes=[pltpu.SemaphoreType.DMA],
    )
    return green_out[None, None], sigma_out[None, None]


def swapped(body, *arguments):
    fixed = [a for a in arguments if isinstance(a, (int, bool))]
    axes, *refs = arguments[len(fixed) :]
    return body(axes, *fixed, *refs)


def solution(mesh):
    cores = 2
    axes = (mesh.shape["energy"] // cores, cores, mesh.shape["space"])
    split_mesh = jax.sharding.Mesh(mesh.devices.reshape(axes), ("chip", "core", "space"))
    energy = ("chip", "core")
    placed = (
        P("space", None, None, None),
        P("space", None, None, None),
        P(energy, "space", None, None, None),
        P(energy, "space", None, None, None, None, None),
    )
    return jax.shard_map(
        functools.partial(local, axes),
        mesh=split_mesh,
        in_specs=placed,
        out_specs=(
            P(energy, "space", None, None, None, None),
            P(energy, "space", None, None, None, None, None),
        ),
        check_vma=False,
    )
```

```python
import functools
import math

import jax
import jax.numpy as jnp
from jax import lax
from jax.experimental import pallas as pl
from jax.experimental.pallas import tpu as pltpu
from jax.sharding import PartitionSpec as P

BROADEN = 0.45
THERMAL = 0.1
F32 = jnp.float32
BF16 = jnp.bfloat16

LOWEST = 1.0 / 128.0
SQUARINGS = 6
DONE = 1e-4
STEPS_MAX = 60
ROWS = 16
WORK = 1
WORK2 = 2
WORK3 = 0.1
WORK4 = 0.1
WORK5 = 0.01
WORK6 = 0.1


def schedule():
    rho = (1.0 - LOWEST) / (1.0 + LOWEST)
    scales = []
    for _ in range(SQUARINGS):
        scales.append(2.0 / (2.0 - rho * rho))
        rho = rho * rho / (2.0 - rho * rho)
    return 2.0 / (1.0 + LOWEST), scales


def real_of(x):
    return x[:, : x.shape[1] // 2]


def imag_of(x):
    return x[:, x.shape[1] // 2 :]


def wide(x):
    return jnp.concatenate([x, jnp.concatenate([-imag_of(x), real_of(x)], axis=1)], axis=0)


def dagger(x):
    return jnp.concatenate([real_of(x).T, -imag_of(x).T], axis=1)


def dot(a, b):
    return jnp.dot(a, b, preferred_element_type=F32)


def split(x):
    high = x.astype(BF16)
    return high, (x - high.astype(F32)).astype(BF16)


def product(a, b):
    rows = a.shape[0]
    a_high, a_low = split(a)
    b_high, b_low = split(b)
    both = dot(jnp.concatenate([a_high, a_low], axis=0), wide(b_high))
    return both[:rows] + both[rows:] + dot(a_high, wide(b_low))


def times_complex(x, re, im):
    return jnp.concatenate(
        [re * real_of(x) - im * imag_of(x), re * imag_of(x) + im * real_of(x)], axis=1
    )


def identity_like(x):
    size = x.shape[0]
    row = lax.broadcasted_iota(jnp.int32, x.shape, 0)
    column = lax.broadcasted_iota(jnp.int32, x.shape, 1)
    return jnp.where(row == column, 1.0, 0.0).astype(F32)


def largest(x, axis):
    return jnp.max(x, axis=axis, keepdims=True)


def invert(s, out_ref):
    size = s.shape[0]
    one = identity_like(s)
    first, scales = schedule()
    s_dagger = dagger(s)
    s_dagger_b = s_dagger.astype(BF16)
    normal = dot(s.astype(BF16), wide(s_dagger_b))
    normal_b = normal.astype(BF16)
    both = dot(jnp.concatenate([s_dagger_b, normal_b], axis=0), wide(normal_b))
    square = both[size:]
    sums = jnp.sum(jnp.sqrt(real_of(square) ** 2 + imag_of(square) ** 2), axis=0, keepdims=True)
    a = first * lax.rsqrt(largest(sums, 1))
    c = scales[0]
    x = (2.0 * c * a) * s_dagger - (c * a * a) * both[:size]
    r = one - (2.0 * c * a) * normal + (c * a * a) * square
    for c in scales[1:]:
        r_b = r.astype(BF16)
        both = dot(jnp.concatenate([x.astype(BF16), r_b], axis=0), wide(r_b))
        x = c * (x + both[:size])
        r = (1.0 - c) * one + c * both[size:]
    s_high, s_low = split(s)
    s_both = jnp.concatenate([s_high, s_low], axis=0)
    x_b = x.astype(BF16)
    both = dot(s_both, wide(x_b))
    e_b = (one - both[:size] - both[size:]).astype(BF16)
    x = x_b.astype(F32) + dot(x_b, wide(e_b))

    def step(x):
        x_high, x_low = split(x)
        both = dot(s_both, wide(x_high))
        e = one - both[:size] - both[size:] - dot(s_high, wide(x_low))
        return x + dot(x_high, wide(e.astype(BF16))), jnp.sum(e * e)

    x, left = step(x)
    out_ref[...] = x

    @pl.when(jnp.logical_not(left < DONE))
    def _():
        bound = jnp.sqrt(largest(jnp.sum(jnp.abs(s), axis=1, keepdims=True), 0))
        other = jnp.sqrt(largest(jnp.sum(jnp.abs(real_of(s)) + jnp.abs(imag_of(s)), axis=0, keepdims=True), 1))
        safe = s_dagger / (bound * bound) / (other * other)
        good = left < 0.5
        start = jnp.where(good, x, safe)

        def unfinished(state):
            count, value, _ = state
            return jnp.logical_and(count < STEPS_MAX, jnp.logical_not(value < DONE))

        def body(state):
            count, _, x = state
            new = product(x, one - product(s, x))
            e = one - product(s, x)
            return count + 1, jnp.sum(e * e), x + new

        _, _, result = lax.while_loop(unfinished, body, (0, left, start))
        out_ref[...] = result


def energy_at(index, energies_all):
    return -1.5 + 3.0 * (index + 0.5) / energies_all


def energy_point(axes):
    chips, cores, _ = axes
    index = lax.axis_index("chip") * cores + lax.axis_index("core")
    return energy_at(index.astype(F32), chips * cores)


def place(axes):
    position, cells_all = lax.axis_index("space"), axes[2]
    return position, jnp.minimum(position, cells_all - 1 - position), position < cells_all // 2


def outer_kernel(
    axes, onsite_far, hopping_far, sigma_far, system_ref, green_ref, message_ref, h_ref, hd_ref, token_ref, onsite, hopping, sigma, arrivals
):
    copies = [
        pltpu.make_async_copy(far, near, arrivals.at[i])
        for i, (far, near) in enumerate(((onsite_far, onsite), (hopping_far, hopping), (sigma_far, sigma)))
    ]
    for copy in copies:
        copy.start()
    for copy in copies:
        copy.wait()
    position, depth, left = place(axes)
    energy = energy_point(axes)
    on = jnp.concatenate([onsite[0, 0], onsite[0, 1]], axis=1)
    sg = jnp.concatenate([sigma[0, 0, 0], sigma[0, 0, 1]], axis=1)
    h = jnp.concatenate([hopping[0, 0], hopping[0, 1]], axis=1)
    hd = dagger(h)
    h_ref[...] = h
    token_ref[...] = jnp.zeros_like(token_ref)
    hd_ref[...] = hd
    shape = on.shape
    row = lax.broadcasted_iota(jnp.int32, shape, 0)
    column = lax.broadcasted_iota(jnp.int32, shape, 1)
    point = jnp.where(row == column, energy, 0.0) + jnp.where(row + shape[0] == column, BROADEN, 0.0)
    system_ref[...] = point - 0.5 * (on + dagger(on)) - sg

    @pl.when(position == 0)
    def _():
        magnitude = energy * energy + BROADEN * BROADEN
        system_ref[...] = system_ref[...] - times_complex(product(hd, h), energy / magnitude, -BROADEN / magnitude)

    @pl.when(depth == 0)
    def _():
        invert(system_ref[...], green_ref)
        send(left, green_ref, h, hd, message_ref)

    @pl.when(depth != 0)
    def _():
        green_ref[...] = jnp.zeros(shape, F32)
        message_ref[...] = jnp.zeros(shape, F32)


def send(plain, green_ref, h, hd, message_ref):
    @pl.when(plain)
    def _():
        message_ref[...] = green_ref[...]

    @pl.when(jnp.logical_not(plain))
    def _():
        message_ref[...] = product(h, product(green_ref[...], hd))


def inward_kernel(axes, level, _, received, system, green, message, u, outside, h, hd, system_ref, green_ref, message_ref, u_ref, outside_ref):
    _, depth, left = place(axes)

    @pl.when(depth == level)
    def _():
        got = received[...]

        @pl.when(left)
        def _():
            gh = product(got, h[...])
            u_ref[...] = gh
            outside_ref[...] = got
            system_ref[...] = system[...] - product(hd[...], gh)

        @pl.when(jnp.logical_not(left))
        def _():
            system_ref[...] = system[...] - got
            u_ref[...] = u[...]
            outside_ref[...] = outside[...]

        invert(system_ref[...], green_ref)
        send(left, green_ref, h[...], hd[...], message_ref)

    @pl.when(depth != level)
    def _():
        system_ref[...] = system[...]
        green_ref[...] = green[...]
        message_ref[...] = message[...]
        u_ref[...] = u[...]
        outside_ref[...] = outside[...]


def middle_kernel(axes, received, system, green, h, hd, diagonal_ref, message_ref, u_ref):
    _, depth, left = place(axes)

    @pl.when(depth == axes[2] // 2 - 1)
    def _():
        got = received[...]

        @pl.when(left)
        def _():
            u_ref[...] = system[...] - got

        @pl.when(jnp.logical_not(left))
        def _():
            message_ref[...] = product(got, h[...])
            u_ref[...] = system[...] - product(hd[...], message_ref[...])

        s = u_ref[...]
        u_ref[...] = message_ref[...]
        invert(s, diagonal_ref)
        send(jnp.logical_not(left), diagonal_ref, h[...], hd[...], message_ref)

    @pl.when(depth != axes[2] // 2 - 1)
    def _():
        diagonal_ref[...] = green[...]
        u_ref[...] = jnp.zeros_like(u_ref)
        message_ref[...] = jnp.zeros_like(message_ref)


def waiting_kernel(axes, waited, *refs):
    received, diagonal, u_in, u_out, outside, h, hd, upper_ref, lower_ref, ready_ref = refs[waited:]
    position, depth, left = place(axes)
    energy = energy_point(axes)
    magnitude = energy * energy + BROADEN * BROADEN
    contact_re, contact_im = energy / magnitude, -BROADEN / magnitude

    @pl.when(depth == axes[2] // 2 - 1)
    def _():
        u = jnp.where(left, u_out[...], u_in[...])
        v = product(hd[...], jnp.where(left, outside[...], received[...]))
        upper_ref[...] = product(u, diagonal[...])
        lower_ref[...] = product(diagonal[...], v)
        ready_ref[...] = jnp.zeros_like(ready_ref)

    @pl.when(depth != axes[2] // 2 - 1)
    def _():
        g = diagonal[...]

        @pl.when(left)
        def _():
            at_contact = position == 0
            u = jnp.where(at_contact, times_complex(h[...], contact_re, contact_im), u_out[...])
            v = jnp.where(at_contact, times_complex(hd[...], contact_re, contact_im), product(hd[...], outside[...]))
            ready_ref[0] = g
            ready_ref[1] = g
            ready_ref[2] = product(u, g)
            ready_ref[3] = product(g, v)

        @pl.when(jnp.logical_not(left))
        def _():
            ready_ref[0] = product(g, hd[...])
            ready_ref[1] = product(h[...], g)
            ready_ref[2] = jnp.zeros_like(g)
            ready_ref[3] = jnp.zeros_like(g)

        upper_ref[...] = jnp.zeros_like(upper_ref)
        lower_ref[...] = jnp.zeros_like(lower_ref)


def outward_kernel(axes, level, final, received, ready, diagonal, upper, lower, h, hd, *outputs):
    _, depth, left = place(axes)
    if final:
        packed_ref, green_ref, upper_ref, lower_ref = outputs
    else:
        message_ref, green_ref, upper_ref, lower_ref = outputs
        message_ref[...] = jnp.zeros_like(message_ref)

    @pl.when(depth != level)
    def _():
        green_ref[...] = diagonal[...]
        upper_ref[...] = upper[...]
        lower_ref[...] = lower[...]

    @pl.when(depth == level)
    def _():
        g_in = received[...]
        p = ready[0]
        w = product(g_in, ready[1])
        green_ref[...] = diagonal[...] + product(p, w)

        @pl.when(left)
        def _():
            upper_ref[...] = ready[2] + product(ready[2], w)
            lower_ref[...] = ready[3] + product(p, product(g_in, ready[3]))

        @pl.when(jnp.logical_not(left))
        def _():
            upper_ref[...] = w
            lower_ref[...] = product(p, g_in)

        if not final:
            send(jnp.logical_not(left), green_ref, h[...], hd[...], message_ref)

    if final:
        size = diagonal.shape[0]
        blocks = (green_ref[...], upper_ref[...], lower_ref[...])
        d0 = blocks[0] - dagger(blocks[0])
        d1 = blocks[1] - dagger(blocks[2])
        row = lax.broadcasted_iota(jnp.int32, (size, size), 0)
        column = lax.broadcasted_iota(jnp.int32, (size, size), 1)
        packed_ref[0] = jnp.where(row > column, real_of(d0), imag_of(d0))
        packed_ref[1] = real_of(d1)
        packed_ref[2] = imag_of(d1)


def store_kernel(axes, diagonal, upper, lower, out, arrivals):
    size = diagonal.shape[0]
    copies = [
        pltpu.make_async_copy(block.at[:, pl.ds(part * size, size)], out.at[b, part], arrivals.at[2 * b + part])
        for b, block in enumerate((diagonal, upper, lower))
        for part in range(2)
    ]
    for copy in copies:
        copy.start()
    for copy in copies:
        copy.wait()


def unpack(pack, out, scale):
    size = pack.shape[-1]
    row = lax.broadcasted_iota(jnp.int32, (size, size), 0)
    column = lax.broadcasted_iota(jnp.int32, (size, size), 1)
    mixed = pack[0] * scale
    turned = mixed.T
    out[0, 0] = jnp.where(row > column, mixed, jnp.where(row < column, -turned, 0.0))
    out[0, 1] = jnp.where(row > column, turned, mixed)
    re, im = pack[1] * scale, pack[2] * scale
    out[1, 0], out[1, 1] = re, im
    out[2, 0], out[2, 1] = -re.T, im.T


def unpack_all(axes, same, packs, spectral):
    chips, cores, _ = axes
    chip, core = lax.axis_index("chip"), lax.axis_index("core")
    spectral[chips] = jnp.zeros(spectral.shape[1:], F32)
    for offset in range(chips):
        lower = jnp.bitwise_xor(chip, offset)

        @pl.when(lower <= chip)
        def _():
            index = lower * cores + (core if same else 1 - core)
            energy = energy_at(index.astype(F32), chips * cores)
            occupation = 1.0 / (1.0 + jnp.exp(jnp.full((1, 1), energy / THERMAL, F32)))
            unpack(packs[offset], spectral.at[offset], jnp.where(core == 0, -occupation, 1.0 - occupation))


def add_terms(axes, same, only, pieces, outs, spectral):
    chips, cores, _ = axes
    chip, core = lax.axis_index("chip"), lax.axis_index("core")
    size = spectral.shape[-1]
    for c in range(cores):
        p = c if same else 1 - c

        @pl.when(core == c)
        def _():
            for to in only:
                k = (c + to + p) % 2
                terms = []
                for offset in range(chips):
                    kappa = jnp.bitwise_xor(chip, offset) if len(pieces) > 1 else jnp.int32(offset)
                    d = chip - kappa - (p + k) // 2
                    place_of = jnp.where(d >= 0, jnp.bitwise_xor(chip, d), chips)
                    terms.append((place_of, screened_at(pieces, offset, kappa, k)))

                @pl.loop(0, size // ROWS)
                def _(tile):
                    rows = pl.ds(pl.multiple_of(tile * ROWS, ROWS), ROWS)
                    for b in range(3):
                        re, im = outs[to][b, 0, rows], outs[to][b, 1, rows]
                        for place_of, blocks in terms:
                            g_re, g_im = spectral[place_of, b, 0, rows], spectral[place_of, b, 1, rows]
                            w_re, w_im = blocks[b, 0, rows], blocks[b, 1, rows]
                            re = re - g_re * w_im - g_im * w_re
                            im = im + g_re * w_re - g_im * w_im
                        outs[to][b, 0, rows] = re
                        outs[to][b, 1, rows] = im


def same_core_kernel(axes, *refs):
    chips = axes[0]
    packs, pieces, outs, spectral = refs[:chips], refs[chips:-3], refs[-3:-1], refs[-1]
    for out in outs:
        out[...] = jnp.zeros_like(out)
    unpack_all(axes, True, packs, spectral)
    add_terms(axes, True, (0, 1), pieces, outs, spectral)


def theirs_kernel(axes, *refs):
    chips = axes[0]
    packs, before, pieces, out, spectral = refs[:chips], refs[chips], refs[chips + 1 : -2], refs[-2], refs[-1]
    out[...] = before[...]
    unpack_all(axes, False, packs, spectral)
    add_terms(axes, False, (1,), pieces, (None, out), spectral)


def mine_kernel(axes, spectral, before, *refs):
    pieces, out, held, arrival = refs[:-3], refs[-3], refs[-2], refs[-1]
    held[...] = before[...]
    add_terms(axes, False, (0,), pieces, (held, None), spectral)
    copy = pltpu.make_async_copy(held, out.at[lax.axis_index("core")], arrival)
    copy.start()
    copy.wait()


def screened_at(pieces, offset, kappa, k):
    if len(pieces) == 1:
        return pieces[0].at[kappa, k]
    return pieces[2 * offset + k]


def join_kernel(axes, received, _, out, arrival):
    copy = pltpu.make_async_copy(received, out.at[1 - lax.axis_index("core")], arrival)
    copy.start()
    copy.wait()


class Exchange:
    def __init__(self, chips, screened, swap):
        self.paired = chips == 4
        self.own = screened[0, 0]
        self.got = lax.ppermute(self.own, "core", swap)
        self.later = []

    def moved(self, piece, offset):
        return lax.ppermute(piece, "chip", [(i, i ^ offset) for i in range(4)])

    def begin(self, after):
        core = lax.axis_index("core")
        own, got, _ = lax.optimization_barrier((self.own, self.got, after))
        one, two = jnp.where(core == 0, own[0], got[1]), jnp.where(core == 0, got[0], own[1])
        if self.paired:
            self.along = [self.moved(one, 1), self.moved(two, 2)]
            self.later = [self.moved(two, 1), self.moved(one, 2)]
            self.pieces = [one, two, self.along[0], self.later[0], self.later[1], self.along[1]]
        else:
            self.pieces = [lax.all_gather(jnp.stack([one, two]), "chip", axis=0)]

    def go_on(self, after):
        if self.paired:
            first, second, _ = lax.optimization_barrier((*self.along, after))
            self.pieces += [self.moved(first, 2), self.moved(second, 1)]


def local(axes, onsite, hopping, sigma_old, screened):
    chips, cores, cells_all = axes
    size = sigma_old.shape[-1]
    half = cells_all // 2
    matrix = jax.ShapeDtypeStruct((size, 2 * size), F32)
    def call(body, out_shape, *operands, space=pltpu.VMEM, grant=16, work=WORK, out_space=None, **options):
        spec = pl.BlockSpec(memory_space=pltpu.VMEM)
        spaces = space if isinstance(space, list) else [space] * len(operands)
        return pl.pallas_call(
            functools.partial(body, axes),
            out_shape=out_shape,
            in_specs=[pl.BlockSpec(memory_space=space) for space in spaces],
            out_specs=jax.tree.map(lambda _: spec, out_shape)
            if out_space is None
            else jax.tree.map(lambda space: pl.BlockSpec(memory_space=space), out_space),
            compiler_params=pltpu.CompilerParams(vmem_limit_bytes=grant * 1024 * 1024),
            cost_estimate=pl.CostEstimate(
                flops=int(work * 80 * (2 * size) ** 3), bytes_accessed=2 * 1024 * 1024, transcendentals=0
            ),
            **options,
        )(*operands)

    swap = [(i, i ^ 1) for i in range(cores)]
    exchange = Exchange(chips, screened, swap)
    token = jax.ShapeDtypeStruct((8, size), F32)
    system, green, message, h, hd, mark = call(
        outer_kernel,
        (matrix,) * 5 + (token,),
        *(pltpu.with_memory_space_constraint(a, pltpu.HBM) for a in (onsite, hopping, sigma_old)),
        space=pltpu.HBM,
        scratch_shapes=[pltpu.VMEM(a.shape, F32) for a in (onsite, hopping, sigma_old)]
        + [pltpu.SemaphoreType.DMA((3,))],
    )
    mark = lax.ppermute(mark, "core", swap)
    exchange.begin(mark)
    u_out = outside = jnp.zeros((size, 2 * size), F32)
    for level in range(1, half):
        route = [(level - 1, level), (cells_all - level, cells_all - 1 - level)]
        received = lax.ppermute(message, "space", route)
        system, green, message, u_out, outside = call(
            functools.partial(swapped, inward_kernel, level),
            (matrix,) * 5,
            mark, received, system, green, message, u_out, outside, h, hd,
            work=WORK2,
        )
        if level == half - 1:
            exchange.go_on(message)
    received = lax.ppermute(message, "space", [(half - 1, half), (half, half - 1)])
    diagonal, message, u_in = call(
        middle_kernel, (matrix,) * 3, received, system, green, h, hd,
        work=WORK3,
    )
    upper = None
    for level in reversed(range(half - 1)):
        route = [(level + 1, level), (cells_all - 2 - level, cells_all - 1 - level)]
        arrived = lax.ppermute(message, "space", route)
        if upper is None:
            upper, lower, ready = call(
                functools.partial(swapped, waiting_kernel, len(exchange.later)),
                (matrix, matrix, jax.ShapeDtypeStruct((4, size, 2 * size), F32)),
                *exchange.later, received, diagonal, u_in, u_out, outside, h, hd,
                space=[pl.ANY] * len(exchange.later) + [pltpu.VMEM] * 7,
                work=WORK4,
            )
        final = level == 0
        shapes = (jax.ShapeDtypeStruct((3, size, size), F32) if final else matrix,) + (matrix,) * 3
        results = call(
            functools.partial(swapped, outward_kernel, level, final),
            shapes,
            arrived, ready, diagonal, upper, lower, h, hd,
            work=WORK6,
        )
        message, diagonal, upper, lower = results
    packed = message
    green_out = call(
        store_kernel,
        jax.ShapeDtypeStruct((3, 2, size, size), F32),
        diagonal, upper, lower,
        out_space=pl.ANY,
        scratch_shapes=[pltpu.SemaphoreType.DMA((6,))],
    )
    own = [packed] + [
        lax.ppermute(packed, "chip", [(i, i ^ offset) for i in range(chips)]) for offset in range(1, chips)
    ]
    kept, green_out = lax.optimization_barrier((packed, green_out))
    other = [lax.ppermute(pack, "core", swap) for pack in [kept] + own[1:]]
    kind = jax.ShapeDtypeStruct(screened.shape[3:], F32)
    unpacked = (chips + 1, 3, 2, size, size)
    mine, theirs = call(
        same_core_kernel, (kind,) * 2, *own, *exchange.pieces,
        scratch_shapes=[pltpu.VMEM(unpacked, F32)],
        work=WORK5,
    )
    theirs, spectral = call(
        theirs_kernel, (kind, jax.ShapeDtypeStruct(unpacked, F32)), *other, theirs, *exchange.pieces
    )
    received = lax.ppermute(theirs, "core", swap)
    half_out = call(
        mine_kernel,
        jax.ShapeDtypeStruct(screened.shape[2:], F32),
        spectral, mine, *exchange.pieces,
        out_space=pl.ANY,
        scratch_shapes=[pltpu.VMEM(kind.shape, F32), pltpu.SemaphoreType.DMA],
    )
    sigma_out = call(
        join_kernel,
        jax.ShapeDtypeStruct(screened.shape[2:], F32),
        received, half_out,
        space=pl.ANY,
        out_space=pl.ANY,
        input_output_aliases={1: 0},
        scratch_shapes=[pltpu.SemaphoreType.DMA],
    )
    return green_out[None, None], sigma_out[None, None]


def swapped(body, *arguments):
    fixed = [a for a in arguments if isinstance(a, (int, bool))]
    axes, *refs = arguments[len(fixed) :]
    return body(axes, *fixed, *refs)


def solution(mesh):
    cores = 2
    axes = (mesh.shape["energy"] // cores, cores, mesh.shape["space"])
    split_mesh = jax.sharding.Mesh(mesh.devices.reshape(axes), ("chip", "core", "space"))
    energy = ("chip", "core")
    placed = (
        P("space", None, None, None),
        P("space", None, None, None),
        P(energy, "space", None, None, None),
        P(energy, "space", None, None, None, None, None),
    )
    return jax.shard_map(
        functools.partial(local, axes),
        mesh=split_mesh,
        in_specs=placed,
        out_specs=(
            P(energy, "space", None, None, None, None),
            P(energy, "space", None, None, None, None, None),
        ),
        check_vma=False,
    )
```

```python
import functools
import math

import jax
import jax.numpy as jnp
from jax import lax
from jax.experimental import pallas as pl
from jax.experimental.pallas import tpu as pltpu
from jax.sharding import PartitionSpec as P

BROADEN = 0.45
THERMAL = 0.1
F32 = jnp.float32
BF16 = jnp.bfloat16

LOWEST = 1.0 / 128.0
SQUARINGS = 6
DONE = 1e-4
STEPS_MAX = 60
ROWS = 16
WORK = 1
WORK2 = 2
WORK3 = 0.1
WORK4 = 0.1
WORK5 = 0.01
WORK6 = 0.1


def schedule():
    rho = (1.0 - LOWEST) / (1.0 + LOWEST)
    scales = []
    for _ in range(SQUARINGS):
        scales.append(2.0 / (2.0 - rho * rho))
        rho = rho * rho / (2.0 - rho * rho)
    return 2.0 / (1.0 + LOWEST), scales


def real_of(x):
    return x[:, : x.shape[1] // 2]


def imag_of(x):
    return x[:, x.shape[1] // 2 :]


def wide(x):
    return jnp.concatenate([x, jnp.concatenate([-imag_of(x), real_of(x)], axis=1)], axis=0)


def dagger(x):
    return jnp.concatenate([real_of(x).T, -imag_of(x).T], axis=1)


def dot(a, b):
    return jnp.dot(a, b, preferred_element_type=F32)


def split(x):
    high = x.astype(BF16)
    return high, (x - high.astype(F32)).astype(BF16)


def product(a, b):
    rows = a.shape[0]
    a_high, a_low = split(a)
    b_high, b_low = split(b)
    both = dot(jnp.concatenate([a_high, a_low], axis=0), wide(b_high))
    return both[:rows] + both[rows:] + dot(a_high, wide(b_low))


def times_complex(x, re, im):
    return jnp.concatenate(
        [re * real_of(x) - im * imag_of(x), re * imag_of(x) + im * real_of(x)], axis=1
    )


def identity_like(x):
    size = x.shape[0]
    row = lax.broadcasted_iota(jnp.int32, x.shape, 0)
    column = lax.broadcasted_iota(jnp.int32, x.shape, 1)
    return jnp.where(row == column, 1.0, 0.0).astype(F32)


def largest(x, axis):
    return jnp.max(x, axis=axis, keepdims=True)


def invert(s, out_ref):
    size = s.shape[0]
    one = identity_like(s)
    first, scales = schedule()
    s_dagger = dagger(s)
    s_dagger_b = s_dagger.astype(BF16)
    normal = dot(s.astype(BF16), wide(s_dagger_b))
    normal_b = normal.astype(BF16)
    both = dot(jnp.concatenate([s_dagger_b, normal_b], axis=0), wide(normal_b))
    square = both[size:]
    sums = jnp.sum(jnp.sqrt(real_of(square) ** 2 + imag_of(square) ** 2), axis=0, keepdims=True)
    a = first * lax.rsqrt(largest(sums, 1))
    c = scales[0]
    x = (2.0 * c * a) * s_dagger - (c * a * a) * both[:size]
    r = one - (2.0 * c * a) * normal + (c * a * a) * square
    for c in scales[1:]:
        r_b = r.astype(BF16)
        both = dot(jnp.concatenate([x.astype(BF16), r_b], axis=0), wide(r_b))
        x = c * (x + both[:size])
        r = (1.0 - c) * one + c * both[size:]
    s_high, s_low = split(s)
    s_both = jnp.concatenate([s_high, s_low], axis=0)
    x_b = x.astype(BF16)
    both = dot(s_both, wide(x_b))
    e_b = (one - both[:size] - both[size:]).astype(BF16)
    x = x_b.astype(F32) + dot(x_b, wide(e_b))

    def step(x):
        x_high, x_low = split(x)
        both = dot(s_both, wide(x_high))
        e = one - both[:size] - both[size:] - dot(s_high, wide(x_low))
        return x + dot(x_high, wide(e.astype(BF16))), jnp.sum(e * e)

    x, left = step(x)
    out_ref[...] = x

    @pl.when(jnp.logical_not(left < DONE))
    def _():
        bound = jnp.sqrt(largest(jnp.sum(jnp.abs(s), axis=1, keepdims=True), 0))
        other = jnp.sqrt(largest(jnp.sum(jnp.abs(real_of(s)) + jnp.abs(imag_of(s)), axis=0, keepdims=True), 1))
        safe = s_dagger / (bound * bound) / (other * other)
        good = left < 0.5
        start = jnp.where(good, x, safe)

        def unfinished(state):
            count, value, _ = state
            return jnp.logical_and(count < STEPS_MAX, jnp.logical_not(value < DONE))

        def body(state):
            count, _, x = state
            new = product(x, one - product(s, x))
            e = one - product(s, x)
            return count + 1, jnp.sum(e * e), x + new

        _, _, result = lax.while_loop(unfinished, body, (0, left, start))
        out_ref[...] = result


def energy_at(index, energies_all):
    return -1.5 + 3.0 * (index + 0.5) / energies_all


def energy_point(axes):
    chips, cores, _ = axes
    index = lax.axis_index("chip") * cores + lax.axis_index("core")
    return energy_at(index.astype(F32), chips * cores)


def place(axes):
    position, cells_all = lax.axis_index("space"), axes[2]
    return position, jnp.minimum(position, cells_all - 1 - position), position < cells_all // 2


def outer_kernel(
    axes, onsite_far, hopping_far, sigma_far, system_ref, green_ref, message_ref, h_ref, hd_ref, token_ref, onsite, hopping, sigma, arrivals
):
    copies = [
        pltpu.make_async_copy(far, near, arrivals.at[i])
        for i, (far, near) in enumerate(((onsite_far, onsite), (hopping_far, hopping), (sigma_far, sigma)))
    ]
    for copy in copies:
        copy.start()
    for copy in copies:
        copy.wait()
    position, depth, left = place(axes)
    energy = energy_point(axes)
    on = jnp.concatenate([onsite[0, 0], onsite[0, 1]], axis=1)
    sg = jnp.concatenate([sigma[0, 0, 0], sigma[0, 0, 1]], axis=1)
    h = jnp.concatenate([hopping[0, 0], hopping[0, 1]], axis=1)
    hd = dagger(h)
    h_ref[...] = h
    token_ref[...] = jnp.zeros_like(token_ref)
    hd_ref[...] = hd
    shape = on.shape
    row = lax.broadcasted_iota(jnp.int32, shape, 0)
    column = lax.broadcasted_iota(jnp.int32, shape, 1)
    point = jnp.where(row == column, energy, 0.0) + jnp.where(row + shape[0] == column, BROADEN, 0.0)
    system_ref[...] = point - 0.5 * (on + dagger(on)) - sg

    @pl.when(position == 0)
    def _():
        magnitude = energy * energy + BROADEN * BROADEN
        system_ref[...] = system_ref[...] - times_complex(product(hd, h), energy / magnitude, -BROADEN / magnitude)

    @pl.when(depth == 0)
    def _():
        invert(system_ref[...], green_ref)
        send(left, green_ref, h, hd, message_ref)

    @pl.when(depth != 0)
    def _():
        green_ref[...] = jnp.zeros(shape, F32)
        message_ref[...] = jnp.zeros(shape, F32)


def send(plain, green_ref, h, hd, message_ref):
    @pl.when(plain)
    def _():
        message_ref[...] = green_ref[...]

    @pl.when(jnp.logical_not(plain))
    def _():
        message_ref[...] = product(h, product(green_ref[...], hd))


def inward_kernel(axes, level, _, received, system, green, message, u, outside, h, hd, system_ref, green_ref, message_ref, u_ref, outside_ref):
    _, depth, left = place(axes)

    @pl.when(depth == level)
    def _():
        got = received[...]

        @pl.when(left)
        def _():
            gh = product(got, h[...])
            u_ref[...] = gh
            outside_ref[...] = got
            system_ref[...] = system[...] - product(hd[...], gh)

        @pl.when(jnp.logical_not(left))
        def _():
            system_ref[...] = system[...] - got
            u_ref[...] = u[...]
            outside_ref[...] = outside[...]

        invert(system_ref[...], green_ref)
        send(left, green_ref, h[...], hd[...], message_ref)

    @pl.when(depth != level)
    def _():
        system_ref[...] = system[...]
        green_ref[...] = green[...]
        message_ref[...] = message[...]
        u_ref[...] = u[...]
        outside_ref[...] = outside[...]


def middle_kernel(axes, received, system, green, h, hd, diagonal_ref, message_ref, u_ref):
    _, depth, left = place(axes)

    @pl.when(depth == axes[2] // 2 - 1)
    def _():
        got = received[...]

        @pl.when(left)
        def _():
            u_ref[...] = system[...] - got

        @pl.when(jnp.logical_not(left))
        def _():
            message_ref[...] = product(got, h[...])
            u_ref[...] = system[...] - product(hd[...], message_ref[...])

        s = u_ref[...]
        u_ref[...] = message_ref[...]
        invert(s, diagonal_ref)
        send(jnp.logical_not(left), diagonal_ref, h[...], hd[...], message_ref)

    @pl.when(depth != axes[2] // 2 - 1)
    def _():
        diagonal_ref[...] = green[...]
        u_ref[...] = jnp.zeros_like(u_ref)
        message_ref[...] = jnp.zeros_like(message_ref)


def waiting_kernel(axes, waited, *refs):
    received, diagonal, u_in, u_out, outside, h, hd, upper_ref, lower_ref, ready_ref = refs[waited:]
    position, depth, left = place(axes)
    energy = energy_point(axes)
    magnitude = energy * energy + BROADEN * BROADEN
    contact_re, contact_im = energy / magnitude, -BROADEN / magnitude

    @pl.when(depth == axes[2] // 2 - 1)
    def _():
        u = jnp.where(left, u_out[...], u_in[...])
        v = product(hd[...], jnp.where(left, outside[...], received[...]))
        upper_ref[...] = product(u, diagonal[...])
        lower_ref[...] = product(diagonal[...], v)
        ready_ref[...] = jnp.zeros_like(ready_ref)

    @pl.when(depth != axes[2] // 2 - 1)
    def _():
        g = diagonal[...]

        @pl.when(left)
        def _():
            at_contact = position == 0
            u = jnp.where(at_contact, times_complex(h[...], contact_re, contact_im), u_out[...])
            v = jnp.where(at_contact, times_complex(hd[...], contact_re, contact_im), product(hd[...], outside[...]))
            ready_ref[0] = g
            ready_ref[1] = g
            ready_ref[2] = product(u, g)
            ready_ref[3] = product(g, v)

        @pl.when(jnp.logical_not(left))
        def _():
            ready_ref[0] = product(g, hd[...])
            ready_ref[1] = product(h[...], g)
            ready_ref[2] = jnp.zeros_like(g)
            ready_ref[3] = jnp.zeros_like(g)

        upper_ref[...] = jnp.zeros_like(upper_ref)
        lower_ref[...] = jnp.zeros_like(lower_ref)


def outward_kernel(axes, level, final, received, ready, diagonal, upper, lower, h, hd, *outputs):
    _, depth, left = place(axes)
    if final:
        packed_ref, green_ref, upper_ref, lower_ref = outputs
    else:
        message_ref, green_ref, upper_ref, lower_ref = outputs
        message_ref[...] = jnp.zeros_like(message_ref)

    @pl.when(depth != level)
    def _():
        green_ref[...] = diagonal[...]
        upper_ref[...] = upper[...]
        lower_ref[...] = lower[...]

    @pl.when(depth == level)
    def _():
        g_in = received[...]
        p = ready[0]
        w = product(g_in, ready[1])
        green_ref[...] = diagonal[...] + product(p, w)

        @pl.when(left)
        def _():
            upper_ref[...] = ready[2] + product(ready[2], w)
            lower_ref[...] = ready[3] + product(p, product(g_in, ready[3]))

        @pl.when(jnp.logical_not(left))
        def _():
            upper_ref[...] = w
            lower_ref[...] = product(p, g_in)

        if not final:
            send(jnp.logical_not(left), green_ref, h[...], hd[...], message_ref)

    if final:
        size = diagonal.shape[0]
        blocks = (green_ref[...], upper_ref[...], lower_ref[...])
        d0 = blocks[0] - dagger(blocks[0])
        d1 = blocks[1] - dagger(blocks[2])
        row = lax.broadcasted_iota(jnp.int32, (size, size), 0)
        column = lax.broadcasted_iota(jnp.int32, (size, size), 1)
        packed_ref[0] = jnp.where(row > column, real_of(d0), imag_of(d0))
        packed_ref[1] = real_of(d1)
        packed_ref[2] = imag_of(d1)


def store_kernel(axes, diagonal, upper, lower, out, arrivals):
    size = diagonal.shape[0]
    copies = [
        pltpu.make_async_copy(block.at[:, pl.ds(part * size, size)], out.at[b, part], arrivals.at[2 * b + part])
        for b, block in enumerate((diagonal, upper, lower))
        for part in range(2)
    ]
    for copy in copies:
        copy.start()
    for copy in copies:
        copy.wait()


def unpack(pack, out, scale):
    size = pack.shape[-1]
    row = lax.broadcasted_iota(jnp.int32, (size, size), 0)
    column = lax.broadcasted_iota(jnp.int32, (size, size), 1)
    mixed = pack[0] * scale
    turned = mixed.T
    out[0, 0] = jnp.where(row > column, mixed, jnp.where(row < column, -turned, 0.0))
    out[0, 1] = jnp.where(row > column, turned, mixed)
    re, im = pack[1] * scale, pack[2] * scale
    out[1, 0], out[1, 1] = re, im
    out[2, 0], out[2, 1] = -re.T, im.T


def unpack_all(axes, same, packs, spectral):
    chips, cores, _ = axes
    chip, core = lax.axis_index("chip"), lax.axis_index("core")
    spectral[chips] = jnp.zeros(spectral.shape[1:], F32)
    for offset in range(chips):
        lower = jnp.bitwise_xor(chip, offset)

        @pl.when(lower <= chip)
        def _():
            index = lower * cores + (core if same else 1 - core)
            energy = energy_at(index.astype(F32), chips * cores)
            occupation = 1.0 / (1.0 + jnp.exp(jnp.full((1, 1), energy / THERMAL, F32)))
            unpack(packs[offset], spectral.at[offset], jnp.where(core == 0, -occupation, 1.0 - occupation))


def add_terms(axes, same, only, pieces, outs, spectral):
    chips, cores, _ = axes
    chip, core = lax.axis_index("chip"), lax.axis_index("core")
    size = spectral.shape[-1]
    for c in range(cores):
        p = c if same else 1 - c

        @pl.when(core == c)
        def _():
            for to in only:
                k = (c + to + p) % 2
                terms = []
                for offset in range(chips):
                    kappa = jnp.bitwise_xor(chip, offset) if len(pieces) > 1 else jnp.int32(offset)
                    d = chip - kappa - (p + k) // 2
                    place_of = jnp.where(d >= 0, jnp.bitwise_xor(chip, d), chips)
                    terms.append((place_of, screened_at(pieces, offset, kappa, k)))

                @pl.loop(0, size // ROWS)
                def _(tile):
                    rows = pl.ds(pl.multiple_of(tile * ROWS, ROWS), ROWS)
                    for b in range(3):
                        re, im = outs[to][b, 0, rows], outs[to][b, 1, rows]
                        for place_of, blocks in terms:
                            g_re, g_im = spectral[place_of, b, 0, rows], spectral[place_of, b, 1, rows]
                            w_re, w_im = blocks[b, 0, rows], blocks[b, 1, rows]
                            re = re - g_re * w_im - g_im * w_re
                            im = im + g_re * w_re - g_im * w_im
                        outs[to][b, 0, rows] = re
                        outs[to][b, 1, rows] = im


def same_core_kernel(axes, *refs):
    chips = axes[0]
    packs, pieces, outs, spectral = refs[:chips], refs[chips:-3], refs[-3:-1], refs[-1]
    for out in outs:
        out[...] = jnp.zeros_like(out)
    unpack_all(axes, True, packs, spectral)
    add_terms(axes, True, (0, 1), pieces, outs, spectral)


def theirs_kernel(axes, *refs):
    chips = axes[0]
    packs, before, pieces, out, spectral = refs[:chips], refs[chips], refs[chips + 1 : -2], refs[-2], refs[-1]
    out[...] = before[...]
    unpack_all(axes, False, packs, spectral)
    add_terms(axes, False, (1,), pieces, (None, out), spectral)


def mine_kernel(axes, spectral, before, *refs):
    pieces, out, held, arrival = refs[:-3], refs[-3], refs[-2], refs[-1]
    held[...] = before[...]
    add_terms(axes, False, (0,), pieces, (held, None), spectral)
    copy = pltpu.make_async_copy(held, out.at[lax.axis_index("core")], arrival)
    copy.start()
    copy.wait()


def screened_at(pieces, offset, kappa, k):
    if len(pieces) == 1:
        return pieces[0].at[kappa, k]
    return pieces[2 * offset + k]


def join_kernel(axes, received, _, out, arrival):
    copy = pltpu.make_async_copy(received, out.at[1 - lax.axis_index("core")], arrival)
    copy.start()
    copy.wait()


class Exchange:
    def __init__(self, chips, screened, swap):
        self.paired = chips == 4
        self.own = screened[0, 0]
        self.got = lax.ppermute(self.own, "core", swap)
        self.later = []

    def moved(self, piece, route):
        return lax.ppermute(piece, "chip", route)

    def begin(self, after):
        core = lax.axis_index("core")
        own, got, _ = lax.optimization_barrier((self.own, self.got, after))
        one, two = jnp.where(core == 0, own[0], got[1]), jnp.where(core == 0, got[0], own[1])
        if self.paired:
            self.along = [self.moved(one, [(0, 1), (1, 0), (2, 3)]), self.moved(two, [(0, 2), (1, 3)])]
            self.later = [self.moved(two, [(0, 1), (2, 3)]), self.moved(one, [(0, 2), (1, 3)])]
            self.pieces = [one, two, self.along[0], self.later[0], self.later[1], self.along[1]]
        else:
            self.pieces = [lax.all_gather(jnp.stack([one, two]), "chip", axis=0)]

    def go_on(self, after):
        if self.paired:
            first, second, _ = lax.optimization_barrier((*self.along, after))
            self.pieces += [self.moved(first, [(0, 2), (1, 3)]), self.moved(second, [(2, 3), (3, 2)])]


def local(axes, onsite, hopping, sigma_old, screened):
    chips, cores, cells_all = axes
    size = sigma_old.shape[-1]
    half = cells_all // 2
    matrix = jax.ShapeDtypeStruct((size, 2 * size), F32)
    def call(body, out_shape, *operands, space=pltpu.VMEM, grant=16, work=WORK, out_space=None, **options):
        spec = pl.BlockSpec(memory_space=pltpu.VMEM)
        spaces = space if isinstance(space, list) else [space] * len(operands)
        return pl.pallas_call(
            functools.partial(body, axes),
            out_shape=out_shape,
            in_specs=[pl.BlockSpec(memory_space=space) for space in spaces],
            out_specs=jax.tree.map(lambda _: spec, out_shape)
            if out_space is None
            else jax.tree.map(lambda space: pl.BlockSpec(memory_space=space), out_space),
            compiler_params=pltpu.CompilerParams(vmem_limit_bytes=grant * 1024 * 1024),
            cost_estimate=pl.CostEstimate(
                flops=int(work * 80 * (2 * size) ** 3), bytes_accessed=2 * 1024 * 1024, transcendentals=0
            ),
            **options,
        )(*operands)

    swap = [(i, i ^ 1) for i in range(cores)]
    exchange = Exchange(chips, screened, swap)
    token = jax.ShapeDtypeStruct((8, size), F32)
    system, green, message, h, hd, mark = call(
        outer_kernel,
        (matrix,) * 5 + (token,),
        *(pltpu.with_memory_space_constraint(a, pltpu.HBM) for a in (onsite, hopping, sigma_old)),
        space=pltpu.HBM,
        scratch_shapes=[pltpu.VMEM(a.shape, F32) for a in (onsite, hopping, sigma_old)]
        + [pltpu.SemaphoreType.DMA((3,))],
    )
    mark = lax.ppermute(mark, "core", swap)
    exchange.begin(mark)
    u_out = outside = jnp.zeros((size, 2 * size), F32)
    for level in range(1, half):
        route = [(level - 1, level), (cells_all - level, cells_all - 1 - level)]
        received = lax.ppermute(message, "space", route)
        system, green, message, u_out, outside = call(
            functools.partial(swapped, inward_kernel, level),
            (matrix,) * 5,
            mark, received, system, green, message, u_out, outside, h, hd,
            work=WORK2,
        )
        if level == half - 1:
            exchange.go_on(message)
    received = lax.ppermute(message, "space", [(half - 1, half), (half, half - 1)])
    diagonal, message, u_in = call(
        middle_kernel, (matrix,) * 3, received, system, green, h, hd,
        work=WORK3,
    )
    upper = None
    for level in reversed(range(half - 1)):
        route = [(level + 1, level), (cells_all - 2 - level, cells_all - 1 - level)]
        arrived = lax.ppermute(message, "space", route)
        if upper is None:
            upper, lower, ready = call(
                functools.partial(swapped, waiting_kernel, len(exchange.later)),
                (matrix, matrix, jax.ShapeDtypeStruct((4, size, 2 * size), F32)),
                *exchange.later, received, diagonal, u_in, u_out, outside, h, hd,
                space=[pl.ANY] * len(exchange.later) + [pltpu.VMEM] * 7,
                work=WORK4,
            )
        final = level == 0
        shapes = (jax.ShapeDtypeStruct((3, size, size), F32) if final else matrix,) + (matrix,) * 3
        results = call(
            functools.partial(swapped, outward_kernel, level, final),
            shapes,
            arrived, ready, diagonal, upper, lower, h, hd,
            work=WORK6,
        )
        message, diagonal, upper, lower = results
    packed = message
    green_out = call(
        store_kernel,
        jax.ShapeDtypeStruct((3, 2, size, size), F32),
        diagonal, upper, lower,
        out_space=pl.ANY,
        scratch_shapes=[pltpu.SemaphoreType.DMA((6,))],
    )
    own = [packed] + [
        lax.ppermute(packed, "chip", [(i, i ^ offset) for i in range(chips)]) for offset in range(1, chips)
    ]
    kept, green_out = lax.optimization_barrier((packed, green_out))
    other = [lax.ppermute(pack, "core", swap) for pack in [kept] + own[1:]]
    kind = jax.ShapeDtypeStruct(screened.shape[3:], F32)
    unpacked = (chips + 1, 3, 2, size, size)
    mine, theirs = call(
        same_core_kernel, (kind,) * 2, *own, *exchange.pieces,
        scratch_shapes=[pltpu.VMEM(unpacked, F32)],
        work=WORK5,
    )
    theirs, spectral = call(
        theirs_kernel, (kind, jax.ShapeDtypeStruct(unpacked, F32)), *other, theirs, *exchange.pieces
    )
    received = lax.ppermute(theirs, "core", swap)
    half_out = call(
        mine_kernel,
        jax.ShapeDtypeStruct(screened.shape[2:], F32),
        spectral, mine, *exchange.pieces,
        out_space=pl.ANY,
        scratch_shapes=[pltpu.VMEM(kind.shape, F32), pltpu.SemaphoreType.DMA],
    )
    sigma_out = call(
        join_kernel,
        jax.ShapeDtypeStruct(screened.shape[2:], F32),
        received, half_out,
        space=pl.ANY,
        out_space=pl.ANY,
        input_output_aliases={1: 0},
        scratch_shapes=[pltpu.SemaphoreType.DMA],
    )
    return green_out[None, None], sigma_out[None, None]


def swapped(body, *arguments):
    fixed = [a for a in arguments if isinstance(a, (int, bool))]
    axes, *refs = arguments[len(fixed) :]
    return body(axes, *fixed, *refs)


def solution(mesh):
    cores = 2
    axes = (mesh.shape["energy"] // cores, cores, mesh.shape["space"])
    split_mesh = jax.sharding.Mesh(mesh.devices.reshape(axes), ("chip", "core", "space"))
    energy = ("chip", "core")
    placed = (
        P("space", None, None, None),
        P("space", None, None, None),
        P(energy, "space", None, None, None),
        P(energy, "space", None, None, None, None, None),
    )
    return jax.shard_map(
        functools.partial(local, axes),
        mesh=split_mesh,
        in_specs=placed,
        out_specs=(
            P(energy, "space", None, None, None, None),
            P(energy, "space", None, None, None, None, None),
        ),
        check_vma=False,
    )
```

```python
import functools
import math

import jax
import jax.numpy as jnp
from jax import lax
from jax.experimental import pallas as pl
from jax.experimental.pallas import tpu as pltpu
from jax.sharding import PartitionSpec as P

BROADEN = 0.45
THERMAL = 0.1
F32 = jnp.float32
BF16 = jnp.bfloat16

LOWEST = 1.0 / 128.0
SQUARINGS = 6
DONE = 1e-4
STEPS_MAX = 60
ROWS = 16
WORK = 1
WORK2 = 8
WORK3 = 2
WORK4 = 1
WORK5 = 0.01
WORK6 = 1


def schedule():
    rho = (1.0 - LOWEST) / (1.0 + LOWEST)
    scales = []
    for _ in range(SQUARINGS):
        scales.append(2.0 / (2.0 - rho * rho))
        rho = rho * rho / (2.0 - rho * rho)
    return 2.0 / (1.0 + LOWEST), scales


def real_of(x):
    return x[:, : x.shape[1] // 2]


def imag_of(x):
    return x[:, x.shape[1] // 2 :]


def wide(x):
    return jnp.concatenate([x, jnp.concatenate([-imag_of(x), real_of(x)], axis=1)], axis=0)


def dagger(x):
    return jnp.concatenate([real_of(x).T, -imag_of(x).T], axis=1)


def dot(a, b):
    return jnp.dot(a, b, preferred_element_type=F32)


def split(x):
    high = x.astype(BF16)
    return high, (x - high.astype(F32)).astype(BF16)


def product(a, b):
    rows = a.shape[0]
    a_high, a_low = split(a)
    b_high, b_low = split(b)
    both = dot(jnp.concatenate([a_high, a_low], axis=0), wide(b_high))
    return both[:rows] + both[rows:] + dot(a_high, wide(b_low))


def times_complex(x, re, im):
    return jnp.concatenate(
        [re * real_of(x) - im * imag_of(x), re * imag_of(x) + im * real_of(x)], axis=1
    )


def identity_like(x):
    size = x.shape[0]
    row = lax.broadcasted_iota(jnp.int32, x.shape, 0)
    column = lax.broadcasted_iota(jnp.int32, x.shape, 1)
    return jnp.where(row == column, 1.0, 0.0).astype(F32)


def largest(x, axis):
    return jnp.max(x, axis=axis, keepdims=True)


def invert(s, out_ref):
    size = s.shape[0]
    one = identity_like(s)
    first, scales = schedule()
    s_dagger = dagger(s)
    s_dagger_b = s_dagger.astype(BF16)
    normal = dot(s.astype(BF16), wide(s_dagger_b))
    normal_b = normal.astype(BF16)
    both = dot(jnp.concatenate([s_dagger_b, normal_b], axis=0), wide(normal_b))
    square = both[size:]
    sums = jnp.sum(jnp.sqrt(real_of(square) ** 2 + imag_of(square) ** 2), axis=0, keepdims=True)
    a = first * lax.rsqrt(largest(sums, 1))
    c = scales[0]
    x = (2.0 * c * a) * s_dagger - (c * a * a) * both[:size]
    r = one - (2.0 * c * a) * normal + (c * a * a) * square
    for c in scales[1:]:
        r_b = r.astype(BF16)
        both = dot(jnp.concatenate([x.astype(BF16), r_b], axis=0), wide(r_b))
        x = c * (x + both[:size])
        r = (1.0 - c) * one + c * both[size:]
    s_high, s_low = split(s)
    s_both = jnp.concatenate([s_high, s_low], axis=0)
    x_b = x.astype(BF16)
    both = dot(s_both, wide(x_b))
    e_b = (one - both[:size] - both[size:]).astype(BF16)
    x = x_b.astype(F32) + dot(x_b, wide(e_b))

    def step(x):
        x_high, x_low = split(x)
        both = dot(s_both, wide(x_high))
        e = one - both[:size] - both[size:] - dot(s_high, wide(x_low))
        return x + dot(x_high, wide(e.astype(BF16))), jnp.sum(e * e)

    x, left = step(x)
    out_ref[...] = x

    @pl.when(jnp.logical_not(left < DONE))
    def _():
        bound = jnp.sqrt(largest(jnp.sum(jnp.abs(s), axis=1, keepdims=True), 0))
        other = jnp.sqrt(largest(jnp.sum(jnp.abs(real_of(s)) + jnp.abs(imag_of(s)), axis=0, keepdims=True), 1))
        safe = s_dagger / (bound * bound) / (other * other)
        good = left < 0.5
        start = jnp.where(good, x, safe)

        def unfinished(state):
            count, value, _ = state
            return jnp.logical_and(count < STEPS_MAX, jnp.logical_not(value < DONE))

        def body(state):
            count, _, x = state
            new = product(x, one - product(s, x))
            e = one - product(s, x)
            return count + 1, jnp.sum(e * e), x + new

        _, _, result = lax.while_loop(unfinished, body, (0, left, start))
        out_ref[...] = result


def energy_at(index, energies_all):
    return -1.5 + 3.0 * (index + 0.5) / energies_all


def energy_point(axes):
    chips, cores, _ = axes
    index = lax.axis_index("chip") * cores + lax.axis_index("core")
    return energy_at(index.astype(F32), chips * cores)


def place(axes):
    position, cells_all = lax.axis_index("space"), axes[2]
    return position, jnp.minimum(position, cells_all - 1 - position), position < cells_all // 2


def outer_kernel(
    axes, onsite_far, hopping_far, sigma_far, system_ref, green_ref, message_ref, h_ref, hd_ref, token_ref, onsite, hopping, sigma, arrivals
):
    copies = [
        pltpu.make_async_copy(far, near, arrivals.at[i])
        for i, (far, near) in enumerate(((onsite_far, onsite), (hopping_far, hopping), (sigma_far, sigma)))
    ]
    for copy in copies:
        copy.start()
    for copy in copies:
        copy.wait()
    position, depth, left = place(axes)
    energy = energy_point(axes)
    on = jnp.concatenate([onsite[0, 0], onsite[0, 1]], axis=1)
    sg = jnp.concatenate([sigma[0, 0, 0], sigma[0, 0, 1]], axis=1)
    h = jnp.concatenate([hopping[0, 0], hopping[0, 1]], axis=1)
    hd = dagger(h)
    h_ref[...] = h
    token_ref[...] = jnp.zeros_like(token_ref)
    hd_ref[...] = hd
    shape = on.shape
    row = lax.broadcasted_iota(jnp.int32, shape, 0)
    column = lax.broadcasted_iota(jnp.int32, shape, 1)
    point = jnp.where(row == column, energy, 0.0) + jnp.where(row + shape[0] == column, BROADEN, 0.0)
    system_ref[...] = point - 0.5 * (on + dagger(on)) - sg

    @pl.when(position == 0)
    def _():
        magnitude = energy * energy + BROADEN * BROADEN
        system_ref[...] = system_ref[...] - times_complex(product(hd, h), energy / magnitude, -BROADEN / magnitude)

    @pl.when(depth == 0)
    def _():
        invert(system_ref[...], green_ref)
        send(left, green_ref, h, hd, message_ref)

    @pl.when(depth != 0)
    def _():
        green_ref[...] = jnp.zeros(shape, F32)
        message_ref[...] = jnp.zeros(shape, F32)


def send(plain, green_ref, h, hd, message_ref):
    @pl.when(plain)
    def _():
        message_ref[...] = green_ref[...]

    @pl.when(jnp.logical_not(plain))
    def _():
        message_ref[...] = product(h, product(green_ref[...], hd))


def inward_kernel(axes, level, _, received, system, green, message, u, outside, h, hd, system_ref, green_ref, message_ref, u_ref, outside_ref):
    _, depth, left = place(axes)

    @pl.when(depth == level)
    def _():
        got = received[...]

        @pl.when(left)
        def _():
            gh = product(got, h[...])
            u_ref[...] = gh
            outside_ref[...] = got
            system_ref[...] = system[...] - product(hd[...], gh)

        @pl.when(jnp.logical_not(left))
        def _():
            system_ref[...] = system[...] - got
            u_ref[...] = u[...]
            outside_ref[...] = outside[...]

        invert(system_ref[...], green_ref)
        send(left, green_ref, h[...], hd[...], message_ref)

    @pl.when(depth != level)
    def _():
        system_ref[...] = system[...]
        green_ref[...] = green[...]
        message_ref[...] = message[...]
        u_ref[...] = u[...]
        outside_ref[...] = outside[...]


def middle_kernel(axes, received, system, green, h, hd, diagonal_ref, message_ref, u_ref):
    _, depth, left = place(axes)

    @pl.when(depth == axes[2] // 2 - 1)
    def _():
        got = received[...]

        @pl.when(left)
        def _():
            u_ref[...] = system[...] - got

        @pl.when(jnp.logical_not(left))
        def _():
            message_ref[...] = product(got, h[...])
            u_ref[...] = system[...] - product(hd[...], message_ref[...])

        s = u_ref[...]
        u_ref[...] = message_ref[...]
        invert(s, diagonal_ref)
        send(jnp.logical_not(left), diagonal_ref, h[...], hd[...], message_ref)

    @pl.when(depth != axes[2] // 2 - 1)
    def _():
        diagonal_ref[...] = green[...]
        u_ref[...] = jnp.zeros_like(u_ref)
        message_ref[...] = jnp.zeros_like(message_ref)


def waiting_kernel(axes, waited, *refs):
    received, diagonal, u_in, u_out, outside, h, hd, upper_ref, lower_ref, ready_ref = refs[waited:]
    position, depth, left = place(axes)
    energy = energy_point(axes)
    magnitude = energy * energy + BROADEN * BROADEN
    contact_re, contact_im = energy / magnitude, -BROADEN / magnitude

    @pl.when(depth == axes[2] // 2 - 1)
    def _():
        u = jnp.where(left, u_out[...], u_in[...])
        v = product(hd[...], jnp.where(left, outside[...], received[...]))
        upper_ref[...] = product(u, diagonal[...])
        lower_ref[...] = product(diagonal[...], v)
        ready_ref[...] = jnp.zeros_like(ready_ref)

    @pl.when(depth != axes[2] // 2 - 1)
    def _():
        g = diagonal[...]

        @pl.when(left)
        def _():
            at_contact = position == 0
            u = jnp.where(at_contact, times_complex(h[...], contact_re, contact_im), u_out[...])
            v = jnp.where(at_contact, times_complex(hd[...], contact_re, contact_im), product(hd[...], outside[...]))
            ready_ref[0] = g
            ready_ref[1] = g
            ready_ref[2] = product(u, g)
            ready_ref[3] = product(g, v)

        @pl.when(jnp.logical_not(left))
        def _():
            ready_ref[0] = product(g, hd[...])
            ready_ref[1] = product(h[...], g)
            ready_ref[2] = jnp.zeros_like(g)
            ready_ref[3] = jnp.zeros_like(g)

        upper_ref[...] = jnp.zeros_like(upper_ref)
        lower_ref[...] = jnp.zeros_like(lower_ref)


def outward_kernel(axes, level, final, received, ready, diagonal, upper, lower, h, hd, *outputs):
    _, depth, left = place(axes)
    if final:
        packed_ref, green_ref, upper_ref, lower_ref = outputs
    else:
        message_ref, green_ref, upper_ref, lower_ref = outputs
        message_ref[...] = jnp.zeros_like(message_ref)

    @pl.when(depth != level)
    def _():
        green_ref[...] = diagonal[...]
        upper_ref[...] = upper[...]
        lower_ref[...] = lower[...]

    @pl.when(depth == level)
    def _():
        g_in = received[...]
        p = ready[0]
        w = product(g_in, ready[1])
        green_ref[...] = diagonal[...] + product(p, w)

        @pl.when(left)
        def _():
            upper_ref[...] = ready[2] + product(ready[2], w)
            lower_ref[...] = ready[3] + product(p, product(g_in, ready[3]))

        @pl.when(jnp.logical_not(left))
        def _():
            upper_ref[...] = w
            lower_ref[...] = product(p, g_in)

        if not final:
            send(jnp.logical_not(left), green_ref, h[...], hd[...], message_ref)

    if final:
        size = diagonal.shape[0]
        blocks = (green_ref[...], upper_ref[...], lower_ref[...])
        d0 = blocks[0] - dagger(blocks[0])
        d1 = blocks[1] - dagger(blocks[2])
        row = lax.broadcasted_iota(jnp.int32, (size, size), 0)
        column = lax.broadcasted_iota(jnp.int32, (size, size), 1)
        packed_ref[0] = jnp.where(row > column, real_of(d0), imag_of(d0))
        packed_ref[1] = real_of(d1)
        packed_ref[2] = imag_of(d1)


def store_kernel(axes, diagonal, upper, lower, out, arrivals):
    size = diagonal.shape[0]
    copies = [
        pltpu.make_async_copy(block.at[:, pl.ds(part * size, size)], out.at[b, part], arrivals.at[2 * b + part])
        for b, block in enumerate((diagonal, upper, lower))
        for part in range(2)
    ]
    for copy in copies:
        copy.start()
    for copy in copies:
        copy.wait()


def unpack(pack, out, scale):
    size = pack.shape[-1]
    row = lax.broadcasted_iota(jnp.int32, (size, size), 0)
    column = lax.broadcasted_iota(jnp.int32, (size, size), 1)
    mixed = pack[0] * scale
    turned = mixed.T
    out[0, 0] = jnp.where(row > column, mixed, jnp.where(row < column, -turned, 0.0))
    out[0, 1] = jnp.where(row > column, turned, mixed)
    re, im = pack[1] * scale, pack[2] * scale
    out[1, 0], out[1, 1] = re, im
    out[2, 0], out[2, 1] = -re.T, im.T


def unpack_all(axes, same, packs, spectral):
    chips, cores, _ = axes
    chip, core = lax.axis_index("chip"), lax.axis_index("core")
    spectral[chips] = jnp.zeros(spectral.shape[1:], F32)
    for offset in range(chips):
        lower = jnp.bitwise_xor(chip, offset)

        @pl.when(lower <= chip)
        def _():
            index = lower * cores + (core if same else 1 - core)
            energy = energy_at(index.astype(F32), chips * cores)
            occupation = 1.0 / (1.0 + jnp.exp(jnp.full((1, 1), energy / THERMAL, F32)))
            unpack(packs[offset], spectral.at[offset], jnp.where(core == 0, -occupation, 1.0 - occupation))


def add_terms(axes, same, only, pieces, outs, spectral):
    chips, cores, _ = axes
    chip, core = lax.axis_index("chip"), lax.axis_index("core")
    size = spectral.shape[-1]
    for c in range(cores):
        p = c if same else 1 - c

        @pl.when(core == c)
        def _():
            for to in only:
                k = (c + to + p) % 2
                terms = []
                for offset in range(chips):
                    kappa = jnp.bitwise_xor(chip, offset) if len(pieces) > 1 else jnp.int32(offset)
                    d = chip - kappa - (p + k) // 2
                    place_of = jnp.where(d >= 0, jnp.bitwise_xor(chip, d), chips)
                    terms.append((place_of, screened_at(pieces, offset, kappa, k)))

                @pl.loop(0, size // ROWS)
                def _(tile):
                    rows = pl.ds(pl.multiple_of(tile * ROWS, ROWS), ROWS)
                    for b in range(3):
                        re, im = outs[to][b, 0, rows], outs[to][b, 1, rows]
                        for place_of, blocks in terms:
                            g_re, g_im = spectral[place_of, b, 0, rows], spectral[place_of, b, 1, rows]
                            w_re, w_im = blocks[b, 0, rows], blocks[b, 1, rows]
                            re = re - g_re * w_im - g_im * w_re
                            im = im + g_re * w_re - g_im * w_im
                        outs[to][b, 0, rows] = re
                        outs[to][b, 1, rows] = im


def same_core_kernel(axes, *refs):
    chips = axes[0]
    packs, pieces, outs, spectral = refs[:chips], refs[chips:-3], refs[-3:-1], refs[-1]
    for out in outs:
        out[...] = jnp.zeros_like(out)
    unpack_all(axes, True, packs, spectral)
    add_terms(axes, True, (0, 1), pieces, outs, spectral)


def theirs_kernel(axes, *refs):
    chips = axes[0]
    packs, before, pieces, out, spectral = refs[:chips], refs[chips], refs[chips + 1 : -2], refs[-2], refs[-1]
    out[...] = before[...]
    unpack_all(axes, False, packs, spectral)
    add_terms(axes, False, (1,), pieces, (None, out), spectral)


def mine_kernel(axes, spectral, before, *refs):
    pieces, out, held, arrival = refs[:-3], refs[-3], refs[-2], refs[-1]
    held[...] = before[...]
    add_terms(axes, False, (0,), pieces, (held, None), spectral)
    copy = pltpu.make_async_copy(held, out.at[lax.axis_index("core")], arrival)
    copy.start()
    copy.wait()


def screened_at(pieces, offset, kappa, k):
    if len(pieces) == 1:
        return pieces[0].at[kappa, k]
    one, two, first, second, along_x, along_y = pieces
    return ((one, two), (first, along_x.at[0]), (along_y.at[0], second), (along_y.at[1], along_x.at[1]))[offset][k]


def join_kernel(axes, received, _, out, arrival):
    copy = pltpu.make_async_copy(received, out.at[1 - lax.axis_index("core")], arrival)
    copy.start()
    copy.wait()


class Exchange:
    def __init__(self, chips, screened, swap):
        self.paired = chips == 4
        self.own = screened[0, 0]
        self.got = lax.ppermute(self.own, "core", swap)
        self.later = []

    def moved(self, piece, offset):
        return lax.ppermute(piece, "chip", [(i, i ^ offset) for i in range(4)])

    def begin(self, after):
        core = lax.axis_index("core")
        own, got, _ = lax.optimization_barrier((self.own, self.got, after))
        one, two = jnp.where(core == 0, own[0], got[1]), jnp.where(core == 0, got[0], own[1])
        if self.paired:
            self.along = [self.moved(one, 1), self.moved(two, 2)]
            self.pair = [one, two]
        else:
            self.pieces = [lax.all_gather(jnp.stack([one, two]), "chip", axis=0)]

    def go_on(self, after):
        if self.paired:
            one, two, first, second, _ = lax.optimization_barrier((*self.pair, *self.along, after))
            self.later = [self.moved(jnp.stack([two, second]), 1), self.moved(jnp.stack([one, first]), 2)]
            self.pieces = [*self.pair, *self.along, *self.later]


def local(axes, onsite, hopping, sigma_old, screened):
    chips, cores, cells_all = axes
    size = sigma_old.shape[-1]
    half = cells_all // 2
    matrix = jax.ShapeDtypeStruct((size, 2 * size), F32)
    def call(body, out_shape, *operands, space=pltpu.VMEM, grant=16, work=WORK, out_space=None, **options):
        spec = pl.BlockSpec(memory_space=pltpu.VMEM)
        spaces = space if isinstance(space, list) else [space] * len(operands)
        return pl.pallas_call(
            functools.partial(body, axes),
            out_shape=out_shape,
            in_specs=[pl.BlockSpec(memory_space=space) for space in spaces],
            out_specs=jax.tree.map(lambda _: spec, out_shape)
            if out_space is None
            else jax.tree.map(lambda space: pl.BlockSpec(memory_space=space), out_space),
            compiler_params=pltpu.CompilerParams(vmem_limit_bytes=grant * 1024 * 1024),
            cost_estimate=pl.CostEstimate(
                flops=int(work * 80 * (2 * size) ** 3), bytes_accessed=2 * 1024 * 1024, transcendentals=0
            ),
            **options,
        )(*operands)

    swap = [(i, i ^ 1) for i in range(cores)]
    exchange = Exchange(chips, screened, swap)
    token = jax.ShapeDtypeStruct((8, size), F32)
    system, green, message, h, hd, mark = call(
        outer_kernel,
        (matrix,) * 5 + (token,),
        *(pltpu.with_memory_space_constraint(a, pltpu.HBM) for a in (onsite, hopping, sigma_old)),
        space=pltpu.HBM,
        scratch_shapes=[pltpu.VMEM(a.shape, F32) for a in (onsite, hopping, sigma_old)]
        + [pltpu.SemaphoreType.DMA((3,))],
    )
    mark = lax.ppermute(mark, "core", swap)
    exchange.begin(mark)
    u_out = outside = jnp.zeros((size, 2 * size), F32)
    for level in range(1, half):
        route = [(level - 1, level), (cells_all - level, cells_all - 1 - level)]
        received = lax.ppermute(message, "space", route)
        system, green, message, u_out, outside = call(
            functools.partial(swapped, inward_kernel, level),
            (matrix,) * 5,
            mark, received, system, green, message, u_out, outside, h, hd,
            work=WORK2,
        )
        if level == half - 1:
            exchange.go_on(message)
    received = lax.ppermute(message, "space", [(half - 1, half), (half, half - 1)])
    diagonal, message, u_in = call(
        middle_kernel, (matrix,) * 3, received, system, green, h, hd,
        work=WORK3,
    )
    upper = None
    for level in reversed(range(half - 1)):
        route = [(level + 1, level), (cells_all - 2 - level, cells_all - 1 - level)]
        arrived = lax.ppermute(message, "space", route)
        if upper is None:
            upper, lower, ready = call(
                functools.partial(swapped, waiting_kernel, 0),
                (matrix, matrix, jax.ShapeDtypeStruct((4, size, 2 * size), F32)),
                received, diagonal, u_in, u_out, outside, h, hd,
                work=WORK4,
            )
        final = level == 0
        shapes = (jax.ShapeDtypeStruct((3, size, size), F32) if final else matrix,) + (matrix,) * 3
        results = call(
            functools.partial(swapped, outward_kernel, level, final),
            shapes,
            arrived, ready, diagonal, upper, lower, h, hd,
            work=WORK6,
        )
        message, diagonal, upper, lower = results
    packed = message
    green_out = call(
        store_kernel,
        jax.ShapeDtypeStruct((3, 2, size, size), F32),
        diagonal, upper, lower,
        out_space=pl.ANY,
        scratch_shapes=[pltpu.SemaphoreType.DMA((6,))],
    )
    own = [packed] + [
        lax.ppermute(packed, "chip", [(i, i ^ offset) for i in range(chips)]) for offset in range(1, chips)
    ]
    kept, green_out = lax.optimization_barrier((packed, green_out))
    other = [lax.ppermute(pack, "core", swap) for pack in [kept] + own[1:]]
    kind = jax.ShapeDtypeStruct(screened.shape[3:], F32)
    unpacked = (chips + 1, 3, 2, size, size)
    mine, theirs = call(
        same_core_kernel, (kind,) * 2, *own, *exchange.pieces,
        scratch_shapes=[pltpu.VMEM(unpacked, F32)],
        work=WORK5,
    )
    theirs, spectral = call(
        theirs_kernel, (kind, jax.ShapeDtypeStruct(unpacked, F32)), *other, theirs, *exchange.pieces
    )
    received = lax.ppermute(theirs, "core", swap)
    half_out = call(
        mine_kernel,
        jax.ShapeDtypeStruct(screened.shape[2:], F32),
        spectral, mine, *exchange.pieces,
        out_space=pl.ANY,
        scratch_shapes=[pltpu.VMEM(kind.shape, F32), pltpu.SemaphoreType.DMA],
    )
    sigma_out = call(
        join_kernel,
        jax.ShapeDtypeStruct(screened.shape[2:], F32),
        received, half_out,
        space=pl.ANY,
        out_space=pl.ANY,
        input_output_aliases={1: 0},
        scratch_shapes=[pltpu.SemaphoreType.DMA],
    )
    return green_out[None, None], sigma_out[None, None]


def swapped(body, *arguments):
    fixed = [a for a in arguments if isinstance(a, (int, bool))]
    axes, *refs = arguments[len(fixed) :]
    return body(axes, *fixed, *refs)


def solution(mesh):
    cores = 2
    axes = (mesh.shape["energy"] // cores, cores, mesh.shape["space"])
    split_mesh = jax.sharding.Mesh(mesh.devices.reshape(axes), ("chip", "core", "space"))
    energy = ("chip", "core")
    placed = (
        P("space", None, None, None),
        P("space", None, None, None),
        P(energy, "space", None, None, None),
        P(energy, "space", None, None, None, None, None),
    )
    return jax.shard_map(
        functools.partial(local, axes),
        mesh=split_mesh,
        in_specs=placed,
        out_specs=(
            P(energy, "space", None, None, None, None),
            P(energy, "space", None, None, None, None, None),
        ),
        check_vma=False,
    )
```

```python
import functools
import math

import jax
import jax.numpy as jnp
from jax import lax
from jax.experimental import pallas as pl
from jax.experimental.pallas import tpu as pltpu
from jax.sharding import PartitionSpec as P

BROADEN = 0.45
THERMAL = 0.1
F32 = jnp.float32
BF16 = jnp.bfloat16

LOWEST = 1.0 / 128.0
SQUARINGS = 6
DONE = 1e-4
STEPS_MAX = 60
ROWS = 16
WORK = 1
WORK2 = 2
WORK3 = 0.1
WORK4 = 0.1
WORK5 = 0.01
WORK6 = 0.1


def schedule():
    rho = (1.0 - LOWEST) / (1.0 + LOWEST)
    scales = []
    for _ in range(SQUARINGS):
        scales.append(2.0 / (2.0 - rho * rho))
        rho = rho * rho / (2.0 - rho * rho)
    return 2.0 / (1.0 + LOWEST), scales


def real_of(x):
    return x[:, : x.shape[1] // 2]


def imag_of(x):
    return x[:, x.shape[1] // 2 :]


def wide(x):
    return jnp.concatenate([x, jnp.concatenate([-imag_of(x), real_of(x)], axis=1)], axis=0)


def dagger(x):
    return jnp.concatenate([real_of(x).T, -imag_of(x).T], axis=1)


def dot(a, b):
    return jnp.dot(a, b, preferred_element_type=F32)


def split(x):
    high = x.astype(BF16)
    return high, (x - high.astype(F32)).astype(BF16)


def product(a, b):
    rows = a.shape[0]
    a_high, a_low = split(a)
    b_high, b_low = split(b)
    both = dot(jnp.concatenate([a_high, a_low], axis=0), wide(b_high))
    return both[:rows] + both[rows:] + dot(a_high, wide(b_low))


def times_complex(x, re, im):
    return jnp.concatenate(
        [re * real_of(x) - im * imag_of(x), re * imag_of(x) + im * real_of(x)], axis=1
    )


def identity_like(x):
    size = x.shape[0]
    row = lax.broadcasted_iota(jnp.int32, x.shape, 0)
    column = lax.broadcasted_iota(jnp.int32, x.shape, 1)
    return jnp.where(row == column, 1.0, 0.0).astype(F32)


def largest(x, axis):
    return jnp.max(x, axis=axis, keepdims=True)


def invert(s, out_ref):
    size = s.shape[0]
    one = identity_like(s)
    first, scales = schedule()
    s_dagger = dagger(s)
    s_dagger_b = s_dagger.astype(BF16)
    normal = dot(s.astype(BF16), wide(s_dagger_b))
    normal_b = normal.astype(BF16)
    both = dot(jnp.concatenate([s_dagger_b, normal_b], axis=0), wide(normal_b))
    square = both[size:]
    sums = jnp.sum(jnp.sqrt(real_of(square) ** 2 + imag_of(square) ** 2), axis=0, keepdims=True)
    a = first * lax.rsqrt(largest(sums, 1))
    c = scales[0]
    x = (2.0 * c * a) * s_dagger - (c * a * a) * both[:size]
    r = one - (2.0 * c * a) * normal + (c * a * a) * square
    for c in scales[1:]:
        r_b = r.astype(BF16)
        both = dot(jnp.concatenate([x.astype(BF16), r_b], axis=0), wide(r_b))
        x = c * (x + both[:size])
        r = (1.0 - c) * one + c * both[size:]
    s_high, s_low = split(s)
    s_both = jnp.concatenate([s_high, s_low], axis=0)
    x_b = x.astype(BF16)
    both = dot(s_both, wide(x_b))
    e_b = (one - both[:size] - both[size:]).astype(BF16)
    x = x_b.astype(F32) + dot(x_b, wide(e_b))

    def step(x):
        x_high, x_low = split(x)
        both = dot(s_both, wide(x_high))
        e = one - both[:size] - both[size:] - dot(s_high, wide(x_low))
        return x + dot(x_high, wide(e.astype(BF16))), jnp.sum(e * e)

    x, left = step(x)
    out_ref[...] = x

    @pl.when(jnp.logical_not(left < DONE))
    def _():
        bound = jnp.sqrt(largest(jnp.sum(jnp.abs(s), axis=1, keepdims=True), 0))
        other = jnp.sqrt(largest(jnp.sum(jnp.abs(real_of(s)) + jnp.abs(imag_of(s)), axis=0, keepdims=True), 1))
        safe = s_dagger / (bound * bound) / (other * other)
        good = left < 0.5
        start = jnp.where(good, x, safe)

        def unfinished(state):
            count, value, _ = state
            return jnp.logical_and(count < STEPS_MAX, jnp.logical_not(value < DONE))

        def body(state):
            count, _, x = state
            new = product(x, one - product(s, x))
            e = one - product(s, x)
            return count + 1, jnp.sum(e * e), x + new

        _, _, result = lax.while_loop(unfinished, body, (0, left, start))
        out_ref[...] = result


def energy_at(index, energies_all):
    return -1.5 + 3.0 * (index + 0.5) / energies_all


def energy_point(axes):
    chips, cores, _ = axes
    index = lax.axis_index("chip") * cores + lax.axis_index("core")
    return energy_at(index.astype(F32), chips * cores)


def place(axes):
    position, cells_all = lax.axis_index("space"), axes[2]
    return position, jnp.minimum(position, cells_all - 1 - position), position < cells_all // 2


def outer_kernel(
    axes, onsite_far, hopping_far, sigma_far, system_ref, green_ref, message_ref, h_ref, hd_ref, token_ref, onsite, hopping, sigma, arrivals
):
    copies = [
        pltpu.make_async_copy(far, near, arrivals.at[i])
        for i, (far, near) in enumerate(((onsite_far, onsite), (hopping_far, hopping), (sigma_far, sigma)))
    ]
    for copy in copies:
        copy.start()
    for copy in copies:
        copy.wait()
    position, depth, left = place(axes)
    energy = energy_point(axes)
    on = jnp.concatenate([onsite[0, 0], onsite[0, 1]], axis=1)
    sg = jnp.concatenate([sigma[0, 0, 0], sigma[0, 0, 1]], axis=1)
    h = jnp.concatenate([hopping[0, 0], hopping[0, 1]], axis=1)
    hd = dagger(h)
    h_ref[...] = h
    token_ref[...] = jnp.zeros_like(token_ref)
    hd_ref[...] = hd
    shape = on.shape
    row = lax.broadcasted_iota(jnp.int32, shape, 0)
    column = lax.broadcasted_iota(jnp.int32, shape, 1)
    point = jnp.where(row == column, energy, 0.0) + jnp.where(row + shape[0] == column, BROADEN, 0.0)
    system_ref[...] = point - 0.5 * (on + dagger(on)) - sg

    @pl.when(position == 0)
    def _():
        magnitude = energy * energy + BROADEN * BROADEN
        system_ref[...] = system_ref[...] - times_complex(product(hd, h), energy / magnitude, -BROADEN / magnitude)

    @pl.when(depth == 0)
    def _():
        invert(system_ref[...], green_ref)
        send(left, green_ref, h, hd, message_ref)

    @pl.when(depth != 0)
    def _():
        green_ref[...] = jnp.zeros(shape, F32)
        message_ref[...] = jnp.zeros(shape, F32)


def send(plain, green_ref, h, hd, message_ref):
    @pl.when(plain)
    def _():
        message_ref[...] = green_ref[...]

    @pl.when(jnp.logical_not(plain))
    def _():
        message_ref[...] = product(h, product(green_ref[...], hd))


def inward_kernel(axes, level, _, received, system, green, message, u, outside, h, hd, system_ref, green_ref, message_ref, u_ref, outside_ref):
    _, depth, left = place(axes)

    @pl.when(depth == level)
    def _():
        got = received[...]

        @pl.when(left)
        def _():
            gh = product(got, h[...])
            u_ref[...] = gh
            outside_ref[...] = got
            system_ref[...] = system[...] - product(hd[...], gh)

        @pl.when(jnp.logical_not(left))
        def _():
            system_ref[...] = system[...] - got
            u_ref[...] = u[...]
            outside_ref[...] = outside[...]

        invert(system_ref[...], green_ref)
        send(left, green_ref, h[...], hd[...], message_ref)

    @pl.when(depth != level)
    def _():
        system_ref[...] = system[...]
        green_ref[...] = green[...]
        message_ref[...] = message[...]
        u_ref[...] = u[...]
        outside_ref[...] = outside[...]


def middle_kernel(axes, received, system, green, h, hd, diagonal_ref, message_ref, u_ref):
    _, depth, left = place(axes)

    @pl.when(depth == axes[2] // 2 - 1)
    def _():
        got = received[...]

        @pl.when(left)
        def _():
            u_ref[...] = system[...] - got

        @pl.when(jnp.logical_not(left))
        def _():
            message_ref[...] = product(got, h[...])
            u_ref[...] = system[...] - product(hd[...], message_ref[...])

        s = u_ref[...]
        u_ref[...] = message_ref[...]
        invert(s, diagonal_ref)
        send(jnp.logical_not(left), diagonal_ref, h[...], hd[...], message_ref)

    @pl.when(depth != axes[2] // 2 - 1)
    def _():
        diagonal_ref[...] = green[...]
        u_ref[...] = jnp.zeros_like(u_ref)
        message_ref[...] = jnp.zeros_like(message_ref)


def waiting_kernel(axes, received, diagonal, u_in, u_out, outside, h, hd, upper_ref, lower_ref, ready_ref):
    position, depth, left = place(axes)
    energy = energy_point(axes)
    magnitude = energy * energy + BROADEN * BROADEN
    contact_re, contact_im = energy / magnitude, -BROADEN / magnitude

    @pl.when(depth == axes[2] // 2 - 1)
    def _():
        u = jnp.where(left, u_out[...], u_in[...])
        v = product(hd[...], jnp.where(left, outside[...], received[...]))
        upper_ref[...] = product(u, diagonal[...])
        lower_ref[...] = product(diagonal[...], v)
        ready_ref[...] = jnp.zeros_like(ready_ref)

    @pl.when(depth != axes[2] // 2 - 1)
    def _():
        g = diagonal[...]

        @pl.when(left)
        def _():
            at_contact = position == 0
            u = jnp.where(at_contact, times_complex(h[...], contact_re, contact_im), u_out[...])
            v = jnp.where(at_contact, times_complex(hd[...], contact_re, contact_im), product(hd[...], outside[...]))
            ready_ref[0] = g
            ready_ref[1] = g
            ready_ref[2] = product(u, g)
            ready_ref[3] = product(g, v)

        @pl.when(jnp.logical_not(left))
        def _():
            ready_ref[0] = product(g, hd[...])
            ready_ref[1] = product(h[...], g)
            ready_ref[2] = jnp.zeros_like(g)
            ready_ref[3] = jnp.zeros_like(g)

        upper_ref[...] = jnp.zeros_like(upper_ref)
        lower_ref[...] = jnp.zeros_like(lower_ref)


def outward_kernel(axes, level, final, waited, *refs):
    outward(axes, level, final, *refs[waited:])


def outward(axes, level, final, received, ready, diagonal, upper, lower, h, hd, *outputs):
    _, depth, left = place(axes)
    if final:
        packed_ref, green_ref, upper_ref, lower_ref = outputs
    else:
        message_ref, green_ref, upper_ref, lower_ref = outputs
        message_ref[...] = jnp.zeros_like(message_ref)

    @pl.when(depth != level)
    def _():
        green_ref[...] = diagonal[...]
        upper_ref[...] = upper[...]
        lower_ref[...] = lower[...]

    @pl.when(depth == level)
    def _():
        g_in = received[...]
        p = ready[0]
        w = product(g_in, ready[1])
        green_ref[...] = diagonal[...] + product(p, w)

        @pl.when(left)
        def _():
            upper_ref[...] = ready[2] + product(ready[2], w)
            lower_ref[...] = ready[3] + product(p, product(g_in, ready[3]))

        @pl.when(jnp.logical_not(left))
        def _():
            upper_ref[...] = w
            lower_ref[...] = product(p, g_in)

        if not final:
            send(jnp.logical_not(left), green_ref, h[...], hd[...], message_ref)

    if final:
        size = diagonal.shape[0]
        blocks = (green_ref[...], upper_ref[...], lower_ref[...])
        d0 = blocks[0] - dagger(blocks[0])
        d1 = blocks[1] - dagger(blocks[2])
        row = lax.broadcasted_iota(jnp.int32, (size, size), 0)
        column = lax.broadcasted_iota(jnp.int32, (size, size), 1)
        packed_ref[0] = jnp.where(row > column, real_of(d0), imag_of(d0))
        packed_ref[1] = real_of(d1)
        packed_ref[2] = imag_of(d1)


def store_kernel(axes, diagonal, upper, lower, out, arrivals):
    size = diagonal.shape[0]
    copies = [
        pltpu.make_async_copy(block.at[:, pl.ds(part * size, size)], out.at[b, part], arrivals.at[2 * b + part])
        for b, block in enumerate((diagonal, upper, lower))
        for part in range(2)
    ]
    for copy in copies:
        copy.start()
    for copy in copies:
        copy.wait()


def unpack(pack, out, scale):
    size = pack.shape[-1]
    row = lax.broadcasted_iota(jnp.int32, (size, size), 0)
    column = lax.broadcasted_iota(jnp.int32, (size, size), 1)
    mixed = pack[0] * scale
    turned = mixed.T
    out[0, 0] = jnp.where(row > column, mixed, jnp.where(row < column, -turned, 0.0))
    out[0, 1] = jnp.where(row > column, turned, mixed)
    re, im = pack[1] * scale, pack[2] * scale
    out[1, 0], out[1, 1] = re, im
    out[2, 0], out[2, 1] = -re.T, im.T


def unpack_all(axes, same, packs, spectral):
    chips, cores, _ = axes
    chip, core = lax.axis_index("chip"), lax.axis_index("core")
    spectral[chips] = jnp.zeros(spectral.shape[1:], F32)
    for offset in range(chips):
        lower = jnp.bitwise_xor(chip, offset)

        @pl.when(lower <= chip)
        def _():
            index = lower * cores + (core if same else 1 - core)
            energy = energy_at(index.astype(F32), chips * cores)
            occupation = 1.0 / (1.0 + jnp.exp(jnp.full((1, 1), energy / THERMAL, F32)))
            unpack(packs[offset], spectral.at[offset], jnp.where(core == 0, -occupation, 1.0 - occupation))


def add_terms(axes, same, only, pieces, outs, spectral):
    chips, cores, _ = axes
    chip, core = lax.axis_index("chip"), lax.axis_index("core")
    size = spectral.shape[-1]
    for c in range(cores):
        p = c if same else 1 - c

        @pl.when(core == c)
        def _():
            for to in only:
                k = (c + to + p) % 2
                terms = []
                for offset in range(chips):
                    kappa = jnp.bitwise_xor(chip, offset) if len(pieces) > 1 else jnp.int32(offset)
                    d = chip - kappa - (p + k) // 2
                    place_of = jnp.where(d >= 0, jnp.bitwise_xor(chip, d), chips)
                    terms.append((place_of, screened_at(pieces, offset, kappa, k)))

                @pl.loop(0, size // ROWS)
                def _(tile):
                    rows = pl.ds(pl.multiple_of(tile * ROWS, ROWS), ROWS)
                    for b in range(3):
                        re, im = outs[to][b, 0, rows], outs[to][b, 1, rows]
                        for place_of, blocks in terms:
                            g_re, g_im = spectral[place_of, b, 0, rows], spectral[place_of, b, 1, rows]
                            w_re, w_im = blocks[b, 0, rows], blocks[b, 1, rows]
                            re = re - g_re * w_im - g_im * w_re
                            im = im + g_re * w_re - g_im * w_im
                        outs[to][b, 0, rows] = re
                        outs[to][b, 1, rows] = im


def same_core_kernel(axes, *refs):
    chips = axes[0]
    packs, pieces, outs, spectral = refs[:chips], refs[chips:-3], refs[-3:-1], refs[-1]
    for out in outs:
        out[...] = jnp.zeros_like(out)
    unpack_all(axes, True, packs, spectral)
    add_terms(axes, True, (0, 1), pieces, outs, spectral)


def theirs_kernel(axes, *refs):
    chips = axes[0]
    packs, before, pieces, out, spectral = refs[:chips], refs[chips], refs[chips + 1 : -2], refs[-2], refs[-1]
    out[...] = before[...]
    unpack_all(axes, False, packs, spectral)
    add_terms(axes, False, (1,), pieces, (None, out), spectral)


def mine_kernel(axes, spectral, before, *refs):
    pieces, out, held, arrival = refs[:-3], refs[-3], refs[-2], refs[-1]
    held[...] = before[...]
    add_terms(axes, False, (0,), pieces, (held, None), spectral)
    copy = pltpu.make_async_copy(held, out.at[lax.axis_index("core")], arrival)
    copy.start()
    copy.wait()


def screened_at(pieces, offset, kappa, k):
    if len(pieces) == 1:
        return pieces[0].at[kappa, k]
    return pieces[2 * offset + k]


def join_kernel(axes, received, _, out, arrival):
    copy = pltpu.make_async_copy(received, out.at[1 - lax.axis_index("core")], arrival)
    copy.start()
    copy.wait()


class Exchange:
    def __init__(self, chips, screened, swap):
        self.paired = chips == 4
        self.own = screened[0, 0]
        self.got = lax.ppermute(self.own, "core", swap)
        self.later = []

    def moved(self, piece, offset):
        return lax.ppermute(piece, "chip", [(i, i ^ offset) for i in range(4)])

    def begin(self, after):
        core = lax.axis_index("core")
        own, got, _ = lax.optimization_barrier((self.own, self.got, after))
        one, two = jnp.where(core == 0, own[0], got[1]), jnp.where(core == 0, got[0], own[1])
        if self.paired:
            self.along = [self.moved(one, 1), self.moved(two, 2)]
            self.later = [self.moved(two, 1), self.moved(one, 2)]
            self.pieces = [one, two, self.along[0], self.later[0], self.later[1], self.along[1]]
        else:
            self.pieces = [lax.all_gather(jnp.stack([one, two]), "chip", axis=0)]

    def go_on(self, after):
        if self.paired:
            first, second, _ = lax.optimization_barrier((*self.along, after))
            self.pieces += [self.moved(first, 2), self.moved(second, 1)]


def local(axes, onsite, hopping, sigma_old, screened):
    chips, cores, cells_all = axes
    size = sigma_old.shape[-1]
    half = cells_all // 2
    matrix = jax.ShapeDtypeStruct((size, 2 * size), F32)
    def call(body, out_shape, *operands, space=pltpu.VMEM, grant=16, work=WORK, out_space=None, **options):
        spec = pl.BlockSpec(memory_space=pltpu.VMEM)
        spaces = space if isinstance(space, list) else [space] * len(operands)
        return pl.pallas_call(
            functools.partial(body, axes),
            out_shape=out_shape,
            in_specs=[pl.BlockSpec(memory_space=space) for space in spaces],
            out_specs=jax.tree.map(lambda _: spec, out_shape)
            if out_space is None
            else jax.tree.map(lambda space: pl.BlockSpec(memory_space=space), out_space),
            compiler_params=pltpu.CompilerParams(vmem_limit_bytes=grant * 1024 * 1024),
            cost_estimate=pl.CostEstimate(
                flops=int(work * 80 * (2 * size) ** 3), bytes_accessed=2 * 1024 * 1024, transcendentals=0
            ),
            **options,
        )(*operands)

    swap = [(i, i ^ 1) for i in range(cores)]
    exchange = Exchange(chips, screened, swap)
    token = jax.ShapeDtypeStruct((8, size), F32)
    system, green, message, h, hd, mark = call(
        outer_kernel,
        (matrix,) * 5 + (token,),
        *(pltpu.with_memory_space_constraint(a, pltpu.HBM) for a in (onsite, hopping, sigma_old)),
        space=pltpu.HBM,
        scratch_shapes=[pltpu.VMEM(a.shape, F32) for a in (onsite, hopping, sigma_old)]
        + [pltpu.SemaphoreType.DMA((3,))],
    )
    mark = lax.ppermute(mark, "core", swap)
    exchange.begin(mark)
    u_out = outside = jnp.zeros((size, 2 * size), F32)
    for level in range(1, half):
        route = [(level - 1, level), (cells_all - level, cells_all - 1 - level)]
        received = lax.ppermute(message, "space", route)
        system, green, message, u_out, outside = call(
            functools.partial(swapped, inward_kernel, level),
            (matrix,) * 5,
            mark, received, system, green, message, u_out, outside, h, hd,
            work=WORK2,
        )
        if level == half - 1:
            exchange.go_on(message)
    received = lax.ppermute(message, "space", [(half - 1, half), (half, half - 1)])
    diagonal, message, u_in = call(
        middle_kernel, (matrix,) * 3, received, system, green, h, hd,
        work=WORK3,
    )
    upper = None
    for level in reversed(range(half - 1)):
        route = [(level + 1, level), (cells_all - 2 - level, cells_all - 1 - level)]
        arrived = lax.ppermute(message, "space", route)
        if upper is None:
            upper, lower, ready = call(
                waiting_kernel,
                (matrix, matrix, jax.ShapeDtypeStruct((4, size, 2 * size), F32)),
                received, diagonal, u_in, u_out, outside, h, hd,
                work=WORK4,
            )
        final = level == 0
        shapes = (jax.ShapeDtypeStruct((3, size, size), F32) if final else matrix,) + (matrix,) * 3
        results = call(
            functools.partial(swapped, outward_kernel, level, final, len(exchange.later)),
            shapes,
            *exchange.later, arrived, ready, diagonal, upper, lower, h, hd,
            space=[pl.ANY] * len(exchange.later) + [pltpu.VMEM] * 7,
            work=WORK6,
        )
        message, diagonal, upper, lower = results
    packed = message
    green_out = call(
        store_kernel,
        jax.ShapeDtypeStruct((3, 2, size, size), F32),
        diagonal, upper, lower,
        out_space=pl.ANY,
        scratch_shapes=[pltpu.SemaphoreType.DMA((6,))],
    )
    own = [packed] + [
        lax.ppermute(packed, "chip", [(i, i ^ offset) for i in range(chips)]) for offset in range(1, chips)
    ]
    kept, green_out = lax.optimization_barrier((packed, green_out))
    other = [lax.ppermute(pack, "core", swap) for pack in [kept] + own[1:]]
    kind = jax.ShapeDtypeStruct(screened.shape[3:], F32)
    unpacked = (chips + 1, 3, 2, size, size)
    mine, theirs = call(
        same_core_kernel, (kind,) * 2, *own, *exchange.pieces,
        scratch_shapes=[pltpu.VMEM(unpacked, F32)],
        work=WORK5,
    )
    theirs, spectral = call(
        theirs_kernel, (kind, jax.ShapeDtypeStruct(unpacked, F32)), *other, theirs, *exchange.pieces
    )
    received = lax.ppermute(theirs, "core", swap)
    half_out = call(
        mine_kernel,
        jax.ShapeDtypeStruct(screened.shape[2:], F32),
        spectral, mine, *exchange.pieces,
        out_space=pl.ANY,
        scratch_shapes=[pltpu.VMEM(kind.shape, F32), pltpu.SemaphoreType.DMA],
    )
    sigma_out = call(
        join_kernel,
        jax.ShapeDtypeStruct(screened.shape[2:], F32),
        received, half_out,
        space=pl.ANY,
        out_space=pl.ANY,
        input_output_aliases={1: 0},
        scratch_shapes=[pltpu.SemaphoreType.DMA],
    )
    return green_out[None, None], sigma_out[None, None]


def swapped(body, *arguments):
    fixed = [a for a in arguments if isinstance(a, (int, bool))]
    axes, *refs = arguments[len(fixed) :]
    return body(axes, *fixed, *refs)


def solution(mesh):
    cores = 2
    axes = (mesh.shape["energy"] // cores, cores, mesh.shape["space"])
    split_mesh = jax.sharding.Mesh(mesh.devices.reshape(axes), ("chip", "core", "space"))
    energy = ("chip", "core")
    placed = (
        P("space", None, None, None),
        P("space", None, None, None),
        P(energy, "space", None, None, None),
        P(energy, "space", None, None, None, None, None),
    )
    return jax.shard_map(
        functools.partial(local, axes),
        mesh=split_mesh,
        in_specs=placed,
        out_specs=(
            P(energy, "space", None, None, None, None),
            P(energy, "space", None, None, None, None, None),
        ),
        check_vma=False,
    )
```

```python
import functools
import math

import jax
import jax.numpy as jnp
from jax import lax
from jax.experimental import pallas as pl
from jax.experimental.pallas import tpu as pltpu
from jax.sharding import PartitionSpec as P

BROADEN = 0.45
THERMAL = 0.1
F32 = jnp.float32
BF16 = jnp.bfloat16

LOWEST = 1.0 / 128.0
SQUARINGS = 6
DONE = 1e-4
STEPS_MAX = 60
ROWS = 16
WORK = 1
WORK2 = 2
WORK3 = 0.1
WORK4 = 0.1
WORK5 = 0.01
WORK6 = 0.1


def schedule():
    rho = (1.0 - LOWEST) / (1.0 + LOWEST)
    scales = []
    for _ in range(SQUARINGS):
        scales.append(2.0 / (2.0 - rho * rho))
        rho = rho * rho / (2.0 - rho * rho)
    return 2.0 / (1.0 + LOWEST), scales


def real_of(x):
    return x[:, : x.shape[1] // 2]


def imag_of(x):
    return x[:, x.shape[1] // 2 :]


def wide(x):
    return jnp.concatenate([x, jnp.concatenate([-imag_of(x), real_of(x)], axis=1)], axis=0)


def dagger(x):
    return jnp.concatenate([real_of(x).T, -imag_of(x).T], axis=1)


def dot(a, b):
    return jnp.dot(a, b, preferred_element_type=F32)


def split(x):
    high = x.astype(BF16)
    return high, (x - high.astype(F32)).astype(BF16)


def product(a, b):
    rows = a.shape[0]
    a_high, a_low = split(a)
    b_high, b_low = split(b)
    both = dot(jnp.concatenate([a_high, a_low], axis=0), wide(b_high))
    return both[:rows] + both[rows:] + dot(a_high, wide(b_low))


def times_complex(x, re, im):
    return jnp.concatenate(
        [re * real_of(x) - im * imag_of(x), re * imag_of(x) + im * real_of(x)], axis=1
    )


def identity_like(x):
    size = x.shape[0]
    row = lax.broadcasted_iota(jnp.int32, x.shape, 0)
    column = lax.broadcasted_iota(jnp.int32, x.shape, 1)
    return jnp.where(row == column, 1.0, 0.0).astype(F32)


def largest(x, axis):
    return jnp.max(x, axis=axis, keepdims=True)


def invert(s, out_ref):
    size = s.shape[0]
    one = identity_like(s)
    first, scales = schedule()
    s_dagger = dagger(s)
    s_dagger_b = s_dagger.astype(BF16)
    normal = dot(s.astype(BF16), wide(s_dagger_b))
    normal_b = normal.astype(BF16)
    both = dot(jnp.concatenate([s_dagger_b, normal_b], axis=0), wide(normal_b))
    square = both[size:]
    sums = jnp.sum(jnp.sqrt(real_of(square) ** 2 + imag_of(square) ** 2), axis=0, keepdims=True)
    a = first * lax.rsqrt(largest(sums, 1))
    c = scales[0]
    x = (2.0 * c * a) * s_dagger - (c * a * a) * both[:size]
    r = one - (2.0 * c * a) * normal + (c * a * a) * square
    for c in scales[1:]:
        r_b = r.astype(BF16)
        both = dot(jnp.concatenate([x.astype(BF16), r_b], axis=0), wide(r_b))
        x = c * (x + both[:size])
        r = (1.0 - c) * one + c * both[size:]
    s_high, s_low = split(s)
    s_both = jnp.concatenate([s_high, s_low], axis=0)
    x_b = x.astype(BF16)
    both = dot(s_both, wide(x_b))
    e_b = (one - both[:size] - both[size:]).astype(BF16)
    x = x_b.astype(F32) + dot(x_b, wide(e_b))

    def step(x):
        x_high, x_low = split(x)
        both = dot(s_both, wide(x_high))
        e = one - both[:size] - both[size:] - dot(s_high, wide(x_low))
        return x + dot(x_high, wide(e.astype(BF16))), jnp.sum(e * e)

    x, left = step(x)
    out_ref[...] = x

    @pl.when(jnp.logical_not(left < DONE))
    def _():
        bound = jnp.sqrt(largest(jnp.sum(jnp.abs(s), axis=1, keepdims=True), 0))
        other = jnp.sqrt(largest(jnp.sum(jnp.abs(real_of(s)) + jnp.abs(imag_of(s)), axis=0, keepdims=True), 1))
        safe = s_dagger / (bound * bound) / (other * other)
        good = left < 0.5
        start = jnp.where(good, x, safe)

        def unfinished(state):
            count, value, _ = state
            return jnp.logical_and(count < STEPS_MAX, jnp.logical_not(value < DONE))

        def body(state):
            count, _, x = state
            new = product(x, one - product(s, x))
            e = one - product(s, x)
            return count + 1, jnp.sum(e * e), x + new

        _, _, result = lax.while_loop(unfinished, body, (0, left, start))
        out_ref[...] = result


def energy_at(index, energies_all):
    return -1.5 + 3.0 * (index + 0.5) / energies_all


def energy_point(axes):
    chips, cores, _ = axes
    index = lax.axis_index("chip") * cores + lax.axis_index("core")
    return energy_at(index.astype(F32), chips * cores)


def place(axes):
    position, cells_all = lax.axis_index("space"), axes[2]
    return position, jnp.minimum(position, cells_all - 1 - position), position < cells_all // 2


def outer_kernel(
    axes, onsite_far, hopping_far, sigma_far, system_ref, green_ref, message_ref, h_ref, hd_ref, token_ref, onsite, hopping, sigma, arrivals
):
    copies = [
        pltpu.make_async_copy(far, near, arrivals.at[i])
        for i, (far, near) in enumerate(((onsite_far, onsite), (hopping_far, hopping), (sigma_far, sigma)))
    ]
    for copy in copies:
        copy.start()
    for copy in copies:
        copy.wait()
    position, depth, left = place(axes)
    energy = energy_point(axes)
    on = jnp.concatenate([onsite[0, 0], onsite[0, 1]], axis=1)
    sg = jnp.concatenate([sigma[0, 0, 0], sigma[0, 0, 1]], axis=1)
    h = jnp.concatenate([hopping[0, 0], hopping[0, 1]], axis=1)
    hd = dagger(h)
    h_ref[...] = h
    token_ref[...] = jnp.zeros_like(token_ref)
    hd_ref[...] = hd
    shape = on.shape
    row = lax.broadcasted_iota(jnp.int32, shape, 0)
    column = lax.broadcasted_iota(jnp.int32, shape, 1)
    point = jnp.where(row == column, energy, 0.0) + jnp.where(row + shape[0] == column, BROADEN, 0.0)
    system_ref[...] = point - 0.5 * (on + dagger(on)) - sg

    @pl.when(position == 0)
    def _():
        magnitude = energy * energy + BROADEN * BROADEN
        system_ref[...] = system_ref[...] - times_complex(product(hd, h), energy / magnitude, -BROADEN / magnitude)

    @pl.when(depth == 0)
    def _():
        invert(system_ref[...], green_ref)
        send(left, green_ref, h, hd, message_ref)

    @pl.when(depth != 0)
    def _():
        green_ref[...] = jnp.zeros(shape, F32)
        message_ref[...] = jnp.zeros(shape, F32)


def send(plain, green_ref, h, hd, message_ref):
    @pl.when(plain)
    def _():
        message_ref[...] = green_ref[...]

    @pl.when(jnp.logical_not(plain))
    def _():
        message_ref[...] = product(h, product(green_ref[...], hd))


def inward_kernel(axes, level, _, received, system, green, message, u, outside, h, hd, system_ref, green_ref, message_ref, u_ref, outside_ref):
    _, depth, left = place(axes)

    @pl.when(depth == level)
    def _():
        got = received[...]

        @pl.when(left)
        def _():
            gh = product(got, h[...])
            u_ref[...] = gh
            outside_ref[...] = got
            system_ref[...] = system[...] - product(hd[...], gh)

        @pl.when(jnp.logical_not(left))
        def _():
            system_ref[...] = system[...] - got
            u_ref[...] = u[...]
            outside_ref[...] = outside[...]

        invert(system_ref[...], green_ref)
        send(left, green_ref, h[...], hd[...], message_ref)

    @pl.when(depth != level)
    def _():
        system_ref[...] = system[...]
        green_ref[...] = green[...]
        message_ref[...] = message[...]
        u_ref[...] = u[...]
        outside_ref[...] = outside[...]


def middle_kernel(axes, received, system, green, h, hd, diagonal_ref, message_ref, u_ref):
    _, depth, left = place(axes)

    @pl.when(depth == axes[2] // 2 - 1)
    def _():
        got = received[...]

        @pl.when(left)
        def _():
            u_ref[...] = system[...] - got

        @pl.when(jnp.logical_not(left))
        def _():
            message_ref[...] = product(got, h[...])
            u_ref[...] = system[...] - product(hd[...], message_ref[...])

        s = u_ref[...]
        u_ref[...] = message_ref[...]
        invert(s, diagonal_ref)
        send(jnp.logical_not(left), diagonal_ref, h[...], hd[...], message_ref)

    @pl.when(depth != axes[2] // 2 - 1)
    def _():
        diagonal_ref[...] = green[...]
        u_ref[...] = jnp.zeros_like(u_ref)
        message_ref[...] = jnp.zeros_like(message_ref)


def waiting_kernel(axes, received, diagonal, u_in, u_out, outside, h, hd, upper_ref, lower_ref, ready_ref):
    position, depth, left = place(axes)
    energy = energy_point(axes)
    magnitude = energy * energy + BROADEN * BROADEN
    contact_re, contact_im = energy / magnitude, -BROADEN / magnitude

    @pl.when(depth == axes[2] // 2 - 1)
    def _():
        u = jnp.where(left, u_out[...], u_in[...])
        v = product(hd[...], jnp.where(left, outside[...], received[...]))
        upper_ref[...] = product(u, diagonal[...])
        lower_ref[...] = product(diagonal[...], v)
        ready_ref[...] = jnp.zeros_like(ready_ref)

    @pl.when(depth != axes[2] // 2 - 1)
    def _():
        g = diagonal[...]

        @pl.when(left)
        def _():
            at_contact = position == 0
            u = jnp.where(at_contact, times_complex(h[...], contact_re, contact_im), u_out[...])
            v = jnp.where(at_contact, times_complex(hd[...], contact_re, contact_im), product(hd[...], outside[...]))
            ready_ref[0] = g
            ready_ref[1] = g
            ready_ref[2] = product(u, g)
            ready_ref[3] = product(g, v)

        @pl.when(jnp.logical_not(left))
        def _():
            ready_ref[0] = product(g, hd[...])
            ready_ref[1] = product(h[...], g)
            ready_ref[2] = jnp.zeros_like(g)
            ready_ref[3] = jnp.zeros_like(g)

        upper_ref[...] = jnp.zeros_like(upper_ref)
        lower_ref[...] = jnp.zeros_like(lower_ref)


def outward_kernel(axes, level, final, waited, *refs):
    outward(axes, level, final, *refs[waited:])


def outward(axes, level, final, received, ready, diagonal, upper, lower, h, hd, *outputs):
    _, depth, left = place(axes)
    if final:
        packed_ref, green_ref, upper_ref, lower_ref = outputs
    else:
        message_ref, green_ref, upper_ref, lower_ref = outputs
        message_ref[...] = jnp.zeros_like(message_ref)

    @pl.when(depth != level)
    def _():
        green_ref[...] = diagonal[...]
        upper_ref[...] = upper[...]
        lower_ref[...] = lower[...]

    @pl.when(depth == level)
    def _():
        g_in = received[...]
        p = ready[0]
        w = product(g_in, ready[1])
        green_ref[...] = diagonal[...] + product(p, w)

        @pl.when(left)
        def _():
            upper_ref[...] = ready[2] + product(ready[2], w)
            lower_ref[...] = ready[3] + product(p, product(g_in, ready[3]))

        @pl.when(jnp.logical_not(left))
        def _():
            upper_ref[...] = w
            lower_ref[...] = product(p, g_in)

        if not final:
            send(jnp.logical_not(left), green_ref, h[...], hd[...], message_ref)

    if final:
        size = diagonal.shape[0]
        blocks = (green_ref[...], upper_ref[...], lower_ref[...])
        d0 = blocks[0] - dagger(blocks[0])
        d1 = blocks[1] - dagger(blocks[2])
        row = lax.broadcasted_iota(jnp.int32, (size, size), 0)
        column = lax.broadcasted_iota(jnp.int32, (size, size), 1)
        packed_ref[0] = jnp.where(row > column, real_of(d0), imag_of(d0))
        packed_ref[1] = real_of(d1)
        packed_ref[2] = imag_of(d1)


def store_kernel(axes, diagonal, upper, lower, out, arrivals):
    size = diagonal.shape[0]
    copies = [
        pltpu.make_async_copy(block.at[:, pl.ds(part * size, size)], out.at[b, part], arrivals.at[2 * b + part])
        for b, block in enumerate((diagonal, upper, lower))
        for part in range(2)
    ]
    for copy in copies:
        copy.start()
    for copy in copies:
        copy.wait()


def unpack(pack, out, scale):
    size = pack.shape[-1]
    row = lax.broadcasted_iota(jnp.int32, (size, size), 0)
    column = lax.broadcasted_iota(jnp.int32, (size, size), 1)
    mixed = pack[0] * scale
    turned = mixed.T
    out[0, 0] = jnp.where(row > column, mixed, jnp.where(row < column, -turned, 0.0))
    out[0, 1] = jnp.where(row > column, turned, mixed)
    re, im = pack[1] * scale, pack[2] * scale
    out[1, 0], out[1, 1] = re, im
    out[2, 0], out[2, 1] = -re.T, im.T


def unpack_all(axes, same, packs, spectral):
    chips, cores, _ = axes
    chip, core = lax.axis_index("chip"), lax.axis_index("core")
    spectral[chips] = jnp.zeros(spectral.shape[1:], F32)
    for offset in range(chips):
        lower = jnp.bitwise_xor(chip, offset)

        @pl.when(lower <= chip)
        def _():
            index = lower * cores + (core if same else 1 - core)
            energy = energy_at(index.astype(F32), chips * cores)
            occupation = 1.0 / (1.0 + jnp.exp(jnp.full((1, 1), energy / THERMAL, F32)))
            unpack(packs[offset], spectral.at[offset], jnp.where(core == 0, -occupation, 1.0 - occupation))


def add_terms(axes, same, only, pieces, outs, spectral):
    chips, cores, _ = axes
    chip, core = lax.axis_index("chip"), lax.axis_index("core")
    size = spectral.shape[-1]
    for c in range(cores):
        p = c if same else 1 - c

        @pl.when(core == c)
        def _():
            for to in only:
                k = (c + to + p) % 2
                terms = []
                for offset in range(chips):
                    kappa = jnp.bitwise_xor(chip, offset) if len(pieces) > 1 else jnp.int32(offset)
                    d = chip - kappa - (p + k) // 2
                    place_of = jnp.where(d >= 0, jnp.bitwise_xor(chip, d), chips)
                    terms.append((place_of, screened_at(pieces, offset, kappa, k)))

                @pl.loop(0, size // ROWS)
                def _(tile):
                    rows = pl.ds(pl.multiple_of(tile * ROWS, ROWS), ROWS)
                    for b in range(3):
                        re, im = outs[to][b, 0, rows], outs[to][b, 1, rows]
                        for place_of, blocks in terms:
                            g_re, g_im = spectral[place_of, b, 0, rows], spectral[place_of, b, 1, rows]
                            w_re, w_im = blocks[b, 0, rows], blocks[b, 1, rows]
                            re = re - g_re * w_im - g_im * w_re
                            im = im + g_re * w_re - g_im * w_im
                        outs[to][b, 0, rows] = re
                        outs[to][b, 1, rows] = im


def same_core_kernel(axes, *refs):
    chips = axes[0]
    packs, pieces, outs, spectral = refs[:chips], refs[chips:-3], refs[-3:-1], refs[-1]
    for out in outs:
        out[...] = jnp.zeros_like(out)
    unpack_all(axes, True, packs, spectral)
    add_terms(axes, True, (0, 1), pieces, outs, spectral)


def theirs_kernel(axes, *refs):
    chips = axes[0]
    packs, before, pieces, out, spectral = refs[:chips], refs[chips], refs[chips + 1 : -2], refs[-2], refs[-1]
    out[...] = before[...]
    unpack_all(axes, False, packs, spectral)
    add_terms(axes, False, (1,), pieces, (None, out), spectral)


def mine_kernel(axes, spectral, before, *refs):
    pieces, out, held, arrival = refs[:-3], refs[-3], refs[-2], refs[-1]
    held[...] = before[...]
    add_terms(axes, False, (0,), pieces, (held, None), spectral)
    copy = pltpu.make_async_copy(held, out.at[lax.axis_index("core")], arrival)
    copy.start()
    copy.wait()


def screened_at(pieces, offset, kappa, k):
    if len(pieces) == 1:
        return pieces[0].at[kappa, k]
    return pieces[2 * offset + k]


def join_kernel(axes, received, _, out, arrival):
    copy = pltpu.make_async_copy(received, out.at[1 - lax.axis_index("core")], arrival)
    copy.start()
    copy.wait()


class Exchange:
    def __init__(self, chips, screened, swap):
        self.paired = chips == 4
        self.own = screened[0, 0]
        self.got = lax.ppermute(self.own, "core", swap)
        self.later = []

    def moved(self, piece, offset):
        return lax.ppermute(piece, "chip", [(i, i ^ offset) for i in range(4)])

    def begin(self, after):
        core = lax.axis_index("core")
        own, got, _ = lax.optimization_barrier((self.own, self.got, after))
        one, two = jnp.where(core == 0, own[0], got[1]), jnp.where(core == 0, got[0], own[1])
        if self.paired:
            self.along = [self.moved(one, 1), self.moved(two, 2)]
            self.later = [self.moved(two, 1), self.moved(one, 2)]
            self.pieces = [one, two, self.along[0], self.later[0], self.later[1], self.along[1]]
        else:
            self.pieces = [lax.all_gather(jnp.stack([one, two]), "chip", axis=0)]

    def go_on(self, after):
        if self.paired:
            first, _ = lax.optimization_barrier((self.along[0], after))
            second, _ = lax.optimization_barrier((self.along[1], after))
            self.pieces += [self.moved(first, 2), self.moved(second, 1)]


def local(axes, onsite, hopping, sigma_old, screened):
    chips, cores, cells_all = axes
    size = sigma_old.shape[-1]
    half = cells_all // 2
    matrix = jax.ShapeDtypeStruct((size, 2 * size), F32)
    def call(body, out_shape, *operands, space=pltpu.VMEM, grant=16, work=WORK, out_space=None, **options):
        spec = pl.BlockSpec(memory_space=pltpu.VMEM)
        spaces = space if isinstance(space, list) else [space] * len(operands)
        return pl.pallas_call(
            functools.partial(body, axes),
            out_shape=out_shape,
            in_specs=[pl.BlockSpec(memory_space=space) for space in spaces],
            out_specs=jax.tree.map(lambda _: spec, out_shape)
            if out_space is None
            else jax.tree.map(lambda space: pl.BlockSpec(memory_space=space), out_space),
            compiler_params=pltpu.CompilerParams(vmem_limit_bytes=grant * 1024 * 1024),
            cost_estimate=pl.CostEstimate(
                flops=int(work * 80 * (2 * size) ** 3), bytes_accessed=2 * 1024 * 1024, transcendentals=0
            ),
            **options,
        )(*operands)

    swap = [(i, i ^ 1) for i in range(cores)]
    exchange = Exchange(chips, screened, swap)
    token = jax.ShapeDtypeStruct((8, size), F32)
    system, green, message, h, hd, mark = call(
        outer_kernel,
        (matrix,) * 5 + (token,),
        *(pltpu.with_memory_space_constraint(a, pltpu.HBM) for a in (onsite, hopping, sigma_old)),
        space=pltpu.HBM,
        scratch_shapes=[pltpu.VMEM(a.shape, F32) for a in (onsite, hopping, sigma_old)]
        + [pltpu.SemaphoreType.DMA((3,))],
    )
    mark = lax.ppermute(mark, "core", swap)
    exchange.begin(mark)
    u_out = outside = jnp.zeros((size, 2 * size), F32)
    for level in range(1, half):
        route = [(level - 1, level), (cells_all - level, cells_all - 1 - level)]
        received = lax.ppermute(message, "space", route)
        system, green, message, u_out, outside = call(
            functools.partial(swapped, inward_kernel, level),
            (matrix,) * 5,
            mark, received, system, green, message, u_out, outside, h, hd,
            work=WORK2,
        )
        if level == half - 1:
            exchange.go_on(message)
    received = lax.ppermute(message, "space", [(half - 1, half), (half, half - 1)])
    diagonal, message, u_in = call(
        middle_kernel, (matrix,) * 3, received, system, green, h, hd,
        work=WORK3,
    )
    upper = None
    for level in reversed(range(half - 1)):
        route = [(level + 1, level), (cells_all - 2 - level, cells_all - 1 - level)]
        arrived = lax.ppermute(message, "space", route)
        if upper is None:
            upper, lower, ready = call(
                waiting_kernel,
                (matrix, matrix, jax.ShapeDtypeStruct((4, size, 2 * size), F32)),
                received, diagonal, u_in, u_out, outside, h, hd,
                work=WORK4,
            )
        final = level == 0
        shapes = (jax.ShapeDtypeStruct((3, size, size), F32) if final else matrix,) + (matrix,) * 3
        results = call(
            functools.partial(swapped, outward_kernel, level, final, len(exchange.later)),
            shapes,
            *exchange.later, arrived, ready, diagonal, upper, lower, h, hd,
            space=[pl.ANY] * len(exchange.later) + [pltpu.VMEM] * 7,
            work=WORK6,
        )
        message, diagonal, upper, lower = results
    packed = message
    green_out = call(
        store_kernel,
        jax.ShapeDtypeStruct((3, 2, size, size), F32),
        diagonal, upper, lower,
        out_space=pl.ANY,
        scratch_shapes=[pltpu.SemaphoreType.DMA((6,))],
    )
    own = [packed] + [
        lax.ppermute(packed, "chip", [(i, i ^ offset) for i in range(chips)]) for offset in range(1, chips)
    ]
    kept, green_out = lax.optimization_barrier((packed, green_out))
    other = [lax.ppermute(pack, "core", swap) for pack in [kept] + own[1:]]
    kind = jax.ShapeDtypeStruct(screened.shape[3:], F32)
    unpacked = (chips + 1, 3, 2, size, size)
    mine, theirs = call(
        same_core_kernel, (kind,) * 2, *own, *exchange.pieces,
        scratch_shapes=[pltpu.VMEM(unpacked, F32)],
        work=WORK5,
    )
    theirs, spectral = call(
        theirs_kernel, (kind, jax.ShapeDtypeStruct(unpacked, F32)), *other, theirs, *exchange.pieces
    )
    received = lax.ppermute(theirs, "core", swap)
    half_out = call(
        mine_kernel,
        jax.ShapeDtypeStruct(screened.shape[2:], F32),
        spectral, mine, *exchange.pieces,
        out_space=pl.ANY,
        scratch_shapes=[pltpu.VMEM(kind.shape, F32), pltpu.SemaphoreType.DMA],
    )
    sigma_out = call(
        join_kernel,
        jax.ShapeDtypeStruct(screened.shape[2:], F32),
        received, half_out,
        space=pl.ANY,
        out_space=pl.ANY,
        input_output_aliases={1: 0},
        scratch_shapes=[pltpu.SemaphoreType.DMA],
    )
    return green_out[None, None], sigma_out[None, None]


def swapped(body, *arguments):
    fixed = [a for a in arguments if isinstance(a, (int, bool))]
    axes, *refs = arguments[len(fixed) :]
    return body(axes, *fixed, *refs)


def solution(mesh):
    cores = 2
    axes = (mesh.shape["energy"] // cores, cores, mesh.shape["space"])
    split_mesh = jax.sharding.Mesh(mesh.devices.reshape(axes), ("chip", "core", "space"))
    energy = ("chip", "core")
    placed = (
        P("space", None, None, None),
        P("space", None, None, None),
        P(energy, "space", None, None, None),
        P(energy, "space", None, None, None, None, None),
    )
    return jax.shard_map(
        functools.partial(local, axes),
        mesh=split_mesh,
        in_specs=placed,
        out_specs=(
            P(energy, "space", None, None, None, None),
            P(energy, "space", None, None, None, None, None),
        ),
        check_vma=False,
    )
```

```python
import functools
import math

import jax
import jax.numpy as jnp
from jax import lax
from jax.experimental import pallas as pl
from jax.experimental.pallas import tpu as pltpu
from jax.sharding import PartitionSpec as P

BROADEN = 0.45
THERMAL = 0.1
F32 = jnp.float32
BF16 = jnp.bfloat16

LOWEST = 1.0 / 128.0
SQUARINGS = 6
DONE = 1e-4
STEPS_MAX = 60
ROWS = 32
WORK = 1
WORK2 = 2
WORK3 = 0.1
WORK4 = 0.1
WORK5 = 0.01
WORK6 = 0.1


def schedule():
    rho = (1.0 - LOWEST) / (1.0 + LOWEST)
    scales = []
    for _ in range(SQUARINGS):
        scales.append(2.0 / (2.0 - rho * rho))
        rho = rho * rho / (2.0 - rho * rho)
    return 2.0 / (1.0 + LOWEST), scales


def real_of(x):
    return x[:, : x.shape[1] // 2]


def imag_of(x):
    return x[:, x.shape[1] // 2 :]


def wide(x):
    return jnp.concatenate([x, jnp.concatenate([-imag_of(x), real_of(x)], axis=1)], axis=0)


def dagger(x):
    return jnp.concatenate([real_of(x).T, -imag_of(x).T], axis=1)


def dot(a, b):
    return jnp.dot(a, b, preferred_element_type=F32)


def split(x):
    high = x.astype(BF16)
    return high, (x - high.astype(F32)).astype(BF16)


def product(a, b):
    rows = a.shape[0]
    a_high, a_low = split(a)
    b_high, b_low = split(b)
    both = dot(jnp.concatenate([a_high, a_low], axis=0), wide(b_high))
    return both[:rows] + both[rows:] + dot(a_high, wide(b_low))


def times_complex(x, re, im):
    return jnp.concatenate(
        [re * real_of(x) - im * imag_of(x), re * imag_of(x) + im * real_of(x)], axis=1
    )


def identity_like(x):
    size = x.shape[0]
    row = lax.broadcasted_iota(jnp.int32, x.shape, 0)
    column = lax.broadcasted_iota(jnp.int32, x.shape, 1)
    return jnp.where(row == column, 1.0, 0.0).astype(F32)


def largest(x, axis):
    return jnp.max(x, axis=axis, keepdims=True)


def invert(s, out_ref):
    size = s.shape[0]
    one = identity_like(s)
    first, scales = schedule()
    s_dagger = dagger(s)
    s_dagger_b = s_dagger.astype(BF16)
    normal = dot(s.astype(BF16), wide(s_dagger_b))
    normal_b = normal.astype(BF16)
    both = dot(jnp.concatenate([s_dagger_b, normal_b], axis=0), wide(normal_b))
    square = both[size:]
    sums = jnp.sum(jnp.sqrt(real_of(square) ** 2 + imag_of(square) ** 2), axis=0, keepdims=True)
    a = first * lax.rsqrt(largest(sums, 1))
    c = scales[0]
    x = (2.0 * c * a) * s_dagger - (c * a * a) * both[:size]
    r = one - (2.0 * c * a) * normal + (c * a * a) * square
    for c in scales[1:]:
        r_b = r.astype(BF16)
        both = dot(jnp.concatenate([x.astype(BF16), r_b], axis=0), wide(r_b))
        x = c * (x + both[:size])
        r = (1.0 - c) * one + c * both[size:]
    s_high, s_low = split(s)
    s_both = jnp.concatenate([s_high, s_low], axis=0)
    x_b = x.astype(BF16)
    both = dot(s_both, wide(x_b))
    e_b = (one - both[:size] - both[size:]).astype(BF16)
    x = x_b.astype(F32) + dot(x_b, wide(e_b))

    def step(x):
        x_high, x_low = split(x)
        both = dot(s_both, wide(x_high))
        e = one - both[:size] - both[size:] - dot(s_high, wide(x_low))
        return x + dot(x_high, wide(e.astype(BF16))), jnp.sum(e * e)

    x, left = step(x)
    out_ref[...] = x

    @pl.when(jnp.logical_not(left < DONE))
    def _():
        bound = jnp.sqrt(largest(jnp.sum(jnp.abs(s), axis=1, keepdims=True), 0))
        other = jnp.sqrt(largest(jnp.sum(jnp.abs(real_of(s)) + jnp.abs(imag_of(s)), axis=0, keepdims=True), 1))
        safe = s_dagger / (bound * bound) / (other * other)
        good = left < 0.5
        start = jnp.where(good, x, safe)

        def unfinished(state):
            count, value, _ = state
            return jnp.logical_and(count < STEPS_MAX, jnp.logical_not(value < DONE))

        def body(state):
            count, _, x = state
            new = product(x, one - product(s, x))
            e = one - product(s, x)
            return count + 1, jnp.sum(e * e), x + new

        _, _, result = lax.while_loop(unfinished, body, (0, left, start))
        out_ref[...] = result


def energy_at(index, energies_all):
    return -1.5 + 3.0 * (index + 0.5) / energies_all


def energy_point(axes):
    chips, cores, _ = axes
    index = lax.axis_index("chip") * cores + lax.axis_index("core")
    return energy_at(index.astype(F32), chips * cores)


def place(axes):
    position, cells_all = lax.axis_index("space"), axes[2]
    return position, jnp.minimum(position, cells_all - 1 - position), position < cells_all // 2


def outer_kernel(
    axes, onsite_far, hopping_far, sigma_far, system_ref, green_ref, message_ref, h_ref, hd_ref, token_ref, onsite, hopping, sigma, arrivals
):
    copies = [
        pltpu.make_async_copy(far, near, arrivals.at[i])
        for i, (far, near) in enumerate(((onsite_far, onsite), (hopping_far, hopping), (sigma_far, sigma)))
    ]
    for copy in copies:
        copy.start()
    for copy in copies:
        copy.wait()
    position, depth, left = place(axes)
    energy = energy_point(axes)
    on = jnp.concatenate([onsite[0, 0], onsite[0, 1]], axis=1)
    sg = jnp.concatenate([sigma[0, 0, 0], sigma[0, 0, 1]], axis=1)
    h = jnp.concatenate([hopping[0, 0], hopping[0, 1]], axis=1)
    hd = dagger(h)
    h_ref[...] = h
    token_ref[...] = jnp.zeros_like(token_ref)
    hd_ref[...] = hd
    shape = on.shape
    row = lax.broadcasted_iota(jnp.int32, shape, 0)
    column = lax.broadcasted_iota(jnp.int32, shape, 1)
    point = jnp.where(row == column, energy, 0.0) + jnp.where(row + shape[0] == column, BROADEN, 0.0)
    system_ref[...] = point - 0.5 * (on + dagger(on)) - sg

    @pl.when(position == 0)
    def _():
        magnitude = energy * energy + BROADEN * BROADEN
        system_ref[...] = system_ref[...] - times_complex(product(hd, h), energy / magnitude, -BROADEN / magnitude)

    @pl.when(depth == 0)
    def _():
        invert(system_ref[...], green_ref)
        send(left, green_ref, h, hd, message_ref)

    @pl.when(depth != 0)
    def _():
        green_ref[...] = jnp.zeros(shape, F32)
        message_ref[...] = jnp.zeros(shape, F32)


def send(plain, green_ref, h, hd, message_ref):
    @pl.when(plain)
    def _():
        message_ref[...] = green_ref[...]

    @pl.when(jnp.logical_not(plain))
    def _():
        message_ref[...] = product(h, product(green_ref[...], hd))


def inward_kernel(axes, level, _, received, system, green, message, u, outside, h, hd, system_ref, green_ref, message_ref, u_ref, outside_ref):
    _, depth, left = place(axes)

    @pl.when(depth == level)
    def _():
        got = received[...]

        @pl.when(left)
        def _():
            gh = product(got, h[...])
            u_ref[...] = gh
            outside_ref[...] = got
            system_ref[...] = system[...] - product(hd[...], gh)

        @pl.when(jnp.logical_not(left))
        def _():
            system_ref[...] = system[...] - got
            u_ref[...] = u[...]
            outside_ref[...] = outside[...]

        invert(system_ref[...], green_ref)
        send(left, green_ref, h[...], hd[...], message_ref)

    @pl.when(depth != level)
    def _():
        system_ref[...] = system[...]
        green_ref[...] = green[...]
        message_ref[...] = message[...]
        u_ref[...] = u[...]
        outside_ref[...] = outside[...]


def middle_kernel(axes, received, system, green, h, hd, diagonal_ref, message_ref, u_ref):
    _, depth, left = place(axes)

    @pl.when(depth == axes[2] // 2 - 1)
    def _():
        got = received[...]

        @pl.when(left)
        def _():
            u_ref[...] = system[...] - got

        @pl.when(jnp.logical_not(left))
        def _():
            message_ref[...] = product(got, h[...])
            u_ref[...] = system[...] - product(hd[...], message_ref[...])

        s = u_ref[...]
        u_ref[...] = message_ref[...]
        invert(s, diagonal_ref)
        send(jnp.logical_not(left), diagonal_ref, h[...], hd[...], message_ref)

    @pl.when(depth != axes[2] // 2 - 1)
    def _():
        diagonal_ref[...] = green[...]
        u_ref[...] = jnp.zeros_like(u_ref)
        message_ref[...] = jnp.zeros_like(message_ref)


def waiting_kernel(axes, received, diagonal, u_in, u_out, outside, h, hd, upper_ref, lower_ref, ready_ref):
    position, depth, left = place(axes)
    energy = energy_point(axes)
    magnitude = energy * energy + BROADEN * BROADEN
    contact_re, contact_im = energy / magnitude, -BROADEN / magnitude

    @pl.when(depth == axes[2] // 2 - 1)
    def _():
        u = jnp.where(left, u_out[...], u_in[...])
        v = product(hd[...], jnp.where(left, outside[...], received[...]))
        upper_ref[...] = product(u, diagonal[...])
        lower_ref[...] = product(diagonal[...], v)
        ready_ref[...] = jnp.zeros_like(ready_ref)

    @pl.when(depth != axes[2] // 2 - 1)
    def _():
        g = diagonal[...]

        @pl.when(left)
        def _():
            at_contact = position == 0
            u = jnp.where(at_contact, times_complex(h[...], contact_re, contact_im), u_out[...])
            v = jnp.where(at_contact, times_complex(hd[...], contact_re, contact_im), product(hd[...], outside[...]))
            ready_ref[0] = g
            ready_ref[1] = g
            ready_ref[2] = product(u, g)
            ready_ref[3] = product(g, v)

        @pl.when(jnp.logical_not(left))
        def _():
            ready_ref[0] = product(g, hd[...])
            ready_ref[1] = product(h[...], g)
            ready_ref[2] = jnp.zeros_like(g)
            ready_ref[3] = jnp.zeros_like(g)

        upper_ref[...] = jnp.zeros_like(upper_ref)
        lower_ref[...] = jnp.zeros_like(lower_ref)


def outward_kernel(axes, level, final, waited, *refs):
    outward(axes, level, final, *refs[waited:])


def outward(axes, level, final, received, ready, diagonal, upper, lower, h, hd, *outputs):
    _, depth, left = place(axes)
    if final:
        packed_ref, green_ref, upper_ref, lower_ref = outputs
    else:
        message_ref, green_ref, upper_ref, lower_ref = outputs
        message_ref[...] = jnp.zeros_like(message_ref)

    @pl.when(depth != level)
    def _():
        green_ref[...] = diagonal[...]
        upper_ref[...] = upper[...]
        lower_ref[...] = lower[...]

    @pl.when(depth == level)
    def _():
        g_in = received[...]
        p = ready[0]
        w = product(g_in, ready[1])
        green_ref[...] = diagonal[...] + product(p, w)

        @pl.when(left)
        def _():
            upper_ref[...] = ready[2] + product(ready[2], w)
            lower_ref[...] = ready[3] + product(p, product(g_in, ready[3]))

        @pl.when(jnp.logical_not(left))
        def _():
            upper_ref[...] = w
            lower_ref[...] = product(p, g_in)

        if not final:
            send(jnp.logical_not(left), green_ref, h[...], hd[...], message_ref)

    if final:
        size = diagonal.shape[0]
        blocks = (green_ref[...], upper_ref[...], lower_ref[...])
        d0 = blocks[0] - dagger(blocks[0])
        d1 = blocks[1] - dagger(blocks[2])
        row = lax.broadcasted_iota(jnp.int32, (size, size), 0)
        column = lax.broadcasted_iota(jnp.int32, (size, size), 1)
        packed_ref[0] = jnp.where(row > column, real_of(d0), imag_of(d0))
        packed_ref[1] = real_of(d1)
        packed_ref[2] = imag_of(d1)


def store_kernel(axes, diagonal, upper, lower, out, arrivals):
    size = diagonal.shape[0]
    copies = [
        pltpu.make_async_copy(block.at[:, pl.ds(part * size, size)], out.at[b, part], arrivals.at[2 * b + part])
        for b, block in enumerate((diagonal, upper, lower))
        for part in range(2)
    ]
    for copy in copies:
        copy.start()
    for copy in copies:
        copy.wait()


def unpack(pack, out, scale):
    size = pack.shape[-1]
    row = lax.broadcasted_iota(jnp.int32, (size, size), 0)
    column = lax.broadcasted_iota(jnp.int32, (size, size), 1)
    mixed = pack[0] * scale
    turned = mixed.T
    out[0, 0] = jnp.where(row > column, mixed, jnp.where(row < column, -turned, 0.0))
    out[0, 1] = jnp.where(row > column, turned, mixed)
    re, im = pack[1] * scale, pack[2] * scale
    out[1, 0], out[1, 1] = re, im
    out[2, 0], out[2, 1] = -re.T, im.T


def unpack_all(axes, same, packs, spectral):
    chips, cores, _ = axes
    chip, core = lax.axis_index("chip"), lax.axis_index("core")
    spectral[chips] = jnp.zeros(spectral.shape[1:], F32)
    for offset in range(chips):
        lower = jnp.bitwise_xor(chip, offset)

        @pl.when(lower <= chip)
        def _():
            index = lower * cores + (core if same else 1 - core)
            energy = energy_at(index.astype(F32), chips * cores)
            occupation = 1.0 / (1.0 + jnp.exp(jnp.full((1, 1), energy / THERMAL, F32)))
            unpack(packs[offset], spectral.at[offset], jnp.where(core == 0, -occupation, 1.0 - occupation))


def add_terms(axes, same, only, pieces, outs, spectral):
    chips, cores, _ = axes
    chip, core = lax.axis_index("chip"), lax.axis_index("core")
    size = spectral.shape[-1]
    for c in range(cores):
        p = c if same else 1 - c

        @pl.when(core == c)
        def _():
            for to in only:
                k = (c + to + p) % 2
                terms = []
                for offset in range(chips):
                    kappa = jnp.bitwise_xor(chip, offset) if len(pieces) > 1 else jnp.int32(offset)
                    d = chip - kappa - (p + k) // 2
                    place_of = jnp.where(d >= 0, jnp.bitwise_xor(chip, d), chips)
                    terms.append((place_of, screened_at(pieces, offset, kappa, k)))

                @pl.loop(0, size // ROWS)
                def _(tile):
                    rows = pl.ds(pl.multiple_of(tile * ROWS, ROWS), ROWS)
                    for b in range(3):
                        re, im = outs[to][b, 0, rows], outs[to][b, 1, rows]
                        for place_of, blocks in terms:
                            g_re, g_im = spectral[place_of, b, 0, rows], spectral[place_of, b, 1, rows]
                            w_re, w_im = blocks[b, 0, rows], blocks[b, 1, rows]
                            re = re - g_re * w_im - g_im * w_re
                            im = im + g_re * w_re - g_im * w_im
                        outs[to][b, 0, rows] = re
                        outs[to][b, 1, rows] = im


def same_core_kernel(axes, *refs):
    chips = axes[0]
    packs, pieces, outs, spectral = refs[:chips], refs[chips:-3], refs[-3:-1], refs[-1]
    for out in outs:
        out[...] = jnp.zeros_like(out)
    unpack_all(axes, True, packs, spectral)
    add_terms(axes, True, (0, 1), pieces, outs, spectral)


def theirs_kernel(axes, *refs):
    chips = axes[0]
    packs, before, pieces, out, spectral = refs[:chips], refs[chips], refs[chips + 1 : -2], refs[-2], refs[-1]
    out[...] = before[...]
    unpack_all(axes, False, packs, spectral)
    add_terms(axes, False, (1,), pieces, (None, out), spectral)


def mine_kernel(axes, spectral, before, *refs):
    pieces, out, held, arrival = refs[:-3], refs[-3], refs[-2], refs[-1]
    held[...] = before[...]
    add_terms(axes, False, (0,), pieces, (held, None), spectral)
    copy = pltpu.make_async_copy(held, out.at[lax.axis_index("core")], arrival)
    copy.start()
    copy.wait()


def screened_at(pieces, offset, kappa, k):
    if len(pieces) == 1:
        return pieces[0].at[kappa, k]
    return pieces[2 * offset + k]


def join_kernel(axes, received, _, out, arrival):
    copy = pltpu.make_async_copy(received, out.at[1 - lax.axis_index("core")], arrival)
    copy.start()
    copy.wait()


class Exchange:
    def __init__(self, chips, screened, swap):
        self.paired = chips == 4
        self.own = screened[0, 0]
        self.got = lax.ppermute(self.own, "core", swap)
        self.later = []

    def moved(self, piece, offset):
        return lax.ppermute(piece, "chip", [(i, i ^ offset) for i in range(4)])

    def begin(self, after):
        core = lax.axis_index("core")
        own, got, _ = lax.optimization_barrier((self.own, self.got, after))
        one, two = jnp.where(core == 0, own[0], got[1]), jnp.where(core == 0, got[0], own[1])
        if self.paired:
            self.along = [self.moved(one, 1), self.moved(two, 2)]
            self.later = [self.moved(two, 1), self.moved(one, 2)]
            self.pieces = [one, two, self.along[0], self.later[0], self.later[1], self.along[1]]
        else:
            self.pieces = [lax.all_gather(jnp.stack([one, two]), "chip", axis=0)]

    def go_on(self, after):
        if self.paired:
            first, second, _ = lax.optimization_barrier((*self.along, after))
            self.pieces += [self.moved(first, 2), self.moved(second, 1)]


def local(axes, onsite, hopping, sigma_old, screened):
    chips, cores, cells_all = axes
    size = sigma_old.shape[-1]
    half = cells_all // 2
    matrix = jax.ShapeDtypeStruct((size, 2 * size), F32)
    def call(body, out_shape, *operands, space=pltpu.VMEM, grant=16, work=WORK, out_space=None, **options):
        spec = pl.BlockSpec(memory_space=pltpu.VMEM)
        spaces = space if isinstance(space, list) else [space] * len(operands)
        return pl.pallas_call(
            functools.partial(body, axes),
            out_shape=out_shape,
            in_specs=[pl.BlockSpec(memory_space=space) for space in spaces],
            out_specs=jax.tree.map(lambda _: spec, out_shape)
            if out_space is None
            else jax.tree.map(lambda space: pl.BlockSpec(memory_space=space), out_space),
            compiler_params=pltpu.CompilerParams(vmem_limit_bytes=grant * 1024 * 1024),
            cost_estimate=pl.CostEstimate(
                flops=int(work * 80 * (2 * size) ** 3), bytes_accessed=2 * 1024 * 1024, transcendentals=0
            ),
            **options,
        )(*operands)

    swap = [(i, i ^ 1) for i in range(cores)]
    exchange = Exchange(chips, screened, swap)
    token = jax.ShapeDtypeStruct((8, size), F32)
    system, green, message, h, hd, mark = call(
        outer_kernel,
        (matrix,) * 5 + (token,),
        *(pltpu.with_memory_space_constraint(a, pltpu.HBM) for a in (onsite, hopping, sigma_old)),
        space=pltpu.HBM,
        scratch_shapes=[pltpu.VMEM(a.shape, F32) for a in (onsite, hopping, sigma_old)]
        + [pltpu.SemaphoreType.DMA((3,))],
    )
    mark = lax.ppermute(mark, "core", swap)
    exchange.begin(mark)
    u_out = outside = jnp.zeros((size, 2 * size), F32)
    for level in range(1, half):
        route = [(level - 1, level), (cells_all - level, cells_all - 1 - level)]
        received = lax.ppermute(message, "space", route)
        system, green, message, u_out, outside = call(
            functools.partial(swapped, inward_kernel, level),
            (matrix,) * 5,
            mark, received, system, green, message, u_out, outside, h, hd,
            work=WORK2,
        )
        if level == half - 1:
            exchange.go_on(message)
    received = lax.ppermute(message, "space", [(half - 1, half), (half, half - 1)])
    diagonal, message, u_in = call(
        middle_kernel, (matrix,) * 3, received, system, green, h, hd,
        work=WORK3,
    )
    upper = None
    for level in reversed(range(half - 1)):
        route = [(level + 1, level), (cells_all - 2 - level, cells_all - 1 - level)]
        arrived = lax.ppermute(message, "space", route)
        if upper is None:
            upper, lower, ready = call(
                waiting_kernel,
                (matrix, matrix, jax.ShapeDtypeStruct((4, size, 2 * size), F32)),
                received, diagonal, u_in, u_out, outside, h, hd,
                work=WORK4,
            )
        final = level == 0
        shapes = (jax.ShapeDtypeStruct((3, size, size), F32) if final else matrix,) + (matrix,) * 3
        results = call(
            functools.partial(swapped, outward_kernel, level, final, len(exchange.later)),
            shapes,
            *exchange.later, arrived, ready, diagonal, upper, lower, h, hd,
            space=[pl.ANY] * len(exchange.later) + [pltpu.VMEM] * 7,
            work=WORK6,
        )
        message, diagonal, upper, lower = results
    packed = message
    green_out = call(
        store_kernel,
        jax.ShapeDtypeStruct((3, 2, size, size), F32),
        diagonal, upper, lower,
        out_space=pl.ANY,
        scratch_shapes=[pltpu.SemaphoreType.DMA((6,))],
    )
    own = [packed] + [
        lax.ppermute(packed, "chip", [(i, i ^ offset) for i in range(chips)]) for offset in range(1, chips)
    ]
    kept, green_out = lax.optimization_barrier((packed, green_out))
    other = [lax.ppermute(pack, "core", swap) for pack in [kept] + own[1:]]
    kind = jax.ShapeDtypeStruct(screened.shape[3:], F32)
    unpacked = (chips + 1, 3, 2, size, size)
    mine, theirs = call(
        same_core_kernel, (kind,) * 2, *own, *exchange.pieces,
        scratch_shapes=[pltpu.VMEM(unpacked, F32)],
        work=WORK5,
    )
    theirs, spectral = call(
        theirs_kernel, (kind, jax.ShapeDtypeStruct(unpacked, F32)), *other, theirs, *exchange.pieces
    )
    received = lax.ppermute(theirs, "core", swap)
    half_out = call(
        mine_kernel,
        jax.ShapeDtypeStruct(screened.shape[2:], F32),
        spectral, mine, *exchange.pieces,
        out_space=pl.ANY,
        scratch_shapes=[pltpu.VMEM(kind.shape, F32), pltpu.SemaphoreType.DMA],
    )
    sigma_out = call(
        join_kernel,
        jax.ShapeDtypeStruct(screened.shape[2:], F32),
        received, half_out,
        space=pl.ANY,
        out_space=pl.ANY,
        input_output_aliases={1: 0},
        scratch_shapes=[pltpu.SemaphoreType.DMA],
    )
    return green_out[None, None], sigma_out[None, None]


def swapped(body, *arguments):
    fixed = [a for a in arguments if isinstance(a, (int, bool))]
    axes, *refs = arguments[len(fixed) :]
    return body(axes, *fixed, *refs)


def solution(mesh):
    cores = 2
    axes = (mesh.shape["energy"] // cores, cores, mesh.shape["space"])
    split_mesh = jax.sharding.Mesh(mesh.devices.reshape(axes), ("chip", "core", "space"))
    energy = ("chip", "core")
    placed = (
        P("space", None, None, None),
        P("space", None, None, None),
        P(energy, "space", None, None, None),
        P(energy, "space", None, None, None, None, None),
    )
    return jax.shard_map(
        functools.partial(local, axes),
        mesh=split_mesh,
        in_specs=placed,
        out_specs=(
            P(energy, "space", None, None, None, None),
            P(energy, "space", None, None, None, None, None),
        ),
        check_vma=False,
    )
```

```python
import functools
import math

import jax
import jax.numpy as jnp
from jax import lax
from jax.experimental import pallas as pl
from jax.experimental.pallas import tpu as pltpu
from jax.sharding import PartitionSpec as P

BROADEN = 0.45
THERMAL = 0.1
F32 = jnp.float32
BF16 = jnp.bfloat16

LOWEST = 1.0 / 128.0
SQUARINGS = 6
DONE = 1e-4
STEPS_MAX = 60
ROWS = 64
WORK = 1
WORK2 = 2
WORK3 = 0.1
WORK4 = 0.1
WORK5 = 0.01
WORK6 = 0.1


def schedule():
    rho = (1.0 - LOWEST) / (1.0 + LOWEST)
    scales = []
    for _ in range(SQUARINGS):
        scales.append(2.0 / (2.0 - rho * rho))
        rho = rho * rho / (2.0 - rho * rho)
    return 2.0 / (1.0 + LOWEST), scales


def real_of(x):
    return x[:, : x.shape[1] // 2]


def imag_of(x):
    return x[:, x.shape[1] // 2 :]


def wide(x):
    return jnp.concatenate([x, jnp.concatenate([-imag_of(x), real_of(x)], axis=1)], axis=0)


def dagger(x):
    return jnp.concatenate([real_of(x).T, -imag_of(x).T], axis=1)


def dot(a, b):
    return jnp.dot(a, b, preferred_element_type=F32)


def split(x):
    high = x.astype(BF16)
    return high, (x - high.astype(F32)).astype(BF16)


def product(a, b):
    rows = a.shape[0]
    a_high, a_low = split(a)
    b_high, b_low = split(b)
    both = dot(jnp.concatenate([a_high, a_low], axis=0), wide(b_high))
    return both[:rows] + both[rows:] + dot(a_high, wide(b_low))


def times_complex(x, re, im):
    return jnp.concatenate(
        [re * real_of(x) - im * imag_of(x), re * imag_of(x) + im * real_of(x)], axis=1
    )


def identity_like(x):
    size = x.shape[0]
    row = lax.broadcasted_iota(jnp.int32, x.shape, 0)
    column = lax.broadcasted_iota(jnp.int32, x.shape, 1)
    return jnp.where(row == column, 1.0, 0.0).astype(F32)


def largest(x, axis):
    return jnp.max(x, axis=axis, keepdims=True)


def invert(s, out_ref):
    size = s.shape[0]
    one = identity_like(s)
    first, scales = schedule()
    s_dagger = dagger(s)
    s_dagger_b = s_dagger.astype(BF16)
    normal = dot(s.astype(BF16), wide(s_dagger_b))
    normal_b = normal.astype(BF16)
    both = dot(jnp.concatenate([s_dagger_b, normal_b], axis=0), wide(normal_b))
    square = both[size:]
    sums = jnp.sum(jnp.sqrt(real_of(square) ** 2 + imag_of(square) ** 2), axis=0, keepdims=True)
    a = first * lax.rsqrt(largest(sums, 1))
    c = scales[0]
    x = (2.0 * c * a) * s_dagger - (c * a * a) * both[:size]
    r = one - (2.0 * c * a) * normal + (c * a * a) * square
    for c in scales[1:]:
        r_b = r.astype(BF16)
        both = dot(jnp.concatenate([x.astype(BF16), r_b], axis=0), wide(r_b))
        x = c * (x + both[:size])
        r = (1.0 - c) * one + c * both[size:]
    s_high, s_low = split(s)
    s_both = jnp.concatenate([s_high, s_low], axis=0)
    x_b = x.astype(BF16)
    both = dot(s_both, wide(x_b))
    e_b = (one - both[:size] - both[size:]).astype(BF16)
    x = x_b.astype(F32) + dot(x_b, wide(e_b))

    def step(x):
        x_high, x_low = split(x)
        both = dot(s_both, wide(x_high))
        e = one - both[:size] - both[size:] - dot(s_high, wide(x_low))
        return x + dot(x_high, wide(e.astype(BF16))), jnp.sum(e * e)

    x, left = step(x)
    out_ref[...] = x

    @pl.when(jnp.logical_not(left < DONE))
    def _():
        bound = jnp.sqrt(largest(jnp.sum(jnp.abs(s), axis=1, keepdims=True), 0))
        other = jnp.sqrt(largest(jnp.sum(jnp.abs(real_of(s)) + jnp.abs(imag_of(s)), axis=0, keepdims=True), 1))
        safe = s_dagger / (bound * bound) / (other * other)
        good = left < 0.5
        start = jnp.where(good, x, safe)

        def unfinished(state):
            count, value, _ = state
            return jnp.logical_and(count < STEPS_MAX, jnp.logical_not(value < DONE))

        def body(state):
            count, _, x = state
            new = product(x, one - product(s, x))
            e = one - product(s, x)
            return count + 1, jnp.sum(e * e), x + new

        _, _, result = lax.while_loop(unfinished, body, (0, left, start))
        out_ref[...] = result


def energy_at(index, energies_all):
    return -1.5 + 3.0 * (index + 0.5) / energies_all


def energy_point(axes):
    chips, cores, _ = axes
    index = lax.axis_index("chip") * cores + lax.axis_index("core")
    return energy_at(index.astype(F32), chips * cores)


def place(axes):
    position, cells_all = lax.axis_index("space"), axes[2]
    return position, jnp.minimum(position, cells_all - 1 - position), position < cells_all // 2


def outer_kernel(
    axes, onsite_far, hopping_far, sigma_far, system_ref, green_ref, message_ref, h_ref, hd_ref, token_ref, onsite, hopping, sigma, arrivals
):
    copies = [
        pltpu.make_async_copy(far, near, arrivals.at[i])
        for i, (far, near) in enumerate(((onsite_far, onsite), (hopping_far, hopping), (sigma_far, sigma)))
    ]
    for copy in copies:
        copy.start()
    for copy in copies:
        copy.wait()
    position, depth, left = place(axes)
    energy = energy_point(axes)
    on = jnp.concatenate([onsite[0, 0], onsite[0, 1]], axis=1)
    sg = jnp.concatenate([sigma[0, 0, 0], sigma[0, 0, 1]], axis=1)
    h = jnp.concatenate([hopping[0, 0], hopping[0, 1]], axis=1)
    hd = dagger(h)
    h_ref[...] = h
    token_ref[...] = jnp.zeros_like(token_ref)
    hd_ref[...] = hd
    shape = on.shape
    row = lax.broadcasted_iota(jnp.int32, shape, 0)
    column = lax.broadcasted_iota(jnp.int32, shape, 1)
    point = jnp.where(row == column, energy, 0.0) + jnp.where(row + shape[0] == column, BROADEN, 0.0)
    system_ref[...] = point - 0.5 * (on + dagger(on)) - sg

    @pl.when(position == 0)
    def _():
        magnitude = energy * energy + BROADEN * BROADEN
        system_ref[...] = system_ref[...] - times_complex(product(hd, h), energy / magnitude, -BROADEN / magnitude)

    @pl.when(depth == 0)
    def _():
        invert(system_ref[...], green_ref)
        send(left, green_ref, h, hd, message_ref)

    @pl.when(depth != 0)
    def _():
        green_ref[...] = jnp.zeros(shape, F32)
        message_ref[...] = jnp.zeros(shape, F32)


def send(plain, green_ref, h, hd, message_ref):
    @pl.when(plain)
    def _():
        message_ref[...] = green_ref[...]

    @pl.when(jnp.logical_not(plain))
    def _():
        message_ref[...] = product(h, product(green_ref[...], hd))


def inward_kernel(axes, level, _, received, system, green, message, u, outside, h, hd, system_ref, green_ref, message_ref, u_ref, outside_ref):
    _, depth, left = place(axes)

    @pl.when(depth == level)
    def _():
        got = received[...]

        @pl.when(left)
        def _():
            gh = product(got, h[...])
            u_ref[...] = gh
            outside_ref[...] = got
            system_ref[...] = system[...] - product(hd[...], gh)

        @pl.when(jnp.logical_not(left))
        def _():
            system_ref[...] = system[...] - got
            u_ref[...] = u[...]
            outside_ref[...] = outside[...]

        invert(system_ref[...], green_ref)
        send(left, green_ref, h[...], hd[...], message_ref)

    @pl.when(depth != level)
    def _():
        system_ref[...] = system[...]
        green_ref[...] = green[...]
        message_ref[...] = message[...]
        u_ref[...] = u[...]
        outside_ref[...] = outside[...]


def middle_kernel(axes, received, system, green, h, hd, diagonal_ref, message_ref, u_ref):
    _, depth, left = place(axes)

    @pl.when(depth == axes[2] // 2 - 1)
    def _():
        got = received[...]

        @pl.when(left)
        def _():
            u_ref[...] = system[...] - got

        @pl.when(jnp.logical_not(left))
        def _():
            message_ref[...] = product(got, h[...])
            u_ref[...] = system[...] - product(hd[...], message_ref[...])

        s = u_ref[...]
        u_ref[...] = message_ref[...]
        invert(s, diagonal_ref)
        send(jnp.logical_not(left), diagonal_ref, h[...], hd[...], message_ref)

    @pl.when(depth != axes[2] // 2 - 1)
    def _():
        diagonal_ref[...] = green[...]
        u_ref[...] = jnp.zeros_like(u_ref)
        message_ref[...] = jnp.zeros_like(message_ref)


def waiting_kernel(axes, received, diagonal, u_in, u_out, outside, h, hd, upper_ref, lower_ref, ready_ref):
    position, depth, left = place(axes)
    energy = energy_point(axes)
    magnitude = energy * energy + BROADEN * BROADEN
    contact_re, contact_im = energy / magnitude, -BROADEN / magnitude

    @pl.when(depth == axes[2] // 2 - 1)
    def _():
        u = jnp.where(left, u_out[...], u_in[...])
        v = product(hd[...], jnp.where(left, outside[...], received[...]))
        upper_ref[...] = product(u, diagonal[...])
        lower_ref[...] = product(diagonal[...], v)
        ready_ref[...] = jnp.zeros_like(ready_ref)

    @pl.when(depth != axes[2] // 2 - 1)
    def _():
        g = diagonal[...]

        @pl.when(left)
        def _():
            at_contact = position == 0
            u = jnp.where(at_contact, times_complex(h[...], contact_re, contact_im), u_out[...])
            v = jnp.where(at_contact, times_complex(hd[...], contact_re, contact_im), product(hd[...], outside[...]))
            ready_ref[0] = g
            ready_ref[1] = g
            ready_ref[2] = product(u, g)
            ready_ref[3] = product(g, v)

        @pl.when(jnp.logical_not(left))
        def _():
            ready_ref[0] = product(g, hd[...])
            ready_ref[1] = product(h[...], g)
            ready_ref[2] = jnp.zeros_like(g)
            ready_ref[3] = jnp.zeros_like(g)

        upper_ref[...] = jnp.zeros_like(upper_ref)
        lower_ref[...] = jnp.zeros_like(lower_ref)


def outward_kernel(axes, level, final, waited, *refs):
    outward(axes, level, final, *refs[waited:])


def outward(axes, level, final, received, ready, diagonal, upper, lower, h, hd, *outputs):
    _, depth, left = place(axes)
    if final:
        packed_ref, green_ref, upper_ref, lower_ref = outputs
    else:
        message_ref, green_ref, upper_ref, lower_ref = outputs
        message_ref[...] = jnp.zeros_like(message_ref)

    @pl.when(depth != level)
    def _():
        green_ref[...] = diagonal[...]
        upper_ref[...] = upper[...]
        lower_ref[...] = lower[...]

    @pl.when(depth == level)
    def _():
        g_in = received[...]
        p = ready[0]
        w = product(g_in, ready[1])
        green_ref[...] = diagonal[...] + product(p, w)

        @pl.when(left)
        def _():
            upper_ref[...] = ready[2] + product(ready[2], w)
            lower_ref[...] = ready[3] + product(p, product(g_in, ready[3]))

        @pl.when(jnp.logical_not(left))
        def _():
            upper_ref[...] = w
            lower_ref[...] = product(p, g_in)

        if not final:
            send(jnp.logical_not(left), green_ref, h[...], hd[...], message_ref)

    if final:
        size = diagonal.shape[0]
        blocks = (green_ref[...], upper_ref[...], lower_ref[...])
        d0 = blocks[0] - dagger(blocks[0])
        d1 = blocks[1] - dagger(blocks[2])
        row = lax.broadcasted_iota(jnp.int32, (size, size), 0)
        column = lax.broadcasted_iota(jnp.int32, (size, size), 1)
        packed_ref[0] = jnp.where(row > column, real_of(d0), imag_of(d0))
        packed_ref[1] = real_of(d1)
        packed_ref[2] = imag_of(d1)


def store_kernel(axes, diagonal, upper, lower, out, arrivals):
    size = diagonal.shape[0]
    copies = [
        pltpu.make_async_copy(block.at[:, pl.ds(part * size, size)], out.at[b, part], arrivals.at[2 * b + part])
        for b, block in enumerate((diagonal, upper, lower))
        for part in range(2)
    ]
    for copy in copies:
        copy.start()
    for copy in copies:
        copy.wait()


def unpack(pack, out, scale):
    size = pack.shape[-1]
    row = lax.broadcasted_iota(jnp.int32, (size, size), 0)
    column = lax.broadcasted_iota(jnp.int32, (size, size), 1)
    mixed = pack[0] * scale
    turned = mixed.T
    out[0, 0] = jnp.where(row > column, mixed, jnp.where(row < column, -turned, 0.0))
    out[0, 1] = jnp.where(row > column, turned, mixed)
    re, im = pack[1] * scale, pack[2] * scale
    out[1, 0], out[1, 1] = re, im
    out[2, 0], out[2, 1] = -re.T, im.T


def unpack_all(axes, same, packs, spectral):
    chips, cores, _ = axes
    chip, core = lax.axis_index("chip"), lax.axis_index("core")
    spectral[chips] = jnp.zeros(spectral.shape[1:], F32)
    for offset in range(chips):
        lower = jnp.bitwise_xor(chip, offset)

        @pl.when(lower <= chip)
        def _():
            index = lower * cores + (core if same else 1 - core)
            energy = energy_at(index.astype(F32), chips * cores)
            occupation = 1.0 / (1.0 + jnp.exp(jnp.full((1, 1), energy / THERMAL, F32)))
            unpack(packs[offset], spectral.at[offset], jnp.where(core == 0, -occupation, 1.0 - occupation))


def add_terms(axes, same, only, pieces, outs, spectral):
    chips, cores, _ = axes
    chip, core = lax.axis_index("chip"), lax.axis_index("core")
    size = spectral.shape[-1]
    for c in range(cores):
        p = c if same else 1 - c

        @pl.when(core == c)
        def _():
            for to in only:
                k = (c + to + p) % 2
                terms = []
                for offset in range(chips):
                    kappa = jnp.bitwise_xor(chip, offset) if len(pieces) > 1 else jnp.int32(offset)
                    d = chip - kappa - (p + k) // 2
                    place_of = jnp.where(d >= 0, jnp.bitwise_xor(chip, d), chips)
                    terms.append((place_of, screened_at(pieces, offset, kappa, k)))

                @pl.loop(0, size // ROWS)
                def _(tile):
                    rows = pl.ds(pl.multiple_of(tile * ROWS, ROWS), ROWS)
                    for b in range(3):
                        re, im = outs[to][b, 0, rows], outs[to][b, 1, rows]
                        for place_of, blocks in terms:
                            g_re, g_im = spectral[place_of, b, 0, rows], spectral[place_of, b, 1, rows]
                            w_re, w_im = blocks[b, 0, rows], blocks[b, 1, rows]
                            re = re - g_re * w_im - g_im * w_re
                            im = im + g_re * w_re - g_im * w_im
                        outs[to][b, 0, rows] = re
                        outs[to][b, 1, rows] = im


def same_core_kernel(axes, *refs):
    chips = axes[0]
    packs, pieces, outs, spectral = refs[:chips], refs[chips:-3], refs[-3:-1], refs[-1]
    for out in outs:
        out[...] = jnp.zeros_like(out)
    unpack_all(axes, True, packs, spectral)
    add_terms(axes, True, (0, 1), pieces, outs, spectral)


def theirs_kernel(axes, *refs):
    chips = axes[0]
    packs, before, pieces, out, spectral = refs[:chips], refs[chips], refs[chips + 1 : -2], refs[-2], refs[-1]
    out[...] = before[...]
    unpack_all(axes, False, packs, spectral)
    add_terms(axes, False, (1,), pieces, (None, out), spectral)


def mine_kernel(axes, spectral, before, *refs):
    pieces, out, held, arrival = refs[:-3], refs[-3], refs[-2], refs[-1]
    held[...] = before[...]
    add_terms(axes, False, (0,), pieces, (held, None), spectral)
    copy = pltpu.make_async_copy(held, out.at[lax.axis_index("core")], arrival)
    copy.start()
    copy.wait()


def screened_at(pieces, offset, kappa, k):
    if len(pieces) == 1:
        return pieces[0].at[kappa, k]
    return pieces[2 * offset + k]


def join_kernel(axes, received, _, out, arrival):
    copy = pltpu.make_async_copy(received, out.at[1 - lax.axis_index("core")], arrival)
    copy.start()
    copy.wait()


class Exchange:
    def __init__(self, chips, screened, swap):
        self.paired = chips == 4
        self.own = screened[0, 0]
        self.got = lax.ppermute(self.own, "core", swap)
        self.later = []

    def moved(self, piece, offset):
        return lax.ppermute(piece, "chip", [(i, i ^ offset) for i in range(4)])

    def begin(self, after):
        core = lax.axis_index("core")
        own, got, _ = lax.optimization_barrier((self.own, self.got, after))
        one, two = jnp.where(core == 0, own[0], got[1]), jnp.where(core == 0, got[0], own[1])
        if self.paired:
            self.along = [self.moved(one, 1), self.moved(two, 2)]
            self.later = [self.moved(two, 1), self.moved(one, 2)]
            self.pieces = [one, two, self.along[0], self.later[0], self.later[1], self.along[1]]
        else:
            self.pieces = [lax.all_gather(jnp.stack([one, two]), "chip", axis=0)]

    def go_on(self, after):
        if self.paired:
            first, second, _ = lax.optimization_barrier((*self.along, after))
            self.pieces += [self.moved(first, 2), self.moved(second, 1)]


def local(axes, onsite, hopping, sigma_old, screened):
    chips, cores, cells_all = axes
    size = sigma_old.shape[-1]
    half = cells_all // 2
    matrix = jax.ShapeDtypeStruct((size, 2 * size), F32)
    def call(body, out_shape, *operands, space=pltpu.VMEM, grant=16, work=WORK, out_space=None, **options):
        spec = pl.BlockSpec(memory_space=pltpu.VMEM)
        spaces = space if isinstance(space, list) else [space] * len(operands)
        return pl.pallas_call(
            functools.partial(body, axes),
            out_shape=out_shape,
            in_specs=[pl.BlockSpec(memory_space=space) for space in spaces],
            out_specs=jax.tree.map(lambda _: spec, out_shape)
            if out_space is None
            else jax.tree.map(lambda space: pl.BlockSpec(memory_space=space), out_space),
            compiler_params=pltpu.CompilerParams(vmem_limit_bytes=grant * 1024 * 1024),
            cost_estimate=pl.CostEstimate(
                flops=int(work * 80 * (2 * size) ** 3), bytes_accessed=2 * 1024 * 1024, transcendentals=0
            ),
            **options,
        )(*operands)

    swap = [(i, i ^ 1) for i in range(cores)]
    exchange = Exchange(chips, screened, swap)
    token = jax.ShapeDtypeStruct((8, size), F32)
    system, green, message, h, hd, mark = call(
        outer_kernel,
        (matrix,) * 5 + (token,),
        *(pltpu.with_memory_space_constraint(a, pltpu.HBM) for a in (onsite, hopping, sigma_old)),
        space=pltpu.HBM,
        scratch_shapes=[pltpu.VMEM(a.shape, F32) for a in (onsite, hopping, sigma_old)]
        + [pltpu.SemaphoreType.DMA((3,))],
    )
    mark = lax.ppermute(mark, "core", swap)
    exchange.begin(mark)
    u_out = outside = jnp.zeros((size, 2 * size), F32)
    for level in range(1, half):
        route = [(level - 1, level), (cells_all - level, cells_all - 1 - level)]
        received = lax.ppermute(message, "space", route)
        system, green, message, u_out, outside = call(
            functools.partial(swapped, inward_kernel, level),
            (matrix,) * 5,
            mark, received, system, green, message, u_out, outside, h, hd,
            work=WORK2,
        )
        if level == half - 1:
            exchange.go_on(message)
    received = lax.ppermute(message, "space", [(half - 1, half), (half, half - 1)])
    diagonal, message, u_in = call(
        middle_kernel, (matrix,) * 3, received, system, green, h, hd,
        work=WORK3,
    )
    upper = None
    for level in reversed(range(half - 1)):
        route = [(level + 1, level), (cells_all - 2 - level, cells_all - 1 - level)]
        arrived = lax.ppermute(message, "space", route)
        if upper is None:
            upper, lower, ready = call(
                waiting_kernel,
                (matrix, matrix, jax.ShapeDtypeStruct((4, size, 2 * size), F32)),
                received, diagonal, u_in, u_out, outside, h, hd,
                work=WORK4,
            )
        final = level == 0
        shapes = (jax.ShapeDtypeStruct((3, size, size), F32) if final else matrix,) + (matrix,) * 3
        results = call(
            functools.partial(swapped, outward_kernel, level, final, len(exchange.later)),
            shapes,
            *exchange.later, arrived, ready, diagonal, upper, lower, h, hd,
            space=[pl.ANY] * len(exchange.later) + [pltpu.VMEM] * 7,
            work=WORK6,
        )
        message, diagonal, upper, lower = results
    packed = message
    green_out = call(
        store_kernel,
        jax.ShapeDtypeStruct((3, 2, size, size), F32),
        diagonal, upper, lower,
        out_space=pl.ANY,
        scratch_shapes=[pltpu.SemaphoreType.DMA((6,))],
    )
    own = [packed] + [
        lax.ppermute(packed, "chip", [(i, i ^ offset) for i in range(chips)]) for offset in range(1, chips)
    ]
    kept, green_out = lax.optimization_barrier((packed, green_out))
    other = [lax.ppermute(pack, "core", swap) for pack in [kept] + own[1:]]
    kind = jax.ShapeDtypeStruct(screened.shape[3:], F32)
    unpacked = (chips + 1, 3, 2, size, size)
    mine, theirs = call(
        same_core_kernel, (kind,) * 2, *own, *exchange.pieces,
        scratch_shapes=[pltpu.VMEM(unpacked, F32)],
        work=WORK5,
    )
    theirs, spectral = call(
        theirs_kernel, (kind, jax.ShapeDtypeStruct(unpacked, F32)), *other, theirs, *exchange.pieces
    )
    received = lax.ppermute(theirs, "core", swap)
    half_out = call(
        mine_kernel,
        jax.ShapeDtypeStruct(screened.shape[2:], F32),
        spectral, mine, *exchange.pieces,
        out_space=pl.ANY,
        scratch_shapes=[pltpu.VMEM(kind.shape, F32), pltpu.SemaphoreType.DMA],
    )
    sigma_out = call(
        join_kernel,
        jax.ShapeDtypeStruct(screened.shape[2:], F32),
        received, half_out,
        space=pl.ANY,
        out_space=pl.ANY,
        input_output_aliases={1: 0},
        scratch_shapes=[pltpu.SemaphoreType.DMA],
    )
    return green_out[None, None], sigma_out[None, None]


def swapped(body, *arguments):
    fixed = [a for a in arguments if isinstance(a, (int, bool))]
    axes, *refs = arguments[len(fixed) :]
    return body(axes, *fixed, *refs)


def solution(mesh):
    cores = 2
    axes = (mesh.shape["energy"] // cores, cores, mesh.shape["space"])
    split_mesh = jax.sharding.Mesh(mesh.devices.reshape(axes), ("chip", "core", "space"))
    energy = ("chip", "core")
    placed = (
        P("space", None, None, None),
        P("space", None, None, None),
        P(energy, "space", None, None, None),
        P(energy, "space", None, None, None, None, None),
    )
    return jax.shard_map(
        functools.partial(local, axes),
        mesh=split_mesh,
        in_specs=placed,
        out_specs=(
            P(energy, "space", None, None, None, None),
            P(energy, "space", None, None, None, None, None),
        ),
        check_vma=False,
    )
```
